128 devices in a mesh: dp: 2 (over y_lo), ctx: 16 (over x, y_hi, core), tensor: 4 (over z).
Axes of the slice: x: 4, y: 4 (y_hi: 2, y_lo: 2; y = y_hi * 2 + y_lo), z: 4, core: 2. Of those that a mesh axis runs over, the one named last changes fastest.
Arguments:
- tokens: bfloat16 [2, 8192, 2048], P('dp', 'ctx', 'tensor'), may hold values from -6 to 6
- lengths: int32 [2], P('dp'), may hold values from 2048 to 8192, as said below
- conv_first: float32 [4, 2048], P(None, 'tensor'), may hold values from -3 to 3
- conv_second: float32 [4, 2048], P(None, 'tensor'), may hold values from -3 to 3
- norm_gain: float32 [2048], replicated, may hold values from 0.1 to 1.9
- w_query: bfloat16 [2048, 2048], P(None, 'tensor'), may hold values from -0.125 to 0.125
- w_key: bfloat16 [2048, 2048], P(None, 'tensor'), may hold values from -0.125 to 0.125
- w_value: bfloat16 [2048, 2048], P(None, 'tensor'), may hold values from -0.125 to 0.125
- w_out: bfloat16 [2048, 2048], P(None, 'tensor'), may hold values from -0.5 to 0.5
- bias_table: float32 [32, 16], P(None, 'tensor'), may hold values from -8 to 260
- buckets: int32 [512], replicated, may hold values from 0 to 31, as said below
- up_gain: float32 [16, 2048], P(None, 'tensor'), may hold values from 0.1 to 1.9
- grad_out: bfloat16 [2, 8192, 2048], P('dp', 'ctx', 'tensor'), may hold values from -6 to 6
Outputs:
- update: bfloat16 [2, 8192, 2048], P('dp', 'ctx', 'tensor')
- grad_tokens: bfloat16 [2, 8192, 2048], P('dp', 'ctx', 'tensor')
- grad_w_query: float32 [2048, 2048], P(('dp', 'ctx'), 'tensor')
- grad_w_key: float32 [2048, 2048], P(('dp', 'ctx'), 'tensor')
- grad_w_value: float32 [2048, 2048], P(('dp', 'ctx'), 'tensor')
- grad_w_out: float32 [2048, 2048], P(('dp', 'ctx'), 'tensor')
The draws below stay inside these ranges and needn't reach their ends.
Inputs may be any that keep to these rules, and one draw needn't show every extreme that they name: `lengths`: at least one document is exactly 8192 bytes long. `buckets`: non-decreasing in the distance, 0 at distance 0 and 31 at the largest distance.
All inputs are finite; a program needn't handle non-finite values.
Results may differ from the reference program's by a relative error of at most 0.03.
Values may be sent and summed in bfloat16 or wider, within the bound.
No kernel may reach another device: no remote copies, remote signals or barrier semaphores. Data moves between devices by JAX's collectives and lax.ppermute only.
A program may use at most 128 MiB of HBM per device.

```python
import math
import jax
import jax.numpy as jnp
from jax import lax

D = 2048
HEADS = 16
HEAD_DIM = 128
BUCKETS = 32
DOCS = 2
S = 8192
LC_DEV = 32
LC = 512
N_CTX = 16


def draw_lengths(key, part):
    key = jax.random.fold_in(key, 11)
    first_key, second_key = jax.random.split(key)
    base = jax.random.randint(first_key, (DOCS,), S // 4, S + 1)
    chosen = jax.random.randint(second_key, (), 0, DOCS)
    return jnp.where(jnp.arange(DOCS) == chosen, S, base).astype(jnp.int32)


def draw_buckets(key, part):
    key = jax.random.fold_in(key, 23)
    distance = jnp.arange(LC, dtype=jnp.int32)
    picks = jax.random.randint(key, (LC,), 0, distance + 4)
    steps_up = ((picks < 4) & (distance > 0)).astype(jnp.int32)
    levels = jnp.minimum(jnp.cumsum(steps_up), BUCKETS - 1)
    return jnp.where(distance == LC - 1, BUCKETS - 1, levels).astype(jnp.int32)


def draw_bias_table(key, part):
    key = jax.random.fold_in(key, 37)
    first_key = jax.random.fold_in(key, 0)
    return jnp.clip(2.0 * jax.random.normal(first_key, (BUCKETS, HEADS)), -8.0, 8.0).astype(jnp.float32)


def block_scale(own_key, dims, pieces, least, top_value):
    gain = 1.0
    for dim, parts in pieces:
        steps = jax.random.uniform(jax.random.fold_in(jax.random.fold_in(own_key, 6), dim), (parts,), jnp.float32, least / len(pieces), top_value / len(pieces))
        gain = gain * jnp.repeat(jnp.exp(steps), dims[dim] // parts).reshape((-1,) + (1,) * (len(dims) - 1 - dim))
    return gain


def normal_values(rng, dims, deviation, most, shards=(), kind=jnp.bfloat16):
    values = deviation * jax.random.normal(rng, dims, jnp.float32)
    if shards:
        values = values * block_scale(rng, dims, shards, -0.22, 0.18)
    return jnp.clip(values, -most, most).astype(kind)


def setup_inputs(seed: int = 0) -> dict:
    key_list = jax.random.split(jax.random.key(seed), 14)
    tokens = normal_values(key_list[0], (DOCS, S, D), 1.0, 6.0, ((0, 2), (1, 16), (2, 4)))
    lengths = draw_lengths(jax.random.fold_in(key_list[13], 71), 0)
    conv_first = normal_values(key_list[2], (4, D), 4 ** -0.5, 3.0, ((1, 4),), jnp.float32)
    conv_second = normal_values(key_list[3], (4, D), 4 ** -0.5, 3.0, ((1, 4),), jnp.float32)
    norm_gain = jnp.clip(1.0 + 0.18 * jax.random.normal(key_list[4], (D,), jnp.float32), 0.1, 1.9)
    w_query = normal_values(key_list[5], (D, D), D ** -0.5, 0.125, ((1, 4),))
    w_key = normal_values(key_list[6], (D, D), D ** -0.5, 0.125, ((1, 4),))
    w_value = normal_values(key_list[7], (D, D), D ** -0.5, 0.125, ((1, 4),))
    w_out = normal_values(key_list[8], (D, D), (D // 16) ** -0.5, 0.5, ((1, 4),))
    bias_table = draw_bias_table(jax.random.fold_in(key_list[13], 71), 0)
    buckets = draw_buckets(jax.random.fold_in(key_list[13], 71), 0)
    up_gain = jnp.clip(1.0 + 0.18 * jax.random.normal(key_list[11], (16, D), jnp.float32), 0.1, 1.9)
    grad_out = normal_values(key_list[12], (DOCS, S, D), 1.0, 6.0, ((0, 2), (1, 16), (2, 4)))
    return dict(tokens=tokens, lengths=lengths, conv_first=conv_first, conv_second=conv_second, norm_gain=norm_gain, w_query=w_query, w_key=w_key, w_value=w_value, w_out=w_out, bias_table=bias_table, buckets=buckets, up_gain=up_gain, grad_out=grad_out)


def rounded(array):
    return lax.optimization_barrier(array.astype(jnp.bfloat16)).astype(jnp.float32)

def block_probs(queries, keys_all, dist_bias, key_valid, first_row):
    rows = queries.shape[0]
    query_pos = first_row + jnp.arange(rows, dtype=jnp.int32)
    key_pos = jnp.arange(keys_all.shape[0], dtype=jnp.int32)
    distance = query_pos[:, None] - key_pos[None, :]
    allowed = (distance >= 0) & key_valid[None, :]
    lookup = jnp.take(dist_bias, jnp.clip(distance, 0, keys_all.shape[0] - 1), axis=0)
    scores = jnp.einsum('qhd,khd->hqk', queries.astype(jnp.float32), keys_all.astype(jnp.float32))
    scores = scores * (1.0 / math.sqrt(queries.shape[2])) + jnp.transpose(lookup, (2, 0, 1))
    scores = jnp.where(allowed[None], scores, -jnp.inf)
    row_max = lax.optimization_barrier(jnp.max(scores, axis=2, keepdims=True))
    raised = jnp.exp(scores - row_max)
    return raised / lax.optimization_barrier(jnp.sum(raised, axis=2, keepdims=True))

def reference(tokens, lengths, conv_first, conv_second, norm_gain, w_query, w_key, w_value, w_out, bias_table, buckets, up_gain, grad_out):
    score_scale = 1.0 / math.sqrt(HEAD_DIM)
    one_hot = (buckets[:, None] == jnp.arange(BUCKETS, dtype=jnp.int32)[None, :]).astype(jnp.float32)
    dist_bias = jnp.dot(one_hot, bias_table, precision=lax.Precision.HIGHEST)
    updates = []
    grad_inputs = []
    grad_wq = jnp.zeros((D, D), jnp.float32)
    grad_wk = jnp.zeros((D, D), jnp.float32)
    grad_wv = jnp.zeros((D, D), jnp.float32)
    grad_wo = jnp.zeros((D, D), jnp.float32)
    for doc_idx in range(DOCS):
        doc_len = lengths[doc_idx]
        byte_mask = (jnp.arange(S, dtype=jnp.int32) < doc_len).astype(jnp.float32)
        masked = tokens[doc_idx] * byte_mask[:, None].astype(jnp.bfloat16)
        shifted = jnp.concatenate([jnp.zeros((15, D), jnp.bfloat16), masked[:S - 15]], axis=0).astype(jnp.float32)
        level_one = lax.optimization_barrier(jnp.sum(shifted.reshape(S // 4, 4, D) * conv_first[None], axis=1))
        level_two = lax.optimization_barrier(jnp.sum(level_one.reshape(LC, 4, D) * conv_second[None], axis=1))
        coarse_f = rounded(level_two)
        inv_rms = lax.rsqrt(lax.optimization_barrier(jnp.mean(coarse_f * coarse_f, axis=1, keepdims=True)) + 1e-06)
        normed = (coarse_f * inv_rms * norm_gain[None]).astype(jnp.bfloat16)
        queries = jnp.dot(normed, w_query, preferred_element_type=jnp.float32).astype(jnp.bfloat16)
        keys_all = jnp.dot(normed, w_key, preferred_element_type=jnp.float32).astype(jnp.bfloat16)
        values_all = jnp.dot(normed, w_value, preferred_element_type=jnp.float32).astype(jnp.bfloat16)
        q_three = queries.reshape(LC, HEADS, HEAD_DIM)
        k_three = keys_all.reshape(LC, HEADS, HEAD_DIM)
        v_three = values_all.reshape(LC, HEADS, HEAD_DIM)
        key_valid = 16 * jnp.arange(LC, dtype=jnp.int32) < doc_len

        def forward_block(unused, block_idx):
            first_row = (block_idx * LC_DEV).astype(jnp.int32)
            q_block = lax.dynamic_slice_in_dim(q_three, first_row, LC_DEV, 0)
            probs = block_probs(q_block, k_three, dist_bias, key_valid, first_row)
            mixed_vals = jnp.einsum('hqk,khd->qhd', rounded(probs), v_three.astype(jnp.float32))
            return (unused, mixed_vals.astype(jnp.bfloat16).reshape(LC_DEV, D))
        unused_end, attended = lax.scan(forward_block, jnp.zeros((), jnp.float32), jnp.arange(N_CTX, dtype=jnp.int32))
        attended = attended.reshape(LC, D)
        outputs = jnp.dot(attended, w_out.T, preferred_element_type=jnp.float32)
        update = ((outputs[:, None, :] * up_gain[None]).reshape(S, D) * byte_mask[:, None]).astype(jnp.bfloat16)
        weighted = grad_out[doc_idx].astype(jnp.float32) * byte_mask[:, None]
        grad_coarse_out = lax.optimization_barrier(jnp.sum(weighted.reshape(LC, 16, D) * up_gain[None], axis=1)).astype(jnp.bfloat16)
        grad_wo = grad_wo + jnp.dot(grad_coarse_out.T, attended, preferred_element_type=jnp.float32)
        grad_attended = jnp.dot(grad_coarse_out, w_out, preferred_element_type=jnp.float32).astype(jnp.bfloat16)
        ga_three = grad_attended.reshape(LC, HEADS, HEAD_DIM)
        at_three = attended.reshape(LC, HEADS, HEAD_DIM)

        def backward_block(running, block_idx):
            first_row = (block_idx * LC_DEV).astype(jnp.int32)
            q_block = lax.dynamic_slice_in_dim(q_three, first_row, LC_DEV, 0)
            ga_block = lax.dynamic_slice_in_dim(ga_three, first_row, LC_DEV, 0).astype(jnp.float32)
            at_block = lax.dynamic_slice_in_dim(at_three, first_row, LC_DEV, 0).astype(jnp.float32)
            probs = block_probs(q_block, k_three, dist_bias, key_valid, first_row)
            dprob = jnp.einsum('qhd,khd->hqk', ga_block, v_three.astype(jnp.float32))
            row_dot = lax.optimization_barrier(jnp.sum(ga_block * at_block, axis=2)).T
            soft_grad = rounded(probs * (dprob - row_dot[:, :, None]))
            grad_q_block = jnp.einsum('hqk,khd->qhd', soft_grad, k_three.astype(jnp.float32)) * score_scale
            term_key = jnp.einsum('hqk,qhd->khd', soft_grad, q_block.astype(jnp.float32)) * score_scale
            term_value = jnp.einsum('hqk,qhd->khd', rounded(probs), ga_block)
            running = (running[0] + rounded(term_key).reshape(LC, D), running[1] + rounded(term_value).reshape(LC, D))
            return (running, grad_q_block.astype(jnp.bfloat16).reshape(LC_DEV, D))
        start_sums = (jnp.zeros((LC, D), jnp.float32), jnp.zeros((LC, D), jnp.float32))
        sums_end, grad_queries = lax.scan(backward_block, start_sums, jnp.arange(N_CTX, dtype=jnp.int32))
        grad_queries = grad_queries.reshape(LC, D)
        grad_keys = sums_end[0].astype(jnp.bfloat16)
        grad_values = sums_end[1].astype(jnp.bfloat16)
        grad_normed = jnp.dot(grad_queries, w_query.T, preferred_element_type=jnp.float32)
        grad_normed = grad_normed + jnp.dot(grad_keys, w_key.T, preferred_element_type=jnp.float32)
        grad_normed = grad_normed + jnp.dot(grad_values, w_value.T, preferred_element_type=jnp.float32)
        gained = grad_normed * norm_gain[None]
        row_dots = lax.optimization_barrier(jnp.sum(gained * coarse_f, axis=1, keepdims=True))
        grad_coarse = inv_rms * gained - coarse_f * (inv_rms * inv_rms * inv_rms) * row_dots / D
        grad_level_one = (grad_coarse[:, None, :] * conv_second[None]).reshape(S // 4, D)
        grad_shifted = (grad_level_one[:, None, :] * conv_first[None]).reshape(S, D)
        grad_masked = jnp.concatenate([grad_shifted[15:], jnp.zeros((15, D), jnp.float32)], axis=0)
        grad_inputs.append((grad_masked * byte_mask[:, None]).astype(jnp.bfloat16))
        updates.append(update)
        grad_wq = grad_wq + jnp.dot(normed.T, grad_queries, preferred_element_type=jnp.float32)
        grad_wk = grad_wk + jnp.dot(normed.T, grad_keys, preferred_element_type=jnp.float32)
        grad_wv = grad_wv + jnp.dot(normed.T, grad_values, preferred_element_type=jnp.float32)
    return (jnp.stack(updates, axis=0), jnp.stack(grad_inputs, axis=0), grad_wq, grad_wk, grad_wv, grad_wo)
```

```python
import math

import jax
import jax.numpy as jnp
import numpy as np
from jax import lax
from jax.experimental import pallas as pl
from jax.experimental.pallas import tpu as pltpu
from jax.sharding import Mesh, PartitionSpec as P

F32 = jnp.float32
BF16 = jnp.bfloat16
NEG = float("-inf")
D = 2048
WL = 512
LC = 512
CL = 32
SEG = 512
HD = 128
NH = 4
SCALE = 1.0 / math.sqrt(HD)
ROWS = CL + 16
VM = pltpu.VMEM
SM = pltpu.SMEM


def dg(a, b, ca, cb):
    return lax.dot_general(a, b, (((ca,), (cb,)), ((), ())), preferred_element_type=F32)


def tap_weights(first, second):
    taps = jnp.concatenate([second[a : a + 1] * first for a in range(4)], axis=0)
    return jnp.concatenate([taps[15:16], taps[:15]], axis=0)


def byte_mask(ctx, doc_len):
    pos = ctx * SEG + 16 * lax.broadcasted_iota(jnp.int32, (CL, 16, WL), 0)
    pos = pos + lax.broadcasted_iota(jnp.int32, (CL, 16, WL), 1)
    return (pos < doc_len).astype(F32)


def before_kernel(sc, tokens, grad_out, first, second, up_gain, part, last, gco, shift):
    mask = byte_mask(sc[0], sc[1])
    taps = tap_weights(first[...], second[...])
    u = lax.broadcasted_iota(jnp.int32, (CL, 16, WL), 1)
    prod = tokens[...].astype(F32).reshape(CL, 16, WL) * mask * taps[None]
    own = jnp.sum(jnp.where(u == 0, prod, 0.0), axis=1)
    onward = jnp.sum(jnp.where(u == 0, 0.0, prod), axis=1)
    shift[0:8] = jnp.zeros((8, WL), F32)
    shift[8 : 8 + CL] = onward
    part[...] = own + shift[7 : 7 + CL]
    last[...] = jnp.broadcast_to(shift[7 + CL : 8 + CL], (8, WL))
    weighted = grad_out[...].astype(F32).reshape(CL, 16, WL) * mask * up_gain[...][None]
    gco[...] = jnp.sum(weighted, axis=1).astype(BF16)


def bias_kernel(near, table, strip):
    n = near.shape[1]
    which = near[0:1]
    for h in range(NH):
        row = jnp.full((1, n), NEG, F32)
        for b in range(table.shape[0]):
            row = jnp.where(which == b, table[b, h], row)
        rolled = pltpu.roll(jnp.broadcast_to(row, (128, n)), 0, 1, stride=1, stride_axis=0)
        strip[h] = rolled[:, :LC]


def middle_kernel(
    sc, own, rec, gain, wq, wk, wv, wo, strip,
    msg1, msg2, msg3, keep, cz, inv_out, dw_own, dw_send,
    nrm, gco, q, k, v, ga, att, gq, gk, gv, inv, acck, accv, tile,
):
    core, ctx, dp, z, doc_len = sc[0], sc[1], sc[2], sc[3], sc[4]

    def spread(i, carry):
        for src, c in ((own, core), (rec, 1 - core)):
            rows = pl.ds(pl.multiple_of((i * 2 + c) * CL, CL), CL)
            blocks = [src[i * 4 + t, 0:CL].astype(F32) for t in range(4)]
            total = sum(jnp.sum(b * b, axis=1, keepdims=True) for b in blocks)
            r = lax.rsqrt(total * (1.0 / D) + 1e-6)
            inv[rows] = jnp.broadcast_to(r, (CL, 128))
            for t in range(4):
                cols = slice(t * WL, t * WL + WL)
                nrm[rows, cols] = (blocks[t] * r * gain[0:1, cols]).astype(BF16)
                gco[rows, cols] = src[i * 4 + t, CL : 2 * CL]
        return carry

    lax.fori_loop(0, 8, spread, 0)

    def project(i, carry):
        rows = pl.ds(pl.multiple_of(i * 256, 256), 256)
        for dst, src, w in ((q, nrm, wq), (k, nrm, wk), (v, nrm, wv), (ga, gco, wo)):
            dst[rows] = jnp.dot(src[rows], w[...], preferred_element_type=F32).astype(BF16)
        return carry

    lax.fori_loop(0, 2, project, 0)

    key_pos = lax.broadcasted_iota(jnp.int32, (1, LC), 1)
    key_mask = jnp.where(16 * key_pos < doc_len, 0.0, NEG)

    def head(h, carry):
        cols = pl.ds(pl.multiple_of(h * HD, HD), HD)
        for b in (3, 2, 1, 0):
            rows = slice(b * 128, b * 128 + 128)
            n = b * 128 + 128
            qb, gb, kb, vb = q[rows, cols], ga[rows, cols], k[0:n, cols], v[0:n, cols]
            s = dg(qb, kb, 1, 1) * SCALE + strip[h, :, LC - n :] + key_mask[:, :n]
            e = jnp.exp(s - jnp.max(s, axis=1, keepdims=True))
            p = e * (1.0 / jnp.sum(e, axis=1, keepdims=True))
            pb = p.astype(BF16)
            ab = jnp.dot(pb, vb, preferred_element_type=F32).astype(BF16)
            att[rows, cols] = ab
            dot = jnp.sum(gb.astype(F32) * ab.astype(F32), axis=1, keepdims=True)
            sg = (p * (dg(gb, vb, 1, 1) - dot)).astype(BF16)
            gq[rows, cols] = (jnp.dot(sg, kb, preferred_element_type=F32) * SCALE).astype(BF16)
            tk = dg(sg, qb, 0, 0)
            tv = dg(pb, gb, 0, 0)
            if b == 3:
                acck[...] = tk
                accv[...] = tv
            else:
                acck[0:n] += tk
                accv[0:n] += tv
        gk[0:LC, cols] = (acck[...] * SCALE).astype(BF16)
        gv[0:LC, cols] = accv[...].astype(BF16)
        return carry

    lax.fori_loop(0, NH, head, 0)
    for g in (gq, gk, gv):
        g[LC : LC + 16] = jnp.zeros((16, WL), BF16)
    inv[LC : LC + 16] = jnp.zeros((16, 128), F32)

    half = pl.ds(pl.multiple_of(core * 64, 64), 64)
    for which, d in ((0, dp), (1, 1 - dp)):
        cols = pl.ds(pl.multiple_of((d * 8 + ctx // 2) * 128, 128), 128)
        for w, (src, g) in enumerate(((nrm, gq), (nrm, gk), (nrm, gv), (gco, att))):
            tile[...] = dg(src[:, cols], g[0:LC], 0, 0)
            if which == 0:
                dw_own[w] = tile[half]
            else:
                dw_send[w] = tile[half].astype(BF16)

    mine = pl.ds(pl.multiple_of(ctx * CL, CL), CL)
    more = pl.ds(pl.multiple_of(ctx * CL, CL), ROWS)
    here = ctx // 2
    there = jnp.minimum((ctx + 1) // 2, 7)
    gq_m, gk_m, gv_m, att_m = gq[more], gk[more], gv[more], att[mine]
    lane = lax.broadcasted_iota(jnp.int32, (ROWS, 128), 1)
    dots = jnp.zeros((ROWS, 1), F32)
    for shift, msg in ((1, msg1), (2, msg2), (3, msg3), (0, keep)):
        t = lax.rem(z + shift, 4)
        part = pl.ds(pl.multiple_of(t * WL, WL), WL)
        gn = dg(gq_m, wq[part], 1, 1) + dg(gk_m, wk[part], 1, 1) + dg(gv_m, wv[part], 1, 1)
        c0 = own[here * 4 + t, 0:CL]
        c1 = rec[there * 4 + t, 0:16]
        gained = gn * gain[0:1, part]
        d0 = jnp.sum(gained[0:CL] * c0.astype(F32), axis=1, keepdims=True)
        d1 = jnp.sum(gained[CL:ROWS] * c1.astype(F32), axis=1, keepdims=True)
        dots = dots + jnp.concatenate([d0, d1], axis=0)
        msg[0:CL, 0:WL] = dg(att_m, wo[part], 1, 1).astype(msg.dtype)
        msg[CL : CL + ROWS, 0:WL] = gn.astype(msg.dtype)
        msg[0:CL, WL : WL + 128] = jnp.zeros((CL, 128), msg.dtype)
        if shift == 0:
            cz[0:CL] = c0
            cz[CL:ROWS] = c1
    keep[CL : CL + ROWS, WL : WL + 128] = jnp.broadcast_to(dots, (ROWS, 128))
    hi = dots.astype(BF16)
    lo = (dots - hi.astype(F32)).astype(BF16)
    lo2 = (dots - hi.astype(F32) - lo.astype(F32)).astype(BF16)
    packed = jnp.where(lane == 0, hi.astype(F32), jnp.where(lane == 1, lo.astype(F32), lo2.astype(F32)))
    packed = jnp.where(lane < 3, packed, 0.0).astype(BF16)
    for msg in (msg1, msg2, msg3):
        msg[CL : CL + ROWS, WL : WL + 128] = packed
    inv_out[...] = inv[more]


def after_kernel(sc, keep, r1, r2, r3, cz, inv, gain, first, second, up_gain, update, grad, rows):
    ctx, doc_len, z = sc[0], sc[1], sc[2]
    mask = byte_mask(ctx, doc_len)
    body = slice(0, WL)
    out = keep[0:CL, body]
    gn = keep[CL : CL + ROWS, body]
    dots = keep[CL : CL + ROWS, WL : WL + 1]
    for r in (r1, r2, r3):
        out = out + r[0:CL, body].astype(F32)
        gn = gn + r[CL : CL + ROWS, body].astype(F32)
        dots = dots + jnp.sum(r[CL : CL + ROWS, WL : WL + 128].astype(F32), axis=1, keepdims=True)
    update[...] = ((out[:, None, :] * up_gain[...][None]) * mask).reshape(SEG, WL).astype(BF16)
    i = inv[:, 0:1]
    gained = gn * gain[0:1, pl.ds(pl.multiple_of(z * WL, WL), WL)]
    full = i * gained - cz[...].astype(F32) * (i * i * i) * dots * (1.0 / D)
    exists = lax.broadcasted_iota(jnp.int32, (ROWS, WL), 0) + ctx * CL < LC
    rows[...] = jnp.where(exists, full, 0.0)
    taps = tap_weights(first[...], second[...])
    u = lax.broadcasted_iota(jnp.int32, (CL, 16, WL), 1)
    picked = jnp.where(u == 0, rows[0:CL][:, None, :], rows[1 : CL + 1][:, None, :])
    grad[...] = (picked * taps[None] * mask).reshape(SEG, WL).astype(BF16)


def call(kernel, outs, n_in, scratch=(), smem=(0,), flops=0, size=0, vmem=48 * 2**20):
    return pl.pallas_call(
        kernel,
        out_shape=[jax.ShapeDtypeStruct(s, d) for s, d in outs],
        in_specs=[pl.BlockSpec(memory_space=SM if i in smem else VM) for i in range(n_in)],
        out_specs=[pl.BlockSpec(memory_space=VM)] * len(outs),
        scratch_shapes=list(scratch),
        compiler_params=pltpu.CompilerParams(vmem_limit_bytes=vmem),
        cost_estimate=pl.CostEstimate(flops=flops, bytes_accessed=size, transcendentals=0),
    )


def shifted(x, axis, steps):
    n = lax.axis_size(axis)
    return lax.ppermute(x, axis, [(i, (i + steps) % n) for i in range(n)])


def local(
    tokens, lengths, conv_first, conv_second, norm_gain, w_query, w_key, w_value, w_out,
    bias_table, buckets, up_gain, grad_out,
):
    x, y, core = lax.axis_index("x"), lax.axis_index("y"), lax.axis_index("core")
    dp, z = lax.axis_index("dp"), lax.axis_index("tensor")
    ctx = (x * 2 + y) * 2 + core
    doc_len = lengths[0]
    small = jnp.stack([ctx, doc_len, z]).astype(jnp.int32)
    part, last, gco = call(
        before_kernel,
        [((CL, WL), F32), ((8, WL), F32), ((CL, WL), BF16)],
        6,
        [pltpu.VMEM((CL + 8, WL), F32)],
    )(small, tokens[0], grad_out[0], conv_first, conv_second, up_gain)
    rim = lax.ppermute(last, ("x", "y", "core"), [(i, i + 1) for i in range(15)])
    is_first = (jnp.arange(CL) == 0)[:, None]
    coarse = (part + jnp.where(is_first, rim[0:1], 0.0)).astype(BF16)
    payload = jnp.concatenate([coarse, gco], axis=0)
    own = lax.all_to_all(
        jnp.broadcast_to(payload[None], (32, 2 * CL, WL)), ("x", "y", "tensor"), 0, 0, tiled=True
    )
    rec = shifted(own, "core", 1)
    n = 640
    near = jnp.concatenate(
        [
            jnp.flip(buckets[:385]),
            jnp.full((n - LC,), bias_table.shape[0], jnp.int32),
            jnp.flip(buckets[385:]),
        ]
    )
    (strip,) = call(bias_kernel, [((NH, 128, LC), F32)], 2, smem=(1,))(
        jnp.broadcast_to(near[None], (8, n)), bias_table
    )
    gain = norm_gain[None]
    msg = (CL + ROWS, WL + 128)
    big = lambda rows: pltpu.VMEM((rows, WL), BF16)
    m1, m2, m3, keep, cz, inv, dw_own, dw_send = call(
        middle_kernel,
        [
            (msg, BF16), (msg, BF16), (msg, BF16), (msg, F32), ((ROWS, WL), BF16), ((ROWS, 128), F32),
            ((4, 64, WL), F32), ((4, 64, WL), BF16),
        ],
        9,
        [
            pltpu.VMEM((LC, D), BF16), pltpu.VMEM((LC, D), BF16),
            big(LC), big(LC), big(LC), big(LC), big(LC), big(LC + 16), big(LC + 16), big(LC + 16),
            pltpu.VMEM((LC + 16, 128), F32), pltpu.VMEM((LC, HD), F32), pltpu.VMEM((LC, HD), F32),
            pltpu.VMEM((128, WL), F32),
        ],
        flops=10**10,
        size=2 * 10**7,
    )(
        jnp.stack([core, ctx, dp, z, doc_len]).astype(jnp.int32),
        own, rec, gain, w_query, w_key, w_value, w_out, strip,
    )
    r1, r2, r3 = shifted(m1, "tensor", 1), shifted(m2, "tensor", 2), shifted(m3, "tensor", 3)
    other = shifted(dw_send, "dp", 1)
    update, grad_tokens = call(
        after_kernel,
        [((SEG, WL), BF16), ((SEG, WL), BF16)],
        11,
        [pltpu.VMEM((ROWS, WL), F32)],
    )(small, keep, r1, r2, r3, cz, inv, gain, conv_first, conv_second, up_gain)
    dw = dw_own + other.astype(F32)
    return (update[None], grad_tokens[None], dw[0], dw[1], dw[2], dw[3])


def solution(mesh):
    ctx = ("x", "y", "core")
    fine = Mesh(
        np.asarray(mesh.devices).reshape(2, 4, 2, 2, 4), ("dp", "x", "y", "core", "tensor")
    )
    tok = P("dp", ctx, "tensor")
    col = P(None, "tensor")
    in_specs = (tok, P("dp"), col, col, P(), col, col, col, col, col, P(), col, tok)
    dw = P(("dp",) + ctx, "tensor")
    return jax.shard_map(
        local, mesh=fine, in_specs=in_specs, out_specs=(tok, tok, dw, dw, dw, dw), check_vma=False
    )
```

```python
import math

import jax
import jax.numpy as jnp
import numpy as np
from jax import lax
from jax.experimental import pallas as pl
from jax.experimental.pallas import tpu as pltpu
from jax.sharding import Mesh, PartitionSpec as P

F32 = jnp.float32
BF16 = jnp.bfloat16
NEG = float("-inf")
D = 2048
WL = 512
LC = 512
CL = 32
SEG = 512
HD = 128
NH = 2
HW = NH * HD
SCALE = 1.0 / math.sqrt(HD)
ROWS = CL + 16
VM = pltpu.VMEM
SM = pltpu.SMEM


def dg(a, b, ca, cb):
    return lax.dot_general(a, b, (((ca,), (cb,)), ((), ())), preferred_element_type=F32)


def tap_weights(first, second):
    taps = jnp.concatenate([second[a : a + 1] * first for a in range(4)], axis=0)
    return jnp.concatenate([taps[15:16], taps[:15]], axis=0)


def byte_mask(ctx, doc_len):
    pos = ctx * SEG + 16 * lax.broadcasted_iota(jnp.int32, (CL, 16, WL), 0)
    pos = pos + lax.broadcasted_iota(jnp.int32, (CL, 16, WL), 1)
    return (pos < doc_len).astype(F32)


def before_kernel(sc, tokens, grad_out, first, second, up_gain, part, last, gco, shift):
    mask = byte_mask(sc[0], sc[1])
    taps = tap_weights(first[...], second[...])
    u = lax.broadcasted_iota(jnp.int32, (CL, 16, WL), 1)
    prod = tokens[...].astype(F32).reshape(CL, 16, WL) * mask * taps[None]
    own = jnp.sum(jnp.where(u == 0, prod, 0.0), axis=1)
    onward = jnp.sum(jnp.where(u == 0, 0.0, prod), axis=1)
    shift[0:8] = jnp.zeros((8, WL), F32)
    shift[8 : 8 + CL] = onward
    part[...] = own + shift[7 : 7 + CL]
    last[...] = jnp.broadcast_to(shift[7 + CL : 8 + CL], (8, WL))
    weighted = grad_out[...].astype(F32).reshape(CL, 16, WL) * mask * up_gain[...][None]
    gco[...] = jnp.sum(weighted, axis=1).astype(BF16)


def bias_kernel(sc, near, table, strip):
    n = near.shape[1]
    which = near[0:1]
    for h in range(NH):
        row = jnp.full((1, n), NEG, F32)
        for b in range(table.shape[0]):
            row = jnp.where(which == b, table[b, sc[3] * NH + h], row)
        rolled = pltpu.roll(jnp.broadcast_to(row, (128, n)), 0, 1, stride=1, stride_axis=0)
        strip[h] = rolled[:, :LC]


def project_kernel(
    sc, p0, r1, r2, r3, gain, wq, wk, wv, wo, keep, send, blocks, craw, first, nrm, gco, both
):
    z, core = sc[2], sc[3]
    for s, src in enumerate((p0, r1, r2, r3)):
        cols = pl.ds(pl.multiple_of(lax.rem(z + 4 - s, 4) * WL, WL), WL)
        craw[:, cols] = src[0:CL]
        gco[:, cols] = src[CL : 2 * CL]
    first[...] = craw[0:16]
    c = craw[...].astype(F32)
    r = lax.rsqrt(jnp.sum(c * c, axis=1, keepdims=True) * (1.0 / D) + 1e-6)
    nrm[...] = (c * r * gain[...]).astype(BF16)
    for i, (src, w) in enumerate(((nrm, wq), (nrm, wk), (nrm, wv), (gco, wo))):
        y = jnp.dot(src[...], w[...], preferred_element_type=F32).astype(BF16)
        for half in range(2):
            both[half, :, i * HW : i * HW + HW] = y[:, half * HW : half * HW + HW]
    keep[...] = both[core]
    send[...] = both[1 - core]
    for chip in range(8):
        for d in range(2):
            cols = slice((d * 8 + chip) * 128, (d * 8 + chip) * 128 + 128)
            for part in range(2):
                rows = slice(part * 16, part * 16 + 16)
                at = part * 512 + d * 128
                blocks[chip, :, at : at + 128] = nrm[rows, cols]
                blocks[chip, :, at + 256 : at + 384] = gco[rows, cols]


def attend_kernel(sc, got, strip, res, keep, send, q, k, v, ga, acck, accv):
    ctx, doc_len, core = sc[0], sc[1], sc[3]
    for i, dst in enumerate((q, k, v, ga)):
        dst[...] = got[:, 0:64, i * HW : i * HW + HW].reshape(LC, HW)
    key_pos = lax.broadcasted_iota(jnp.int32, (1, LC), 1)
    key_mask = jnp.where(16 * key_pos < doc_len, 0.0, NEG)
    for h in range(NH):
        cols = slice(h * HD, h * HD + HD)
        for b in (3, 2, 1, 0):
            rows = slice(b * 128, b * 128 + 128)
            n = b * 128 + 128
            qb, gb, kb, vb = q[rows, cols], ga[rows, cols], k[0:n, cols], v[0:n, cols]
            s = dg(qb, kb, 1, 1) * SCALE + strip[h, :, LC - n :] + key_mask[:, :n]
            e = jnp.exp(s - jnp.max(s, axis=1, keepdims=True))
            p = e * (1.0 / jnp.sum(e, axis=1, keepdims=True))
            pb = p.astype(BF16)
            ab = jnp.dot(pb, vb, preferred_element_type=F32).astype(BF16)
            res[3, rows, cols] = ab
            dot = jnp.sum(gb.astype(F32) * ab.astype(F32), axis=1, keepdims=True)
            sg = (p * (dg(gb, vb, 1, 1) - dot)).astype(BF16)
            res[0, rows, cols] = (jnp.dot(sg, kb, preferred_element_type=F32) * SCALE).astype(BF16)
            tk = dg(sg, qb, 0, 0)
            tv = dg(pb, gb, 0, 0)
            if b == 3:
                acck[h] = tk
                accv[h] = tv
            else:
                acck[h, 0:n] += tk
                accv[h, 0:n] += tv
        res[1, 0:LC, cols] = (acck[h] * SCALE).astype(BF16)
        res[2, 0:LC, cols] = accv[h].astype(BF16)
    res[:, LC : LC + 16] = jnp.zeros((4, 16, HW), BF16)
    peer = ctx + 1 - 2 * core
    keep[...] = res[:, pl.ds(pl.multiple_of(ctx * CL, CL), ROWS)]
    send[...] = res[:, pl.ds(pl.multiple_of(peer * CL, CL), ROWS)]


def weights_kernel(sc, res, mine, other, keep, send, nb, gb, tile):
    core = sc[3]
    for chip in range(8):
        for src, c in ((mine, core), (other, 1 - core)):
            for part in range(2):
                rows = pl.ds(pl.multiple_of(chip * 64 + c * CL + part * 16, 16), 16)
                nb[rows] = src[chip, :, part * 512 : part * 512 + 256]
                gb[rows] = src[chip, :, part * 512 + 256 : part * 512 + 512]
    for w in range(4):
        tile[...] = dg((gb if w == 3 else nb)[...], res[w, 0:LC], 0, 0)
        for d in range(2):
            keep[w, d] = tile[pl.ds(pl.multiple_of(d * 128 + core * 64, 64), 64)]
            send[w, d] = tile[pl.ds(pl.multiple_of(d * 128 + 64 - core * 64, 64), 64)].astype(BF16)


def join_kernel(sc, keep, got, own, send):
    core, dp = sc[3], sc[4]
    a = pl.ds(pl.multiple_of(core * HW, HW), HW)
    b = pl.ds(pl.multiple_of((1 - core) * HW, HW), HW)
    own[:, :, a] = keep[:, dp]
    own[:, :, b] = got[:, dp].astype(F32)
    send[:, :, a] = keep[:, 1 - dp].astype(BF16)
    send[:, :, b] = got[:, 1 - dp]


def partial_kernel(
    sc, keep_r, got_r, craw, nxt, gain, wq, wk, wv, wo, msg1, msg2, msg3, keep, cz, inv_out, g, c
):
    z, core = sc[2], sc[3]
    g[:, :, pl.ds(pl.multiple_of(core * HW, HW), HW)] = keep_r[...]
    g[:, :, pl.ds(pl.multiple_of((1 - core) * HW, HW), HW)] = got_r[...]
    c[0:CL] = craw[...]
    c[CL:ROWS] = nxt[...]
    cf = c[...].astype(F32)
    r = lax.rsqrt(jnp.sum(cf * cf, axis=1, keepdims=True) * (1.0 / D) + 1e-6)
    inv_out[...] = jnp.broadcast_to(r, (ROWS, 128))
    lane = lax.broadcasted_iota(jnp.int32, (ROWS, 128), 1)
    dots = jnp.zeros((ROWS, 1), F32)
    for shift, msg in ((1, msg1), (2, msg2), (3, msg3), (0, keep)):
        t = lax.rem(z + shift, 4)
        part = pl.ds(pl.multiple_of(t * WL, WL), WL)
        gn = dg(g[0], wq[part], 1, 1) + dg(g[1], wk[part], 1, 1) + dg(g[2], wv[part], 1, 1)
        cb = c[:, part]
        dots = dots + jnp.sum(gn * gain[0:1, part] * cb.astype(F32), axis=1, keepdims=True)
        msg[0:CL, 0:WL] = dg(g[3, 0:CL], wo[part], 1, 1).astype(msg.dtype)
        msg[CL : CL + ROWS, 0:WL] = gn.astype(msg.dtype)
        msg[0:CL, WL : WL + 128] = jnp.zeros((CL, 128), msg.dtype)
        if shift == 0:
            cz[...] = cb
    keep[CL : CL + ROWS, WL : WL + 128] = jnp.broadcast_to(dots, (ROWS, 128))
    hi = dots.astype(BF16)
    lo = (dots - hi.astype(F32)).astype(BF16)
    lo2 = (dots - hi.astype(F32) - lo.astype(F32)).astype(BF16)
    packed = jnp.where(lane == 0, hi.astype(F32), jnp.where(lane == 1, lo.astype(F32), lo2.astype(F32)))
    packed = jnp.where(lane < 3, packed, 0.0).astype(BF16)
    for msg in (msg1, msg2, msg3):
        msg[CL : CL + ROWS, WL : WL + 128] = packed


def after_kernel(
    sc, keep, r1, r2, r3, cz, inv, gain, first, second, up_gain, dw, other,
    update, grad, o0, o1, o2, o3, rows,
):
    ctx, doc_len, z = sc[0], sc[1], sc[2]
    mask = byte_mask(ctx, doc_len)
    body = slice(0, WL)
    out = keep[0:CL, body]
    gn = keep[CL : CL + ROWS, body]
    dots = keep[CL : CL + ROWS, WL : WL + 1]
    for r in (r1, r2, r3):
        out = out + r[0:CL, body].astype(F32)
        gn = gn + r[CL : CL + ROWS, body].astype(F32)
        dots = dots + jnp.sum(r[CL : CL + ROWS, WL : WL + 128].astype(F32), axis=1, keepdims=True)
    update[...] = ((out[:, None, :] * up_gain[...][None]) * mask).reshape(SEG, WL).astype(BF16)
    i = inv[:, 0:1]
    gained = gn * gain[0:1, pl.ds(pl.multiple_of(z * WL, WL), WL)]
    full = i * gained - cz[...].astype(F32) * (i * i * i) * dots * (1.0 / D)
    exists = lax.broadcasted_iota(jnp.int32, (ROWS, WL), 0) + ctx * CL < LC
    rows[...] = jnp.where(exists, full, 0.0)
    taps = tap_weights(first[...], second[...])
    u = lax.broadcasted_iota(jnp.int32, (CL, 16, WL), 1)
    picked = jnp.where(u == 0, rows[0:CL][:, None, :], rows[1 : CL + 1][:, None, :])
    grad[...] = (picked * taps[None] * mask).reshape(SEG, WL).astype(BF16)
    for w, o in enumerate((o0, o1, o2, o3)):
        o[...] = dw[w] + other[w].astype(F32)


def call(kernel, outs, args, scratch=(), smem=(0,), flops=0, size=0, vmem=48 * 2**20, loads=False):
    def spec(i, a):
        if i in smem:
            return pl.BlockSpec(memory_space=SM)
        if loads:
            return pl.BlockSpec(a.shape, lambda i, n=a.ndim: (0,) * n)
        return pl.BlockSpec(memory_space=VM)

    return pl.pallas_call(
        kernel,
        grid=(1,) if loads else (),
        out_shape=[jax.ShapeDtypeStruct(s, d) for s, d in outs],
        in_specs=[spec(i, a) for i, a in enumerate(args)],
        out_specs=[pl.BlockSpec(memory_space=VM)] * len(outs),
        scratch_shapes=[pltpu.VMEM(s, d) for s, d in scratch],
        compiler_params=pltpu.CompilerParams(vmem_limit_bytes=vmem),
        cost_estimate=pl.CostEstimate(flops=flops, bytes_accessed=size, transcendentals=0),
    )(*args)


def shifted(x, axis, steps):
    n = lax.axis_size(axis)
    return lax.ppermute(x, axis, [(i, (i + steps) % n) for i in range(n)])


def local(
    tokens, lengths, conv_first, conv_second, norm_gain, w_query, w_key, w_value, w_out,
    bias_table, buckets, up_gain, grad_out,
):
    x, y, core = lax.axis_index("x"), lax.axis_index("y"), lax.axis_index("core")
    dp, z = lax.axis_index("dp"), lax.axis_index("tensor")
    ctx = (x * 2 + y) * 2 + core
    sc = jnp.stack([ctx, lengths[0], z, core, dp]).astype(jnp.int32)
    gain = norm_gain[None]
    weights = (w_query, w_key, w_value, w_out)
    part, last, gco = call(
        before_kernel,
        [((CL, WL), F32), ((8, WL), F32), ((CL, WL), BF16)],
        (sc, tokens[0], grad_out[0], conv_first, conv_second, up_gain),
        [((CL + 8, WL), F32)],
        loads=True,
    )
    rim = lax.ppermute(last, ("x", "y", "core"), [(i, i + 1) for i in range(15)])
    is_first = (jnp.arange(CL) == 0)[:, None]
    coarse = (part + jnp.where(is_first, rim[0:1], 0.0)).astype(BF16)
    piece = jnp.concatenate([coarse, gco], axis=0)
    n = 640
    near = jnp.concatenate(
        [
            jnp.flip(buckets[:385]),
            jnp.full((n - LC,), bias_table.shape[0], jnp.int32),
            jnp.flip(buckets[385:]),
        ]
    )
    (strip,) = call(
        bias_kernel,
        [((NH, 128, LC), F32)],
        (sc, jnp.broadcast_to(near[None], (8, n)), bias_table),
        smem=(0, 2),
    )
    pieces = [piece] + [shifted(piece, "tensor", s) for s in (1, 2, 3)]
    keep, send, blocks, craw, first = call(
        project_kernel,
        [((CL, 4 * HW), BF16), ((CL, 4 * HW), BF16), ((8, 16, 4 * HW), BF16), ((CL, D), BF16), ((16, D), BF16)],
        (sc, *pieces, gain, *weights),
        [((CL, D), BF16), ((CL, D), BF16), ((2, CL, 4 * HW), BF16)],
    )
    swapped = shifted(send, "core", 1)
    low = core == 0
    pair = jnp.concatenate([jnp.where(low, keep, swapped), jnp.where(low, swapped, keep)], axis=0)
    bundle = jnp.concatenate([jnp.broadcast_to(pair[None], (8,) + pair.shape), blocks], axis=1)
    got = lax.all_to_all(bundle, ("x", "y"), 0, 0, tiled=True)
    nxt = lax.ppermute(first, ("x", "y", "core"), [(i + 1, i) for i in range(15)])
    mine = got[:, 64:80]
    other_rows = shifted(mine, "core", 1)
    res, keep_r, send_r = call(
        attend_kernel,
        [((4, LC + 16, HW), BF16), ((4, ROWS, HW), BF16), ((4, ROWS, HW), BF16)],
        (sc, got, strip),
        [((LC, HW), BF16)] * 4 + [((NH, LC, HD), F32)] * 2,
        flops=6 * 10**9,
    )
    got_r = shifted(send_r, "core", 1)
    dw_keep, dw_send = call(
        weights_kernel,
        [((4, 2, 64, HW), F32), ((4, 2, 64, HW), BF16)],
        (sc, res, mine, other_rows),
        [((LC, 256), BF16), ((LC, 256), BF16), ((256, HW), F32)],
        flops=10**9,
    )
    dw_got = shifted(dw_send, "core", 1)
    dw_own, dw_other = call(
        join_kernel, [((4, 64, WL), F32), ((4, 64, WL), BF16)], (sc, dw_keep, dw_got)
    )
    dw_other = shifted(dw_other, "dp", 1)
    msg = (CL + ROWS, WL + 128)
    m1, m2, m3, own, cz, inv = call(
        partial_kernel,
        [(msg, BF16), (msg, BF16), (msg, BF16), (msg, F32), ((ROWS, WL), BF16), ((ROWS, 128), F32)],
        (sc, keep_r, got_r, craw, nxt, gain, *weights),
        [((4, ROWS, WL), BF16), ((ROWS, D), BF16)],
        flops=10**9,
    )
    r1, r2, r3 = shifted(m1, "tensor", 1), shifted(m2, "tensor", 2), shifted(m3, "tensor", 3)
    update, grad_tokens, *dw = call(
        after_kernel,
        [((SEG, WL), BF16)] * 2 + [((64, WL), F32)] * 4,
        (sc, own, r1, r2, r3, cz, inv, gain, conv_first, conv_second, up_gain, dw_own, dw_other),
        [((ROWS, WL), F32)],
    )
    return (update[None], grad_tokens[None], *dw)


def solution(mesh):
    ctx = ("x", "y", "core")
    fine = Mesh(
        np.asarray(mesh.devices).reshape(2, 4, 2, 2, 4), ("dp", "x", "y", "core", "tensor")
    )
    tok = P("dp", ctx, "tensor")
    col = P(None, "tensor")
    in_specs = (tok, P("dp"), col, col, P(), col, col, col, col, col, P(), col, tok)
    dw = P(("dp",) + ctx, "tensor")
    return jax.shard_map(
        local, mesh=fine, in_specs=in_specs, out_specs=(tok, tok, dw, dw, dw, dw), check_vma=False
    )
```

```python
import math

import jax
import jax.numpy as jnp
import numpy as np
from jax import lax
from jax.experimental import pallas as pl
from jax.experimental.pallas import tpu as pltpu
from jax.sharding import Mesh, PartitionSpec as P

F32 = jnp.float32
BF16 = jnp.bfloat16
NEG = float("-inf")
D = 2048
WL = 512
LC = 512
CL = 32
SEG = 512
HD = 128
NH = 2
HW = NH * HD
SCALE = 1.0 / math.sqrt(HD)
ROWS = CL + 16
VM = pltpu.VMEM
BIG = 63 * 2**20
SM = pltpu.SMEM
PIECE = 4 * CL + 16


def dg(a, b, ca, cb):
    return lax.dot_general(a, b, (((ca,), (cb,)), ((), ())), preferred_element_type=F32)


def tap_weights(first, second):
    taps = jnp.concatenate([second[a : a + 1] * first for a in range(4)], axis=0)
    return jnp.concatenate([taps[15:16], taps[:15]], axis=0)


def byte_mask(ctx, doc_len):
    pos = ctx * SEG + 16 * lax.broadcasted_iota(jnp.int32, (CL, 16, WL), 0)
    pos = pos + lax.broadcasted_iota(jnp.int32, (CL, 16, WL), 1)
    return (pos < doc_len).astype(F32)


def before_kernel(
    sc, tokens_h, grad_h, first_h, second_h, up_h, gain_h, part, last, ahead, gco, gain,
    tokens, grad_out, first, second, up_gain, shift, sems,
):
    pairs = ((tokens_h, tokens), (first_h, first), (second_h, second), (grad_h, grad_out), (up_h, up_gain), (gain_h, gain))
    copies = [pltpu.make_async_copy(a, b, sems.at[i]) for i, (a, b) in enumerate(pairs)]
    for c in copies:
        c.start()
    mask = byte_mask(sc[0], sc[1])
    u = lax.broadcasted_iota(jnp.int32, (CL, 16, WL), 1)
    for c in copies[:3]:
        c.wait()
    taps = tap_weights(first[...], second[...])
    prod = tokens[...].astype(F32).reshape(CL, 16, WL) * mask * taps[None]
    own = jnp.sum(jnp.where(u == 0, prod, 0.0), axis=1)
    onward = jnp.sum(jnp.where(u == 0, 0.0, prod), axis=1)
    shift[0:8] = jnp.zeros((8, WL), F32)
    shift[8 : 8 + CL] = onward
    part[...] = own + shift[7 : 7 + CL]
    last[...] = jnp.broadcast_to(shift[7 + CL : 8 + CL], (8, WL))
    ahead[...] = jnp.broadcast_to(own[0:1], (8, WL))
    for c in copies[3:]:
        c.wait()
    weighted = grad_out[...].astype(F32).reshape(CL, 16, WL) * mask * up_gain[...][None]
    gco[...] = jnp.sum(weighted, axis=1).astype(BF16)


def bias_kernel(sc, near, table, strip):
    n = near.shape[1]
    which = near[0:1]
    for h in range(NH):
        row = jnp.full((1, n), NEG, F32)
        for b in range(table.shape[0]):
            row = jnp.where(which == b, table[b, sc[3] * NH + h], row)
        rolled = pltpu.roll(jnp.broadcast_to(row, (128, n)), 0, 1, stride=1, stride_axis=0)
        strip[h] = rolled[:, :LC]


def project_kernel(
    sc, p0, r1, r2, r3, gain, wq, wk, wv, wo, keep, send, blocks, c48, craw, nrm, gco, both, ws, sems
):
    copies = [pltpu.make_async_copy(w, ws.at[i], sems.at[i]) for i, w in enumerate((wo, wq, wk, wv))]
    for cp in copies:
        cp.start()
    z, core, x, y = sc[2], sc[3], sc[5], sc[6]
    for s, src in enumerate((p0, r1, r2, r3)):
        cols = pl.ds(pl.multiple_of(lax.rem(z + 4 - s, 4) * WL, WL), WL)
        for i in range(2):
            rows = slice(i * CL, i * CL + CL)
            craw[rows, cols] = src[2 * i * CL : 2 * i * CL + CL]
            gco[rows, cols] = src[2 * i * CL + CL : 2 * i * CL + 2 * CL]
        c48[CL:ROWS, cols] = src[4 * CL : PIECE]
    c48[0:CL] = craw[pl.ds(pl.multiple_of(y * CL, CL), CL)]
    c = craw[...].astype(F32)
    r = lax.rsqrt(jnp.sum(c * c, axis=1, keepdims=True) * (1.0 / D) + 1e-6)
    nrm[...] = (c * r * gain[...]).astype(BF16)
    for i, (src, slot) in enumerate(((gco, 3), (nrm, 0), (nrm, 1), (nrm, 2))):
        copies[i].wait()
        v = jnp.dot(src[...], ws[i], preferred_element_type=F32).astype(BF16)
        for half in range(2):
            both[half, :, slot * HW : slot * HW + HW] = v[:, half * HW : half * HW + HW]
    keep[...] = both[core]
    send[...] = both[1 - core]
    for s in range(4):
        for d in range(2):
            chip = lax.rem(x + s, 4) * 2 + y
            cols = pl.ds(pl.multiple_of((d * 8 + chip) * 128, 128), 128)
            for i in range(2):
                rows = slice(i * CL, i * CL + CL)
                at = i * 512 + d * 128
                blocks[s, :, at : at + 128] = nrm[rows, cols]
                blocks[s, :, at + 256 : at + 384] = gco[rows, cols]


def pack_kernel(sc, keep, swapped, blocks, b0, b1, b2, b3):
    core = sc[3]
    for s, b in enumerate((b0, b1, b2, b3)):
        for i in range(2):
            for src, c in ((keep, core), (swapped, 1 - core)):
                rows = pl.ds(pl.multiple_of(i * 64 + c * CL, CL), CL)
                b[rows] = src[i * CL : i * CL + CL]
        b[128:160] = blocks[s]


def attend_kernel(sc, b0, r1, r2, r3, strip, res, keep, send, q, k, v, ga, acck, accv):
    ctx, doc_len, core, x = sc[0], sc[1], sc[3], sc[5]
    for s, src in enumerate((b0, r1, r2, r3)):
        rows = pl.ds(pl.multiple_of(lax.rem(x + 4 - s, 4) * 128, 128), 128)
        for i, dst in enumerate((q, k, v, ga)):
            dst[rows] = src[0:128, i * HW : i * HW + HW]
    key_pos = lax.broadcasted_iota(jnp.int32, (1, LC), 1)
    key_mask = jnp.where(16 * key_pos < doc_len, 0.0, NEG)
    for h in range(NH):
        cols = slice(h * HD, h * HD + HD)
        for b in (3, 2, 1, 0):
            rows = slice(b * 128, b * 128 + 128)
            n = b * 128 + 128
            qb, gb, kb, vb = q[rows, cols], ga[rows, cols], k[0:n, cols], v[0:n, cols]
            s = dg(qb, kb, 1, 1) * SCALE + strip[h, :, LC - n :] + key_mask[:, :n]
            e = jnp.exp(s - jnp.max(s, axis=1, keepdims=True))
            p = e * (1.0 / jnp.sum(e, axis=1, keepdims=True))
            pb = p.astype(BF16)
            ab = jnp.dot(pb, vb, preferred_element_type=F32).astype(BF16)
            res[3, rows, cols] = ab
            dot = jnp.sum(gb.astype(F32) * ab.astype(F32), axis=1, keepdims=True)
            sg = (p * (dg(gb, vb, 1, 1) - dot)).astype(BF16)
            res[0, rows, cols] = (jnp.dot(sg, kb, preferred_element_type=F32) * SCALE).astype(BF16)
            tk = dg(sg, qb, 0, 0)
            tv = dg(pb, gb, 0, 0)
            if b == 3:
                acck[h] = tk
                accv[h] = tv
            else:
                acck[h, 0:n] += tk
                accv[h, 0:n] += tv
        res[1, 0:LC, cols] = (acck[h] * SCALE).astype(BF16)
        res[2, 0:LC, cols] = accv[h].astype(BF16)
    res[:, LC : LC + 16] = jnp.zeros((4, 16, HW), BF16)
    peer = ctx + 1 - 2 * core
    keep[...] = res[:, pl.ds(pl.multiple_of(ctx * CL, CL), ROWS)]
    send[...] = res[:, pl.ds(pl.multiple_of(peer * CL, CL), ROWS)]


def weights_kernel(sc, res, mine, other, keep, send, nb, gb, tile):
    core, x = sc[3], sc[5]
    for s in range(4):
        for src, c in ((mine, core), (other, 1 - core)):
            for i in range(2):
                at = (lax.rem(x + 4 - s, 4) * 4 + i * 2 + c) * CL
                rows = pl.ds(pl.multiple_of(at, CL), CL)
                nb[rows] = src[s, :, i * 512 : i * 512 + 256]
                gb[rows] = src[s, :, i * 512 + 256 : i * 512 + 512]
    for w in range(4):
        tile[...] = dg((gb if w == 3 else nb)[...], res[w, 0:LC], 0, 0)
        for d in range(2):
            keep[w, d] = tile[pl.ds(pl.multiple_of(d * 128 + core * 64, 64), 64)]
            send[w, d] = tile[pl.ds(pl.multiple_of(d * 128 + 64 - core * 64, 64), 64)].astype(BF16)


def join_kernel(sc, keep, got, after, own, send):
    core, dp = sc[3], sc[4]
    a = pl.ds(pl.multiple_of(core * HW, HW), HW)
    b = pl.ds(pl.multiple_of((1 - core) * HW, HW), HW)
    own[:, :, a] = keep[:, dp]
    own[:, :, b] = got[:, dp].astype(F32)
    send[:, :, a] = keep[:, 1 - dp].astype(BF16)
    send[:, :, b] = got[:, 1 - dp]


def partial_kernel(
    sc, keep_r, got_r, c, gain, wq, wk, wv, wo, msg1, msg2, msg3, keep, cz, inv_out, g
):
    z, core = sc[2], sc[3]
    g[:, :, pl.ds(pl.multiple_of(core * HW, HW), HW)] = keep_r[...]
    g[:, :, pl.ds(pl.multiple_of((1 - core) * HW, HW), HW)] = got_r[...]
    cf = c[...].astype(F32)
    r = lax.rsqrt(jnp.sum(cf * cf, axis=1, keepdims=True) * (1.0 / D) + 1e-6)
    inv_out[...] = jnp.broadcast_to(r, (ROWS, 128))
    lane = lax.broadcasted_iota(jnp.int32, (ROWS, 128), 1)
    dots = jnp.zeros((ROWS, 1), F32)
    for shift, msg in ((1, msg1), (2, msg2), (3, msg3), (0, keep)):
        t = lax.rem(z + shift, 4)
        part = pl.ds(pl.multiple_of(t * WL, WL), WL)
        gn = dg(g[0], wq[part], 1, 1) + dg(g[1], wk[part], 1, 1) + dg(g[2], wv[part], 1, 1)
        cb = c[:, part]
        dots = dots + jnp.sum(gn * gain[0:1, part] * cb.astype(F32), axis=1, keepdims=True)
        msg[0:CL, 0:WL] = dg(g[3, 0:CL], wo[part], 1, 1).astype(msg.dtype)
        msg[CL : CL + ROWS, 0:WL] = gn.astype(msg.dtype)
        msg[0:CL, WL : WL + 128] = jnp.zeros((CL, 128), msg.dtype)
        if shift == 0:
            cz[...] = cb
    keep[CL : CL + ROWS, WL : WL + 128] = jnp.broadcast_to(dots, (ROWS, 128))
    hi = dots.astype(BF16)
    lo = (dots - hi.astype(F32)).astype(BF16)
    lo2 = (dots - hi.astype(F32) - lo.astype(F32)).astype(BF16)
    packed = jnp.where(lane == 0, hi.astype(F32), jnp.where(lane == 1, lo.astype(F32), lo2.astype(F32)))
    packed = jnp.where(lane < 3, packed, 0.0).astype(BF16)
    for msg in (msg1, msg2, msg3):
        msg[CL : CL + ROWS, WL : WL + 128] = packed


def after_kernel(
    sc, keep, r1, r2, r3, cz, inv, gain, first, second, up_gain, dw, other,
    update, grad, o0, o1, o2, o3, rows,
):
    ctx, doc_len, z = sc[0], sc[1], sc[2]
    mask = byte_mask(ctx, doc_len)
    body = slice(0, WL)
    out = keep[0:CL, body]
    gn = keep[CL : CL + ROWS, body]
    dots = keep[CL : CL + ROWS, WL : WL + 1]
    for r in (r1, r2, r3):
        out = out + r[0:CL, body].astype(F32)
        gn = gn + r[CL : CL + ROWS, body].astype(F32)
        dots = dots + jnp.sum(r[CL : CL + ROWS, WL : WL + 128].astype(F32), axis=1, keepdims=True)
    update[...] = ((out[:, None, :] * up_gain[...][None]) * mask).reshape(SEG, WL).astype(BF16)
    i = inv[:, 0:1]
    gained = gn * gain[0:1, pl.ds(pl.multiple_of(z * WL, WL), WL)]
    full = i * gained - cz[...].astype(F32) * (i * i * i) * dots * (1.0 / D)
    exists = lax.broadcasted_iota(jnp.int32, (ROWS, WL), 0) + ctx * CL < LC
    rows[...] = jnp.where(exists, full, 0.0)
    taps = tap_weights(first[...], second[...])
    u = lax.broadcasted_iota(jnp.int32, (CL, 16, WL), 1)
    picked = jnp.where(u == 0, rows[0:CL][:, None, :], rows[1 : CL + 1][:, None, :])
    grad[...] = (picked * taps[None] * mask).reshape(SEG, WL).astype(BF16)
    for w, o in enumerate((o0, o1, o2, o3)):
        o[...] = dw[w] + other[w].astype(F32)


def call(kernel, outs, args, scratch=(), smem=(0,), flops=0, size=0, vmem=8 * 2**20, hbm=()):
    def spec(i):
        return pl.BlockSpec(memory_space=SM if i in smem else pltpu.HBM if i in hbm else VM)

    return pl.pallas_call(
        kernel,
        out_shape=[jax.ShapeDtypeStruct(s, d) for s, d in outs],
        in_specs=[spec(i) for i in range(len(args))],
        out_specs=[pl.BlockSpec(memory_space=VM)] * len(outs),
        scratch_shapes=[pltpu.VMEM(*s) if isinstance(s, tuple) else s for s in scratch],
        compiler_params=pltpu.CompilerParams(vmem_limit_bytes=vmem),
        cost_estimate=pl.CostEstimate(flops=flops, bytes_accessed=size, transcendentals=0),
    )(*args)


def shifted(x, axis, steps):
    n = lax.axis_size(axis)
    return lax.ppermute(x, axis, [(i, (i + steps) % n) for i in range(n)])


def local(
    tokens, lengths, conv_first, conv_second, norm_gain, w_query, w_key, w_value, w_out,
    bias_table, buckets, up_gain, grad_out,
):
    x, y, core = lax.axis_index("x"), lax.axis_index("y"), lax.axis_index("core")
    dp, z = lax.axis_index("dp"), lax.axis_index("tensor")
    ctx = (x * 2 + y) * 2 + core
    sc = jnp.stack([ctx, lengths[0], z, core, dp, x, y]).astype(jnp.int32)
    weights = (w_query, w_key, w_value, w_out)
    part, last, ahead, gco, gain = call(
        before_kernel,
        [((CL, WL), F32), ((8, WL), F32), ((8, WL), F32), ((CL, WL), BF16), ((1, D), F32)],
        (sc, tokens[0], grad_out[0], conv_first, conv_second, up_gain, norm_gain[None]),
        [
            ((SEG, WL), BF16), ((SEG, WL), BF16), ((4, WL), F32), ((4, WL), F32), ((16, WL), F32),
            ((CL + 8, WL), F32), pltpu.SemaphoreType.DMA((6,)),
        ],
        hbm=(1, 2, 3, 4, 5, 6),
        vmem=BIG,
    )
    line = ("x", "y", "core")
    rim = lax.ppermute(last, line, [(i, i + 1) for i in range(15)])
    lead = lax.ppermute(ahead, line, [(i + 1, i) for i in range(15)])
    is_first = (jnp.arange(CL) == 0)[:, None]
    coarse = (part + jnp.where(is_first, rim[0:1], 0.0)).astype(BF16)
    piece = jnp.concatenate([coarse, gco], axis=0)
    across = shifted(piece, "y", 1)
    nxt = jnp.where(is_first[:16], lead[0:1] + last[0:1], 0.0).astype(BF16)
    low_y = y == 0
    piece = jnp.concatenate(
        [jnp.where(low_y, piece, across), jnp.where(low_y, across, piece), nxt], axis=0
    )
    n = 640
    near = jnp.concatenate(
        [
            jnp.flip(buckets[:385]),
            jnp.full((n - LC,), bias_table.shape[0], jnp.int32),
            jnp.flip(buckets[385:]),
        ]
    )
    (strip,) = call(
        bias_kernel,
        [((NH, 128, LC), F32)],
        (sc, jnp.broadcast_to(near[None], (8, n)), bias_table),
        smem=(0, 2),
    )
    pieces = [piece] + [shifted(piece, "tensor", s) for s in (1, 2, 3)]
    keep, send, blocks, c48 = call(
        project_kernel,
        [((2 * CL, 4 * HW), BF16), ((2 * CL, 4 * HW), BF16), ((4, CL, 4 * HW), BF16), ((ROWS, D), BF16)],
        (sc, *pieces, gain, *weights),
        [
            ((2 * CL, D), BF16), ((2 * CL, D), BF16), ((2 * CL, D), BF16), ((2, 2 * CL, 4 * HW), BF16),
            ((4, D, WL), BF16), pltpu.SemaphoreType.DMA((4,)),
        ],
        flops=10**9,
        hbm=(6, 7, 8, 9),
        vmem=BIG - 10 * 2**20,
    )
    swapped = shifted(send, "core", 1)
    b0, b1, b2, b3 = call(
        pack_kernel, [((5 * CL, 4 * HW), BF16)] * 4, (sc, keep, swapped, blocks)
    )
    bundles = [b0, shifted(b1, "x", 1), shifted(b2, "x", 2), shifted(b3, "x", 3)]
    mine = jnp.stack([b[4 * CL :] for b in bundles])
    other_rows = shifted(mine, "core", 1)
    res, keep_r, send_r = call(
        attend_kernel,
        [((4, LC + 16, HW), BF16), ((4, ROWS, HW), BF16), ((4, ROWS, HW), BF16)],
        (sc, *bundles, strip),
        [((LC, HW), BF16)] * 4 + [((NH, LC, HD), F32)] * 2,
        flops=6 * 10**9,
    )
    got_r = shifted(send_r, "core", 1)
    dw_keep, dw_send = call(
        weights_kernel,
        [((4, 2, 64, HW), F32), ((4, 2, 64, HW), BF16)],
        (sc, res, mine, other_rows),
        [((LC, 256), BF16), ((LC, 256), BF16), ((256, HW), F32)],
        flops=10**9,
    )
    dw_got = shifted(dw_send, "core", 1)
    msg = (CL + ROWS, WL + 128)
    m1, m2, m3, own, cz, inv = call(
        partial_kernel,
        [(msg, BF16), (msg, BF16), (msg, BF16), (msg, F32), ((ROWS, WL), BF16), ((ROWS, 128), F32)],
        (sc, keep_r, got_r, c48, gain, *weights),
        [((4, ROWS, WL), BF16)],
        flops=10**9,
    )
    r1, r2, r3 = shifted(m1, "tensor", 1), shifted(m2, "tensor", 2), shifted(m3, "tensor", 3)
    dw_own, dw_other = call(
        join_kernel, [((4, 64, WL), F32), ((4, 64, WL), BF16)], (sc, dw_keep, dw_got, inv)
    )
    dw_other = shifted(dw_other, "dp", 1)
    update, grad_tokens, *dw = call(
        after_kernel,
        [((SEG, WL), BF16)] * 2 + [((64, WL), F32)] * 4,
        (sc, own, r1, r2, r3, cz, inv, gain, conv_first, conv_second, up_gain, dw_own, dw_other),
        [((ROWS, WL), F32)],
    )
    return (update[None], grad_tokens[None], *dw)


def solution(mesh):
    ctx = ("x", "y", "core")
    fine = Mesh(
        np.asarray(mesh.devices).reshape(2, 4, 2, 2, 4), ("dp", "x", "y", "core", "tensor")
    )
    tok = P("dp", ctx, "tensor")
    col = P(None, "tensor")
    in_specs = (tok, P("dp"), col, col, P(), col, col, col, col, col, P(), col, tok)
    dw = P(("dp",) + ctx, "tensor")
    return jax.shard_map(
        local, mesh=fine, in_specs=in_specs, out_specs=(tok, tok, dw, dw, dw, dw), check_vma=False
    )
```

```python
import math

import jax
import jax.numpy as jnp
import numpy as np
from jax import lax
from jax.experimental import pallas as pl
from jax.experimental.pallas import tpu as pltpu
from jax.sharding import Mesh, PartitionSpec as P

F32 = jnp.float32
BF16 = jnp.bfloat16
NEG = float("-inf")
D = 2048
WL = 512
LC = 512
CL = 32
SEG = 512
HD = 128
NH = 2
HW = NH * HD
SCALE = 1.0 / math.sqrt(HD)
ROWS = CL + 16
VM = pltpu.VMEM
BIG = 63 * 2**20
SM = pltpu.SMEM
PIECE = 4 * CL + 16


def dg(a, b, ca, cb):
    return lax.dot_general(a, b, (((ca,), (cb,)), ((), ())), preferred_element_type=F32)


class Place:
    def __init__(self):
        self.x, self.y, self.core = (lax.axis_index(a) for a in ("x", "y", "core"))
        self.dp, self.z = lax.axis_index("dp"), lax.axis_index("tensor")
        self.ctx = (self.x * 2 + self.y) * 2 + self.core


def tap_weights(first, second):
    taps = jnp.concatenate([second[a : a + 1] * first for a in range(4)], axis=0)
    return jnp.concatenate([taps[15:16], taps[:15]], axis=0)


def byte_mask(ctx, doc_len):
    pos = ctx * SEG + 16 * lax.broadcasted_iota(jnp.int32, (CL, 16, WL), 0)
    pos = pos + lax.broadcasted_iota(jnp.int32, (CL, 16, WL), 1)
    return (pos < doc_len).astype(F32)


def before_kernel(
    lens, tokens_h, grad_h, first_h, second_h, up_h, gain_h, part, last, ahead, gco, gain,
    tokens, grad_out, first, second, up_gain, shift, sems,
):
    pairs = ((tokens_h, tokens), (first_h, first), (second_h, second), (grad_h, grad_out), (up_h, up_gain), (gain_h, gain))
    copies = [pltpu.make_async_copy(a, b, sems.at[i]) for i, (a, b) in enumerate(pairs)]
    for c in copies:
        c.start()
    mask = byte_mask(Place().ctx, lens[0])
    u = lax.broadcasted_iota(jnp.int32, (CL, 16, WL), 1)
    for c in copies[:3]:
        c.wait()
    taps = tap_weights(first[...], second[...])
    prod = tokens[...].astype(F32).reshape(CL, 16, WL) * mask * taps[None]
    own = jnp.sum(jnp.where(u == 0, prod, 0.0), axis=1)
    onward = jnp.sum(jnp.where(u == 0, 0.0, prod), axis=1)
    shift[0:8] = jnp.zeros((8, WL), F32)
    shift[8 : 8 + CL] = onward
    part[...] = own + shift[7 : 7 + CL]
    last[...] = jnp.broadcast_to(shift[7 + CL : 8 + CL], (8, WL))
    ahead[...] = jnp.broadcast_to(own[0:1], (8, WL))
    for c in copies[3:]:
        c.wait()
    weighted = grad_out[...].astype(F32).reshape(CL, 16, WL) * mask * up_gain[...][None]
    gco[...] = jnp.sum(weighted, axis=1).astype(BF16)


def piece_kernel(part, gco, rim, piece):
    first = lax.broadcasted_iota(jnp.int32, (CL, WL), 0) == 0
    piece[0:CL] = (part[...] + jnp.where(first, rim[0:1], 0.0)).astype(BF16)
    piece[CL : 2 * CL] = gco[...]


def pile_kernel(piece, across, lead, last, out):
    y = Place().y
    out[pl.ds(pl.multiple_of(y * 64, 64), 64)] = piece[...]
    out[pl.ds(pl.multiple_of(64 - y * 64, 64), 64)] = across[...]
    first = lax.broadcasted_iota(jnp.int32, (16, WL), 0) == 0
    out[128:144] = jnp.where(first, lead[0:1] + last[0:1], 0.0).astype(BF16)


def bias_kernel(near, table, strip):
    core = Place().core
    n = near.shape[1]
    which = near[0:1]
    for h in range(NH):
        row = jnp.full((1, n), NEG, F32)
        for b in range(table.shape[0]):
            row = jnp.where(which == b, table[b, core * NH + h], row)
        rolled = pltpu.roll(jnp.broadcast_to(row, (128, n)), 0, 1, stride=1, stride_axis=0)
        strip[h] = rolled[:, :LC]


def project_kernel(
    p0, r1, r2, r3, gain, wq, wk, wv, wo, keep, send, blocks, c48, craw, nrm, gco, both
):
    at = Place()
    z, core, x, y = at.z, at.core, at.x, at.y
    for s, src in enumerate((p0, r1, r2, r3)):
        cols = pl.ds(pl.multiple_of(lax.rem(z + 4 - s, 4) * WL, WL), WL)
        for i in range(2):
            rows = slice(i * CL, i * CL + CL)
            craw[rows, cols] = src[2 * i * CL : 2 * i * CL + CL]
            gco[rows, cols] = src[2 * i * CL + CL : 2 * i * CL + 2 * CL]
        c48[CL:ROWS, cols] = src[4 * CL : PIECE]
    c48[0:CL] = craw[pl.ds(pl.multiple_of(y * CL, CL), CL)]
    c = craw[...].astype(F32)
    r = lax.rsqrt(jnp.sum(c * c, axis=1, keepdims=True) * (1.0 / D) + 1e-6)
    nrm[...] = (c * r * gain[...]).astype(BF16)
    for src, w, slot in ((gco, wo, 3), (nrm, wq, 0), (nrm, wk, 1), (nrm, wv, 2)):
        v = jnp.dot(src[...], w[...], preferred_element_type=F32).astype(BF16)
        for half in range(2):
            both[half, :, slot * HW : slot * HW + HW] = v[:, half * HW : half * HW + HW]
    keep[...] = both[core]
    send[...] = both[1 - core]
    for s in range(4):
        for d in range(2):
            chip = lax.rem(x + s, 4) * 2 + y
            cols = pl.ds(pl.multiple_of((d * 8 + chip) * 128, 128), 128)
            for i in range(2):
                rows = slice(i * CL, i * CL + CL)
                at = i * 512 + d * 128
                blocks[s, :, at : at + 128] = nrm[rows, cols]
                blocks[s, :, at + 256 : at + 384] = gco[rows, cols]


def pack_kernel(keep, swapped, blocks, b0, up, down):
    core = Place().core
    for i in range(2):
        for src, c in ((keep, core), (swapped, 1 - core)):
            row = i * 64 + c * CL
            new = src[i * CL : i * CL + CL]
            b0[pl.ds(pl.multiple_of(row, CL), CL)] = new
            up[pl.ds(pl.multiple_of((96 if i == 0 else -32) + row, CL), CL)] = new
            down[pl.ds(pl.multiple_of(32 + row, CL), CL)] = new
    b0[128:160] = blocks[0]
    up[0:32] = blocks[1]
    down[0:32] = blocks[3]
    up[160:176] = blocks[2, 0:16]
    down[160:176] = blocks[2, 16:32]


def attend_kernel(
    lens, b0, low, high, far_low, far_high, strip, res, keep, send, mine, q, k, v, ga, acck, accv
):
    at = Place()
    ctx, core, x, doc_len = at.ctx, at.core, at.x, lens[0]
    for src, first, n, s, row in (
        (b0, 0, 128, 0, 0),
        (low, 96, 64, 1, 0),
        (low, 32, 64, 1, 64),
        (far_low, 0, 64, 2, 0),
        (far_high, 0, 64, 2, 64),
        (high, 32, 128, 3, 0),
    ):
        rows = pl.ds(pl.multiple_of(lax.rem(x + 4 - s, 4) * 128 + row, 64), n)
        for i, dst in enumerate((q, k, v, ga)):
            dst[rows] = src[first : first + n, i * HW : i * HW + HW]
    mine[0] = b0[128:160]
    mine[1] = low[0:32]
    mine[2, 0:16] = far_low[64:80]
    mine[2, 16:32] = far_high[64:80]
    mine[3] = high[0:32]
    key_pos = lax.broadcasted_iota(jnp.int32, (1, LC), 1)
    key_mask = jnp.where(16 * key_pos < doc_len, 0.0, NEG)
    for h in range(NH):
        cols = slice(h * HD, h * HD + HD)
        for b in (3, 2, 1, 0):
            rows = slice(b * 128, b * 128 + 128)
            n = b * 128 + 128
            qb, gb, kb, vb = q[rows, cols], ga[rows, cols], k[0:n, cols], v[0:n, cols]
            s = dg(qb, kb, 1, 1) * SCALE + strip[h, :, LC - n :] + key_mask[:, :n]
            e = jnp.exp(s - jnp.max(s, axis=1, keepdims=True))
            p = e * (1.0 / jnp.sum(e, axis=1, keepdims=True))
            pb = p.astype(BF16)
            ab = jnp.dot(pb, vb, preferred_element_type=F32).astype(BF16)
            res[3, rows, cols] = ab
            dot = jnp.sum(gb.astype(F32) * ab.astype(F32), axis=1, keepdims=True)
            sg = (p * (dg(gb, vb, 1, 1) - dot)).astype(BF16)
            res[0, rows, cols] = (jnp.dot(sg, kb, preferred_element_type=F32) * SCALE).astype(BF16)
            tk = dg(sg, qb, 0, 0)
            tv = dg(pb, gb, 0, 0)
            if b == 3:
                acck[h] = tk
                accv[h] = tv
            else:
                acck[h, 0:n] += tk
                accv[h, 0:n] += tv
        res[1, 0:LC, cols] = (acck[h] * SCALE).astype(BF16)
        res[2, 0:LC, cols] = accv[h].astype(BF16)
    res[:, LC : LC + 16] = jnp.zeros((4, 16, HW), BF16)
    peer = ctx + 1 - 2 * core
    keep[...] = res[:, pl.ds(pl.multiple_of(ctx * CL, CL), ROWS)]
    send[...] = res[:, pl.ds(pl.multiple_of(peer * CL, CL), ROWS)]


def weights_kernel(res, mine, other, keep, send, nb, gb):
    at = Place()
    core, x, dp = at.core, at.x, at.dp
    for s in range(4):
        for src, c in ((mine, core), (other, 1 - core)):
            for i in range(2):
                row = (lax.rem(x + 4 - s, 4) * 4 + i * 2 + c) * CL
                rows = pl.ds(pl.multiple_of(row, CL), CL)
                nb[rows] = src[s, :, i * 512 : i * 512 + 256]
                gb[rows] = src[s, :, i * 512 + 256 : i * 512 + 512]
    for w in range(4):
        src = gb if w == 3 else nb
        for d, out in ((dp, keep), (1 - dp, send)):
            cols = pl.ds(pl.multiple_of(d * 128, 128), 128)
            out[w] = dg(src[:, cols], res[w, 0:LC], 0, 0).astype(out.dtype)


def total_kernel(keep, got, after, own, send):
    core = Place().core
    for w in range(4):
        for c, out in ((core, own), (1 - core, send)):
            rows = pl.ds(pl.multiple_of(c * 64, 64), 64)
            out[w] = (keep[w, rows] + got[w, rows].astype(F32)).astype(out.dtype)


def partial_kernel(
    keep_r, got_r, c, gain, wq, wk, wv, wo, msg1, msg2, msg3, keep, cz, inv_out, g
):
    at = Place()
    z, core = at.z, at.core
    g[:, :, pl.ds(pl.multiple_of(core * HW, HW), HW)] = keep_r[...]
    g[:, :, pl.ds(pl.multiple_of((1 - core) * HW, HW), HW)] = got_r[...]
    cf = c[...].astype(F32)
    r = lax.rsqrt(jnp.sum(cf * cf, axis=1, keepdims=True) * (1.0 / D) + 1e-6)
    inv_out[...] = jnp.broadcast_to(r, (ROWS, 128))
    lane = lax.broadcasted_iota(jnp.int32, (ROWS, 128), 1)
    dots = jnp.zeros((ROWS, 1), F32)
    for shift, msg in ((1, msg1), (2, msg2), (3, msg3), (0, keep)):
        t = lax.rem(z + shift, 4)
        part = pl.ds(pl.multiple_of(t * WL, WL), WL)
        gn = dg(g[0], wq[part], 1, 1) + dg(g[1], wk[part], 1, 1) + dg(g[2], wv[part], 1, 1)
        cb = c[:, part]
        dots = dots + jnp.sum(gn * gain[0:1, part] * cb.astype(F32), axis=1, keepdims=True)
        msg[0:CL, 0:WL] = dg(g[3, 0:CL], wo[part], 1, 1).astype(msg.dtype)
        msg[CL : CL + ROWS, 0:WL] = gn.astype(msg.dtype)
        msg[0:CL, WL : WL + 128] = jnp.zeros((CL, 128), msg.dtype)
        if shift == 0:
            cz[...] = cb
    keep[CL : CL + ROWS, WL : WL + 128] = jnp.broadcast_to(dots, (ROWS, 128))
    hi = dots.astype(BF16)
    lo = (dots - hi.astype(F32)).astype(BF16)
    lo2 = (dots - hi.astype(F32) - lo.astype(F32)).astype(BF16)
    packed = jnp.where(lane == 0, hi.astype(F32), jnp.where(lane == 1, lo.astype(F32), lo2.astype(F32)))
    packed = jnp.where(lane < 3, packed, 0.0).astype(BF16)
    for msg in (msg1, msg2, msg3):
        msg[CL : CL + ROWS, WL : WL + 128] = packed


def after_kernel(
    lens, keep, r1, r2, r3, cz, inv, gain, first, second, up_gain, dw, other,
    update, grad, o0, o1, o2, o3, rows,
):
    at = Place()
    ctx, doc_len, z, core = at.ctx, lens[0], at.z, at.core
    mask = byte_mask(ctx, doc_len)
    body = slice(0, WL)
    out = keep[0:CL, body]
    gn = keep[CL : CL + ROWS, body]
    dots = keep[CL : CL + ROWS, WL : WL + 1]
    for r in (r1, r2, r3):
        out = out + r[0:CL, body].astype(F32)
        gn = gn + r[CL : CL + ROWS, body].astype(F32)
        dots = dots + jnp.sum(r[CL : CL + ROWS, WL : WL + 128].astype(F32), axis=1, keepdims=True)
    update[...] = ((out[:, None, :] * up_gain[...][None]) * mask).reshape(SEG, WL).astype(BF16)
    i = inv[:, 0:1]
    gained = gn * gain[0:1, pl.ds(pl.multiple_of(z * WL, WL), WL)]
    full = i * gained - cz[...].astype(F32) * (i * i * i) * dots * (1.0 / D)
    exists = lax.broadcasted_iota(jnp.int32, (ROWS, WL), 0) + ctx * CL < LC
    rows[...] = jnp.where(exists, full, 0.0)
    taps = tap_weights(first[...], second[...])
    u = lax.broadcasted_iota(jnp.int32, (CL, 16, WL), 1)
    picked = jnp.where(u == 0, rows[0:CL][:, None, :], rows[1 : CL + 1][:, None, :])
    grad[...] = (picked * taps[None] * mask).reshape(SEG, WL).astype(BF16)
    for w, o in enumerate((o0, o1, o2, o3)):
        o[:, pl.ds(pl.multiple_of(core * HW, HW), HW)] = dw[w]
        o[:, pl.ds(pl.multiple_of((1 - core) * HW, HW), HW)] = other[w].astype(F32)


def call(kernel, outs, args, scratch=(), smem=(0,), flops=0, size=0, vmem=8 * 2**20, hbm=()):
    def spec(i):
        return pl.BlockSpec(memory_space=SM if i in smem else pltpu.HBM if i in hbm else VM)

    return pl.pallas_call(
        kernel,
        out_shape=[jax.ShapeDtypeStruct(s, d) for s, d in outs],
        in_specs=[spec(i) for i in range(len(args))],
        out_specs=[pl.BlockSpec(memory_space=VM)] * len(outs),
        scratch_shapes=[pltpu.VMEM(*s) if isinstance(s, tuple) else s for s in scratch],
        compiler_params=pltpu.CompilerParams(vmem_limit_bytes=vmem),
        cost_estimate=pl.CostEstimate(flops=flops, bytes_accessed=size, transcendentals=0),
    )(*args)


def shifted(x, axis, steps):
    n = lax.axis_size(axis)
    return lax.ppermute(x, axis, [(i, (i + steps) % n) for i in range(n)])


def local(
    tokens, lengths, conv_first, conv_second, norm_gain, w_query, w_key, w_value, w_out,
    bias_table, buckets, up_gain, grad_out,
):
    weights = (w_query, w_key, w_value, w_out)
    part, last, ahead, gco, gain = call(
        before_kernel,
        [((CL, WL), F32), ((8, WL), F32), ((8, WL), F32), ((CL, WL), BF16), ((1, D), F32)],
        (lengths, tokens[0], grad_out[0], conv_first, conv_second, up_gain, norm_gain[None]),
        [
            ((SEG, WL), BF16), ((SEG, WL), BF16), ((4, WL), F32), ((4, WL), F32), ((16, WL), F32),
            ((CL + 8, WL), F32), pltpu.SemaphoreType.DMA((6,)),
        ],
        hbm=(1, 2, 3, 4, 5, 6),
        vmem=BIG,
    )
    line = ("x", "y", "core")
    rim = lax.ppermute(last, line, [(i, i + 1) for i in range(15)])
    (piece,) = call(piece_kernel, [((2 * CL, WL), BF16)], (part, gco, rim), smem=())
    ahead, piece = lax.optimization_barrier((ahead, piece))
    lead = lax.ppermute(ahead, line, [(i + 1, i) for i in range(15)])
    across = shifted(piece, "y", 1)
    (piece,) = call(
        pile_kernel,
        [((PIECE, WL), BF16)],
        (piece, across, lead, last),
        smem=(),
        flops=6 * 10**9,
    )
    n = 640
    near = jnp.concatenate(
        [
            jnp.flip(buckets[:385]),
            jnp.full((n - LC,), bias_table.shape[0], jnp.int32),
            jnp.flip(buckets[385:]),
        ]
    )
    (strip,) = call(
        bias_kernel,
        [((NH, 128, LC), F32)],
        (jnp.broadcast_to(near[None], (8, n)), bias_table),
        smem=(1,),
    )
    pieces = [piece] + [shifted(piece, "tensor", s) for s in (1, 2, 3)]
    keep, send, blocks, c48 = call(
        project_kernel,
        [((2 * CL, 4 * HW), BF16), ((2 * CL, 4 * HW), BF16), ((4, CL, 4 * HW), BF16), ((ROWS, D), BF16)],
        (*pieces, gain, *weights),
        [((2 * CL, D), BF16), ((2 * CL, D), BF16), ((2 * CL, D), BF16), ((2, 2 * CL, 4 * HW), BF16)],
        smem=(),
        flops=10**9,
    )
    swapped = shifted(send, "core", 1)
    b0, up, down = call(
        pack_kernel,
        [((5 * CL, 4 * HW), BF16), ((176, 4 * HW), BF16), ((176, 4 * HW), BF16)],
        (keep, swapped, blocks),
        smem=(),
    )
    low, high = shifted(up, "x", 1), shifted(down, "x", -1)
    far_low, far_high = shifted(low[96:], "x", 1), shifted(high[96:], "x", -1)
    res, keep_r, send_r, mine = call(
        attend_kernel,
        [
            ((4, LC + 16, HW), BF16), ((4, ROWS, HW), BF16), ((4, ROWS, HW), BF16),
            ((4, CL, 4 * HW), BF16),
        ],
        (lengths, b0, low, high, far_low, far_high, strip),
        [((LC, HW), BF16)] * 4 + [((NH, LC, HD), F32)] * 2,
        flops=6 * 10**9,
    )
    other_rows = shifted(mine, "core", 1)
    got_r = shifted(send_r, "core", 1)
    dw_keep, dw_send = call(
        weights_kernel,
        [((4, 128, HW), F32), ((4, 128, HW), BF16)],
        (res, mine, other_rows),
        [((LC, 256), BF16), ((LC, 256), BF16)],
        smem=(),
        flops=10**9,
    )
    dw_got = shifted(dw_send, "dp", 1)
    msg = (CL + ROWS, WL + 128)
    m1, m2, m3, own, cz, inv = call(
        partial_kernel,
        [(msg, BF16), (msg, BF16), (msg, BF16), (msg, F32), ((ROWS, WL), BF16), ((ROWS, 128), F32)],
        (keep_r, got_r, c48, gain, *weights),
        [((4, ROWS, WL), BF16)],
        smem=(),
        flops=10**9,
    )
    r1, r2, r3 = shifted(m1, "tensor", 1), shifted(m2, "tensor", 2), shifted(m3, "tensor", 3)
    dw_own, dw_other = call(
        total_kernel,
        [((4, 64, HW), F32), ((4, 64, HW), BF16)],
        (dw_keep, dw_got, r1),
        smem=(),
    )
    dw_other = shifted(dw_other, "core", 1)
    update, grad_tokens, *dw = call(
        after_kernel,
        [((SEG, WL), BF16)] * 2 + [((64, WL), F32)] * 4,
        (lengths, own, r1, r2, r3, cz, inv, gain, conv_first, conv_second, up_gain, dw_own, dw_other),
        [((ROWS, WL), F32)],
    )
    return (update[None], grad_tokens[None], *dw)


def solution(mesh):
    ctx = ("x", "y", "core")
    fine = Mesh(
        np.asarray(mesh.devices).reshape(2, 4, 2, 2, 4), ("dp", "x", "y", "core", "tensor")
    )
    tok = P("dp", ctx, "tensor")
    col = P(None, "tensor")
    in_specs = (tok, P("dp"), col, col, P(), col, col, col, col, col, P(), col, tok)
    dw = P(("dp",) + ctx, "tensor")
    return jax.shard_map(
        local, mesh=fine, in_specs=in_specs, out_specs=(tok, tok, dw, dw, dw, dw), check_vma=False
    )
```

```python
import math

import jax
import jax.numpy as jnp
import numpy as np
from jax import lax
from jax.experimental import pallas as pl
from jax.experimental.pallas import tpu as pltpu
from jax.sharding import Mesh, PartitionSpec as P

F32 = jnp.float32
BF16 = jnp.bfloat16
NEG = float("-inf")
D = 2048
WL = 512
LC = 512
CL = 32
SEG = 512
HD = 128
NH = 2
HW = NH * HD
SCALE = 1.0 / math.sqrt(HD)
ROWS = CL + 16
VM = pltpu.VMEM
BIG = 63 * 2**20
SM = pltpu.SMEM
PIECE = 4 * CL


def dg(a, b, ca, cb):
    return lax.dot_general(a, b, (((ca,), (cb,)), ((), ())), preferred_element_type=F32)


class Place:
    def __init__(self):
        self.x, self.y, self.core = (lax.axis_index(a) for a in ("x", "y", "core"))
        self.dp, self.z = lax.axis_index("dp"), lax.axis_index("tensor")
        self.ctx = (self.x * 2 + self.y) * 2 + self.core


def tap_weights(first, second):
    taps = jnp.concatenate([second[a : a + 1] * first for a in range(4)], axis=0)
    return jnp.concatenate([taps[15:16], taps[:15]], axis=0)


def byte_mask(ctx, doc_len):
    pos = ctx * SEG + 16 * lax.broadcasted_iota(jnp.int32, (CL, 16, WL), 0)
    pos = pos + lax.broadcasted_iota(jnp.int32, (CL, 16, WL), 1)
    return (pos < doc_len).astype(F32)


def before_kernel(
    lens, tokens_h, grad_h, first_h, second_h, up_h, gain_h, part, last, gco, gain,
    tokens, grad_out, first, second, up_gain, shift, sems,
):
    pairs = ((tokens_h, tokens), (first_h, first), (second_h, second), (grad_h, grad_out), (up_h, up_gain), (gain_h, gain))
    copies = [pltpu.make_async_copy(a, b, sems.at[i]) for i, (a, b) in enumerate(pairs)]
    for c in copies:
        c.start()
    mask = byte_mask(Place().ctx, lens[0])
    u = lax.broadcasted_iota(jnp.int32, (CL, 16, WL), 1)
    for c in copies[:3]:
        c.wait()
    taps = tap_weights(first[...], second[...])
    prod = tokens[...].astype(F32).reshape(CL, 16, WL) * mask * taps[None]
    own = jnp.sum(jnp.where(u == 0, prod, 0.0), axis=1)
    onward = jnp.sum(jnp.where(u == 0, 0.0, prod), axis=1)
    shift[0:8] = jnp.zeros((8, WL), F32)
    shift[8 : 8 + CL] = onward
    part[...] = own + shift[7 : 7 + CL]
    last[...] = jnp.broadcast_to(shift[7 + CL : 8 + CL], (8, WL))
    for c in copies[3:]:
        c.wait()
    weighted = grad_out[...].astype(F32).reshape(CL, 16, WL) * mask * up_gain[...][None]
    gco[...] = jnp.sum(weighted, axis=1).astype(BF16)


def piece_kernel(part, gco, rim, piece):
    first = lax.broadcasted_iota(jnp.int32, (CL, WL), 0) == 0
    piece[0:CL] = (part[...] + jnp.where(first, rim[0:1], 0.0)).astype(BF16)
    piece[CL : 2 * CL] = gco[...]


def pile_kernel(piece, across, out):
    y = Place().y
    out[pl.ds(pl.multiple_of(y * 64, 64), 64)] = piece[...]
    out[pl.ds(pl.multiple_of(64 - y * 64, 64), 64)] = across[...]


def bias_kernel(near, table, strip):
    core = Place().core
    n = near.shape[1]
    which = near[0:1]
    for h in range(NH):
        row = jnp.full((1, n), NEG, F32)
        for b in range(table.shape[0]):
            row = jnp.where(which == b, table[b, core * NH + h], row)
        rolled = pltpu.roll(jnp.broadcast_to(row, (128, n)), 0, 1, stride=1, stride_axis=0)
        strip[h] = rolled[:, :LC]


def project_kernel(
    p0, r1, r2, r3, gain, wq, wk, wv, wo, keep, send, blocks, mine, craw, nrm, gco, both
):
    at = Place()
    z, core, x, y = at.z, at.core, at.x, at.y
    for s, src in enumerate((p0, r1, r2, r3)):
        cols = pl.ds(pl.multiple_of(lax.rem(z + 4 - s, 4) * WL, WL), WL)
        for i in range(2):
            rows = slice(i * CL, i * CL + CL)
            craw[rows, cols] = src[2 * i * CL : 2 * i * CL + CL]
            gco[rows, cols] = src[2 * i * CL + CL : 2 * i * CL + 2 * CL]
    mine[...] = craw[pl.ds(pl.multiple_of(y * CL, CL), CL)]
    c = craw[...].astype(F32)
    r = lax.rsqrt(jnp.sum(c * c, axis=1, keepdims=True) * (1.0 / D) + 1e-6)
    nrm[...] = (c * r * gain[...]).astype(BF16)
    for src, w, slot in ((gco, wo, 3), (nrm, wq, 0), (nrm, wk, 1), (nrm, wv, 2)):
        v = jnp.dot(src[...], w[...], preferred_element_type=F32).astype(BF16)
        for half in range(2):
            both[half, :, slot * HW : slot * HW + HW] = v[:, half * HW : half * HW + HW]
    keep[...] = both[core]
    send[0:64] = both[1 - core]
    tops = [c[i * CL : i * CL + 1, j * 1024 : j * 1024 + 1024] for i in range(2) for j in range(2)]
    send[64:80] = jnp.concatenate(tops + [jnp.zeros((12, 1024), F32)], axis=0).astype(BF16)
    for s in range(4):
        for d in range(2):
            chip = lax.rem(x + s, 4) * 2 + y
            cols = pl.ds(pl.multiple_of((d * 8 + chip) * 128, 128), 128)
            for i in range(2):
                rows = slice(i * CL, i * CL + CL)
                at = i * 512 + d * 128
                blocks[s, :, at : at + 128] = nrm[rows, cols]
                blocks[s, :, at + 256 : at + 384] = gco[rows, cols]


def pack_kernel(keep, swapped, blocks, b0, up, down):
    core = Place().core
    for i in range(2):
        for src, c in ((keep, core), (swapped, 1 - core)):
            row = i * 64 + c * CL
            new = src[i * CL : i * CL + CL]
            b0[pl.ds(pl.multiple_of(row, CL), CL)] = new
            up[pl.ds(pl.multiple_of((96 if i == 0 else -32) + row, CL), CL)] = new
            down[pl.ds(pl.multiple_of(32 + row, CL), CL)] = new
    b0[128:160] = blocks[0]
    up[0:32] = blocks[1]
    down[0:32] = blocks[3]
    up[160:176] = blocks[2, 0:16]
    down[160:176] = blocks[2, 16:32]
    down[176:192] = swapped[64:80]


def onward_kernel(src, out):
    out[...] = src[96:176]


def gather_kernel(b0, low, high, far_low, far_high, swapped, mine, nxt):
    mine[0] = b0[128:160]
    mine[1] = low[0:32]
    mine[2, 0:16] = far_low[64:80]
    mine[2, 16:32] = far_high[64:80]
    mine[3] = high[0:32]
    at = Place()
    wraps = jnp.logical_and(at.core == 1, at.y == 1)
    tops = jnp.where(wraps, high[176:192].astype(F32), swapped[64:80].astype(F32))
    upper = jnp.where(at.core == 0, at.y, 1 - at.y) == 1
    for j in range(2):
        row = jnp.where(upper, tops[2 + j : 3 + j], tops[j : j + 1])
        nxt[:, j * 1024 : j * 1024 + 1024] = jnp.broadcast_to(row, (16, 1024)).astype(BF16)


def attend_kernel(
    lens, b0, low, high, far_low, far_high, strip, res, keep, send, q, k, v, ga, acck, accv
):
    at = Place()
    ctx, core, x, doc_len = at.ctx, at.core, at.x, lens[0]
    for src, first, n, s, row in (
        (b0, 0, 128, 0, 0),
        (low, 96, 64, 1, 0),
        (low, 32, 64, 1, 64),
        (far_low, 0, 64, 2, 0),
        (far_high, 0, 64, 2, 64),
        (high, 32, 128, 3, 0),
    ):
        rows = pl.ds(pl.multiple_of(lax.rem(x + 4 - s, 4) * 128 + row, 64), n)
        for i, dst in enumerate((q, k, v, ga)):
            dst[rows] = src[first : first + n, i * HW : i * HW + HW]
    key_pos = lax.broadcasted_iota(jnp.int32, (1, LC), 1)
    key_mask = jnp.where(16 * key_pos < doc_len, 0.0, NEG)
    for h in range(NH):
        cols = slice(h * HD, h * HD + HD)
        for b in (3, 2, 1, 0):
            rows = slice(b * 128, b * 128 + 128)
            n = b * 128 + 128
            qb, gb, kb, vb = q[rows, cols], ga[rows, cols], k[0:n, cols], v[0:n, cols]
            s = dg(qb, kb, 1, 1) * SCALE + strip[h, :, LC - n :] + key_mask[:, :n]
            e = jnp.exp(s - jnp.max(s, axis=1, keepdims=True))
            p = e * (1.0 / jnp.sum(e, axis=1, keepdims=True))
            pb = p.astype(BF16)
            ab = jnp.dot(pb, vb, preferred_element_type=F32).astype(BF16)
            res[3, rows, cols] = ab
            dot = jnp.sum(gb.astype(F32) * ab.astype(F32), axis=1, keepdims=True)
            sg = (p * (dg(gb, vb, 1, 1) - dot)).astype(BF16)
            res[0, rows, cols] = (jnp.dot(sg, kb, preferred_element_type=F32) * SCALE).astype(BF16)
            tk = dg(sg, qb, 0, 0)
            tv = dg(pb, gb, 0, 0)
            if b == 3:
                acck[h] = tk
                accv[h] = tv
            else:
                acck[h, 0:n] += tk
                accv[h, 0:n] += tv
        res[1, 0:LC, cols] = (acck[h] * SCALE).astype(BF16)
        res[2, 0:LC, cols] = accv[h].astype(BF16)
    res[:, LC : LC + 16] = jnp.zeros((4, 16, HW), BF16)
    peer = ctx + 1 - 2 * core
    keep[...] = res[:, pl.ds(pl.multiple_of(ctx * CL, CL), ROWS)]
    send[...] = res[:, pl.ds(pl.multiple_of(peer * CL, CL), ROWS)]


def weights_kernel(res, mine, other, keep, to_core, to_dp, to_both, nb, gb, tile):
    at = Place()
    core, x, dp = at.core, at.x, at.dp
    for s in range(4):
        for src, c in ((mine, core), (other, 1 - core)):
            for i in range(2):
                row = (lax.rem(x + 4 - s, 4) * 4 + i * 2 + c) * CL
                rows = pl.ds(pl.multiple_of(row, CL), CL)
                nb[rows] = src[s, :, i * 512 : i * 512 + 256]
                gb[rows] = src[s, :, i * 512 + 256 : i * 512 + 512]
    for w in range(4):
        src = gb if w == 3 else nb
        for d, a, b in ((dp, keep, to_core), (1 - dp, to_dp, to_both)):
            cols = pl.ds(pl.multiple_of(d * 128, 128), 128)
            tile[...] = dg(src[:, cols], res[w, 0:LC], 0, 0)
            a[w] = tile[pl.ds(pl.multiple_of(core * 64, 64), 64)].astype(a.dtype)
            b[w] = tile[pl.ds(pl.multiple_of(64 - core * 64, 64), 64)].astype(BF16)


def partial_kernel(
    keep_r, got_r, crow, nxt, after, gain, wq, wk, wv, wo, msg1, msg2, msg3, keep, cz, inv_out, g, c
):
    at = Place()
    z, core = at.z, at.core
    g[:, :, pl.ds(pl.multiple_of(core * HW, HW), HW)] = keep_r[...]
    g[:, :, pl.ds(pl.multiple_of((1 - core) * HW, HW), HW)] = got_r[...]
    c[0:CL] = crow[...]
    c[CL:ROWS] = nxt[...]
    cf = c[...].astype(F32)
    r = lax.rsqrt(jnp.sum(cf * cf, axis=1, keepdims=True) * (1.0 / D) + 1e-6)
    inv_out[...] = jnp.broadcast_to(r, (ROWS, 128))
    lane = lax.broadcasted_iota(jnp.int32, (ROWS, 128), 1)
    dots = jnp.zeros((ROWS, 1), F32)
    for shift, msg in ((1, msg1), (2, msg2), (3, msg3), (0, keep)):
        t = lax.rem(z + shift, 4)
        part = pl.ds(pl.multiple_of(t * WL, WL), WL)
        gn = dg(g[0], wq[part], 1, 1) + dg(g[1], wk[part], 1, 1) + dg(g[2], wv[part], 1, 1)
        cb = c[:, part]
        dots = dots + jnp.sum(gn * gain[0:1, part] * cb.astype(F32), axis=1, keepdims=True)
        msg[0:CL, 0:WL] = dg(g[3, 0:CL], wo[part], 1, 1).astype(msg.dtype)
        msg[CL : CL + ROWS, 0:WL] = gn.astype(msg.dtype)
        msg[0:CL, WL : WL + 128] = jnp.zeros((CL, 128), msg.dtype)
        if shift == 0:
            cz[...] = cb
    keep[CL : CL + ROWS, WL : WL + 128] = jnp.broadcast_to(dots, (ROWS, 128))
    hi = dots.astype(BF16)
    lo = (dots - hi.astype(F32)).astype(BF16)
    lo2 = (dots - hi.astype(F32) - lo.astype(F32)).astype(BF16)
    packed = jnp.where(lane == 0, hi.astype(F32), jnp.where(lane == 1, lo.astype(F32), lo2.astype(F32)))
    packed = jnp.where(lane < 3, packed, 0.0).astype(BF16)
    for msg in (msg1, msg2, msg3):
        msg[CL : CL + ROWS, WL : WL + 128] = packed


def total_kernel(dw, from_core, from_dp, from_both, o0, o1, o2, o3):
    core = Place().core
    for w, o in enumerate((o0, o1, o2, o3)):
        o[:, pl.ds(pl.multiple_of(core * HW, HW), HW)] = dw[w] + from_dp[w].astype(F32)
        there = from_core[w].astype(F32) + from_both[w].astype(F32)
        o[:, pl.ds(pl.multiple_of((1 - core) * HW, HW), HW)] = there


def after_kernel(
    lens, keep, r1, r2, r3, cz, inv, gain, first, second, up_gain, update, grad, rows
):
    at = Place()
    ctx, doc_len, z = at.ctx, lens[0], at.z
    mask = byte_mask(ctx, doc_len)
    body = slice(0, WL)
    out = keep[0:CL, body]
    gn = keep[CL : CL + ROWS, body]
    dots = keep[CL : CL + ROWS, WL : WL + 1]
    for r in (r1, r2, r3):
        out = out + r[0:CL, body].astype(F32)
        gn = gn + r[CL : CL + ROWS, body].astype(F32)
        dots = dots + jnp.sum(r[CL : CL + ROWS, WL : WL + 128].astype(F32), axis=1, keepdims=True)
    update[...] = ((out[:, None, :] * up_gain[...][None]) * mask).reshape(SEG, WL).astype(BF16)
    i = inv[:, 0:1]
    gained = gn * gain[0:1, pl.ds(pl.multiple_of(z * WL, WL), WL)]
    full = i * gained - cz[...].astype(F32) * (i * i * i) * dots * (1.0 / D)
    exists = lax.broadcasted_iota(jnp.int32, (ROWS, WL), 0) + ctx * CL < LC
    rows[...] = jnp.where(exists, full, 0.0)
    taps = tap_weights(first[...], second[...])
    u = lax.broadcasted_iota(jnp.int32, (CL, 16, WL), 1)
    picked = jnp.where(u == 0, rows[0:CL][:, None, :], rows[1 : CL + 1][:, None, :])
    grad[...] = (picked * taps[None] * mask).reshape(SEG, WL).astype(BF16)


def call(kernel, outs, args, scratch=(), smem=(0,), flops=0, size=0, vmem=8 * 2**20, hbm=(), typed=True):
    def spec(i):
        return pl.BlockSpec(memory_space=SM if i in smem else pltpu.HBM if i in hbm else VM)

    return pl.pallas_call(
        kernel,
        out_shape=[pltpu.VMEM(s, d) if typed else jax.ShapeDtypeStruct(s, d) for s, d in outs],
        in_specs=[spec(i) for i in range(len(args))],
        out_specs=[pl.BlockSpec(memory_space=VM)] * len(outs),
        scratch_shapes=[pltpu.VMEM(*s) if isinstance(s, tuple) else s for s in scratch],
        compiler_params=pltpu.CompilerParams(vmem_limit_bytes=vmem),
        cost_estimate=pl.CostEstimate(flops=flops, bytes_accessed=size, transcendentals=0),
    )(*args)


def shifted(x, axis, steps):
    n = lax.axis_size(axis)
    return lax.ppermute(x, axis, [(i, (i + steps) % n) for i in range(n)])


def local(
    tokens, lengths, conv_first, conv_second, norm_gain, w_query, w_key, w_value, w_out,
    bias_table, buckets, up_gain, grad_out,
):
    weights = (w_query, w_key, w_value, w_out)
    part, last, gco, gain = call(
        before_kernel,
        [((CL, WL), F32), ((8, WL), F32), ((CL, WL), BF16), ((1, D), F32)],
        (lengths, tokens[0], grad_out[0], conv_first, conv_second, up_gain, norm_gain[None]),
        [
            ((SEG, WL), BF16), ((SEG, WL), BF16), ((4, WL), F32), ((4, WL), F32), ((16, WL), F32),
            ((CL + 8, WL), F32), pltpu.SemaphoreType.DMA((6,)),
        ],
        hbm=(1, 2, 3, 4, 5, 6),
        vmem=BIG,
    )
    line = ("x", "y", "core")
    rim = lax.ppermute(last, line, [(i, i + 1) for i in range(15)])
    (piece,) = call(piece_kernel, [((2 * CL, WL), BF16)], (part, gco, rim), smem=())
    across = shifted(piece, "y", 1)
    (piece,) = call(
        pile_kernel,
        [((PIECE, WL), BF16)],
        (piece, across),
        smem=(),
        flops=6 * 10**9,
    )
    n = 640
    near = jnp.concatenate(
        [
            jnp.flip(buckets[:385]),
            jnp.full((n - LC,), bias_table.shape[0], jnp.int32),
            jnp.flip(buckets[385:]),
        ]
    )
    (strip,) = call(
        bias_kernel,
        [((NH, 128, LC), F32)],
        (jnp.broadcast_to(near[None], (8, n)), bias_table),
        smem=(1,),
    )
    pieces = [piece] + [shifted(piece, "tensor", s) for s in (1, 2, 3)]
    keep, send, blocks, crow = call(
        project_kernel,
        [((64, 4 * HW), BF16), ((80, 4 * HW), BF16), ((4, CL, 4 * HW), BF16), ((CL, D), BF16)],
        (*pieces, gain, *weights),
        [((2 * CL, D), BF16), ((2 * CL, D), BF16), ((2 * CL, D), BF16), ((2, 2 * CL, 4 * HW), BF16)],
        smem=(),
        flops=10**9,
    )
    swapped = shifted(send, "core", 1)
    b0, up, down = call(
        pack_kernel,
        [((160, 4 * HW), BF16), ((176, 4 * HW), BF16), ((192, 4 * HW), BF16)],
        (keep, swapped, blocks),
        smem=(),
    )
    low, high = shifted(up, "x", 1), shifted(down, "x", -1)
    far = [((80, 4 * HW), BF16)]
    far_low = shifted(call(onward_kernel, far, (low,), smem=())[0], "x", 1)
    far_high = shifted(call(onward_kernel, far, (high,), smem=())[0], "x", -1)
    mine, nxt = call(
        gather_kernel,
        [((4, CL, 4 * HW), BF16), ((16, D), BF16)],
        (b0, low, high, far_low, far_high, swapped),
        smem=(),
    )
    other_rows = shifted(mine, "core", 1)
    res, keep_r, send_r = call(
        attend_kernel,
        [((4, LC + 16, HW), BF16), ((4, ROWS, HW), BF16), ((4, ROWS, HW), BF16)],
        (lengths, b0, low, high, far_low, far_high, strip),
        [((LC, HW), BF16)] * 4 + [((NH, LC, HD), F32)] * 2,
        flops=6 * 10**9,
    )
    got_r = shifted(send_r, "core", 1)
    dw_keep, to_core, to_dp, to_both = call(
        weights_kernel,
        [((4, 64, HW), F32)] + [((4, 64, HW), BF16)] * 3,
        (res, mine, other_rows),
        [((LC, 256), BF16), ((LC, 256), BF16), ((128, HW), F32)],
        smem=(),
        flops=10**9,
    )
    from_core, from_dp = shifted(to_core, "core", 1), shifted(to_dp, "dp", 1)
    from_both = lax.ppermute(to_both, ("dp", "core"), [(i, 3 - i) for i in range(4)])
    msg = (CL + ROWS, WL + 128)
    m1, m2, m3, own, cz, inv = call(
        partial_kernel,
        [(msg, BF16), (msg, BF16), (msg, BF16), (msg, F32), ((ROWS, WL), BF16), ((ROWS, 128), F32)],
        (keep_r, got_r, crow, nxt, dw_keep, gain, *weights),
        [((4, ROWS, WL), BF16), ((ROWS, D), BF16)],
        smem=(),
        flops=10**9,
    )
    r1, r2, r3 = shifted(m1, "tensor", 1), shifted(m2, "tensor", 2), shifted(m3, "tensor", 3)
    dw = call(
        total_kernel,
        [((64, WL), F32)] * 4,
        (dw_keep, from_core, from_dp, from_both),
        smem=(),
        flops=6 * 10**9,
        typed=False,
    )
    update, grad_tokens = call(
        after_kernel,
        [((SEG, WL), BF16)] * 2,
        (lengths, own, r1, r2, r3, cz, inv, gain, conv_first, conv_second, up_gain),
        [((ROWS, WL), F32)],
        typed=False,
    )
    return (update[None], grad_tokens[None], *dw)


def solution(mesh):
    ctx = ("x", "y", "core")
    fine = Mesh(
        np.asarray(mesh.devices).reshape(2, 4, 2, 2, 4), ("dp", "x", "y", "core", "tensor")
    )
    tok = P("dp", ctx, "tensor")
    col = P(None, "tensor")
    in_specs = (tok, P("dp"), col, col, P(), col, col, col, col, col, P(), col, tok)
    dw = P(("dp",) + ctx, "tensor")
    return jax.shard_map(
        local, mesh=fine, in_specs=in_specs, out_specs=(tok, tok, dw, dw, dw, dw), check_vma=False
    )
```

```python
import math

import jax
import jax.numpy as jnp
import numpy as np
from jax import lax
from jax.experimental import pallas as pl
from jax.experimental.pallas import tpu as pltpu
from jax.sharding import Mesh, PartitionSpec as P

F32 = jnp.float32
BF16 = jnp.bfloat16
NEG = float("-inf")
D = 2048
WL = 512
LC = 512
CL = 32
SEG = 512
HD = 128
NH = 2
HW = NH * HD
SCALE = 1.0 / math.sqrt(HD)
ROWS = CL + 16
VM = pltpu.VMEM
BIG = 63 * 2**20
SM = pltpu.SMEM
PIECE = 4 * CL


def dg(a, b, ca, cb):
    return lax.dot_general(a, b, (((ca,), (cb,)), ((), ())), preferred_element_type=F32)


class Place:
    def __init__(self):
        self.x, self.y, self.core = (lax.axis_index(a) for a in ("x", "y", "core"))
        self.dp, self.z = lax.axis_index("dp"), lax.axis_index("tensor")
        self.ctx = (self.x * 2 + self.y) * 2 + self.core


def tap_weights(first, second):
    taps = jnp.concatenate([second[a : a + 1] * first for a in range(4)], axis=0)
    return jnp.concatenate([taps[15:16], taps[:15]], axis=0)


def byte_mask(ctx, doc_len):
    pos = ctx * SEG + 16 * lax.broadcasted_iota(jnp.int32, (CL, 16, WL), 0)
    pos = pos + lax.broadcasted_iota(jnp.int32, (CL, 16, WL), 1)
    return (pos < doc_len).astype(F32)


def before_kernel(
    lens, tokens_h, grad_h, first_h, second_h, up_h, gain_h, part, last, gco, gain,
    tokens, grad_out, first, second, up_gain, shift, sems,
):
    pairs = ((tokens_h, tokens), (first_h, first), (second_h, second), (grad_h, grad_out), (up_h, up_gain), (gain_h, gain))
    copies = [pltpu.make_async_copy(a, b, sems.at[i]) for i, (a, b) in enumerate(pairs)]
    for c in copies:
        c.start()
    mask = byte_mask(Place().ctx, lens[0])
    u = lax.broadcasted_iota(jnp.int32, (CL, 16, WL), 1)
    for c in copies[:3]:
        c.wait()
    taps = tap_weights(first[...], second[...])
    prod = tokens[...].astype(F32).reshape(CL, 16, WL) * mask * taps[None]
    own = jnp.sum(jnp.where(u == 0, prod, 0.0), axis=1)
    onward = jnp.sum(jnp.where(u == 0, 0.0, prod), axis=1)
    shift[0:8] = jnp.zeros((8, WL), F32)
    shift[8 : 8 + CL] = onward
    part[...] = own + shift[7 : 7 + CL]
    last[...] = jnp.broadcast_to(shift[7 + CL : 8 + CL], (8, WL))
    for c in copies[3:]:
        c.wait()
    weighted = grad_out[...].astype(F32).reshape(CL, 16, WL) * mask * up_gain[...][None]
    gco[...] = jnp.sum(weighted, axis=1).astype(BF16)


def piece_kernel(part, gco, rim, piece):
    first = lax.broadcasted_iota(jnp.int32, (CL, WL), 0) == 0
    piece[0:CL] = (part[...] + jnp.where(first, rim[0:1], 0.0)).astype(BF16)
    piece[CL : 2 * CL] = gco[...]


def pile_kernel(piece, across, out):
    y = Place().y
    out[pl.ds(pl.multiple_of(y * 64, 64), 64)] = piece[...]
    out[pl.ds(pl.multiple_of(64 - y * 64, 64), 64)] = across[...]


def bias_kernel(near, table, strip):
    core = Place().core
    n = near.shape[1]
    which = near[0:1]
    for h in range(NH):
        row = jnp.full((1, n), NEG, F32)
        for b in range(table.shape[0]):
            row = jnp.where(which == b, table[b, core * NH + h], row)
        rolled = pltpu.roll(jnp.broadcast_to(row, (128, n)), 0, 1, stride=1, stride_axis=0)
        strip[h] = rolled[:, :LC]


def project_kernel(
    p0, r1, r2, r3, gain, wq, wk, wv, wo, keep, send, blocks, mine, craw, nrm, gco, both
):
    at = Place()
    z, core, x, y = at.z, at.core, at.x, at.y
    for s, src in enumerate((p0, r1, r2, r3)):
        cols = pl.ds(pl.multiple_of(lax.rem(z + 4 - s, 4) * WL, WL), WL)
        for i in range(2):
            rows = slice(i * CL, i * CL + CL)
            craw[rows, cols] = src[2 * i * CL : 2 * i * CL + CL]
            gco[rows, cols] = src[2 * i * CL + CL : 2 * i * CL + 2 * CL]
    mine[...] = craw[pl.ds(pl.multiple_of(y * CL, CL), CL)]
    c = craw[...].astype(F32)
    r = lax.rsqrt(jnp.sum(c * c, axis=1, keepdims=True) * (1.0 / D) + 1e-6)
    nrm[...] = (c * r * gain[...]).astype(BF16)
    for src, w, slot in ((gco, wo, 3), (nrm, wq, 0), (nrm, wk, 1), (nrm, wv, 2)):
        v = jnp.dot(src[...], w[...], preferred_element_type=F32).astype(BF16)
        for half in range(2):
            both[half, :, slot * HW : slot * HW + HW] = v[:, half * HW : half * HW + HW]
    keep[...] = both[core]
    send[0:64] = both[1 - core]
    tops = [c[i * CL : i * CL + 1, j * 1024 : j * 1024 + 1024] for i in range(2) for j in range(2)]
    send[64:80] = jnp.concatenate(tops + [jnp.zeros((12, 1024), F32)], axis=0).astype(BF16)
    for s in range(4):
        for d in range(2):
            chip = lax.rem(x + s, 4) * 2 + y
            cols = pl.ds(pl.multiple_of((d * 8 + chip) * 128, 128), 128)
            for i in range(2):
                rows = slice(i * CL, i * CL + CL)
                at = i * 512 + d * 128
                blocks[s, :, at : at + 128] = nrm[rows, cols]
                blocks[s, :, at + 256 : at + 384] = gco[rows, cols]


def pack_kernel(keep, swapped, blocks, b0, up_far, up_near, down_far, down_near):
    core = Place().core
    for i in range(2):
        for src, c in ((keep, core), (swapped, 1 - core)):
            new = src[i * CL : i * CL + CL]
            row = pl.multiple_of(c * CL, CL)
            b0[pl.ds(pl.multiple_of(i * 64 + row, CL), CL)] = new
            up, down, a, b = ((up_far, down_near, 0, 32), (up_near, down_far, 32, 0))[i]
            up[pl.ds(pl.multiple_of(a + row, CL), CL)] = new
            down[pl.ds(pl.multiple_of(b + row, CL), CL)] = new
    b0[128:160] = blocks[0]
    up_near[0:32] = blocks[1]
    down_near[0:32] = blocks[3]
    up_far[64:80] = blocks[2, 0:16]
    down_far[64:80] = blocks[2, 16:32]
    down_near[96:112] = swapped[64:80]


def gather_kernel(b0, low_near, high_near, far_low, far_high, swapped, mine, nxt):
    mine[0] = b0[128:160]
    mine[1] = low_near[0:32]
    mine[2, 0:16] = far_low[64:80]
    mine[2, 16:32] = far_high[64:80]
    mine[3] = high_near[0:32]
    at = Place()
    wraps = jnp.logical_and(at.core == 1, at.y == 1)
    tops = jnp.where(wraps, high_near[96:112].astype(F32), swapped[64:80].astype(F32))
    upper = jnp.where(at.core == 0, at.y, 1 - at.y) == 1
    for j in range(2):
        row = jnp.where(upper, tops[2 + j : 3 + j], tops[j : j + 1])
        nxt[:, j * 1024 : j * 1024 + 1024] = jnp.broadcast_to(row, (16, 1024)).astype(BF16)


def attend_kernel(
    lens, b0, low_far, low_near, high_far, high_near, far_low, far_high, strip,
    res, keep, send, q, k, v, ga, acck, accv,
):
    at = Place()
    ctx, core, x, doc_len = at.ctx, at.core, at.x, lens[0]
    for src, first, n, s, row in (
        (b0, 0, 128, 0, 0),
        (low_far, 0, 64, 1, 0),
        (low_near, 32, 64, 1, 64),
        (far_low, 0, 64, 2, 0),
        (far_high, 0, 64, 2, 64),
        (high_near, 32, 64, 3, 0),
        (high_far, 0, 64, 3, 64),
    ):
        rows = pl.ds(pl.multiple_of(lax.rem(x + 4 - s, 4) * 128 + row, 64), n)
        for i, dst in enumerate((q, k, v, ga)):
            dst[rows] = src[first : first + n, i * HW : i * HW + HW]
    key_pos = lax.broadcasted_iota(jnp.int32, (1, LC), 1)
    key_mask = jnp.where(16 * key_pos < doc_len, 0.0, NEG)
    heads = [(h, slice(h * HD, h * HD + HD)) for h in range(NH)]
    for b in (3, 2, 1, 0):
        rows = slice(b * 128, b * 128 + 128)
        n = b * 128 + 128
        qb, gb = [[r[rows, c] for _, c in heads] for r in (q, ga)]
        kb, vb = [[r[0:n, c] for _, c in heads] for r in (k, v)]
        s = [dg(qb[h], kb[h], 1, 1) for h, _ in heads]
        dp = [dg(gb[h], vb[h], 1, 1) for h, _ in heads]
        s = [s[h] * SCALE + strip[h, :, LC - n :] + key_mask[:, :n] for h, _ in heads]
        e = [jnp.exp(a - jnp.max(a, axis=1, keepdims=True)) for a in s]
        p = [a * (1.0 / jnp.sum(a, axis=1, keepdims=True)) for a in e]
        dot = [jnp.sum(p[h] * dp[h], axis=1, keepdims=True) for h, _ in heads]
        sg = [(p[h] * (dp[h] - dot[h])).astype(BF16) for h, _ in heads]
        pb = [a.astype(BF16) for a in p]
        for h, c in heads:
            tk = dg(sg[h], qb[h], 0, 0)
            tv = dg(pb[h], gb[h], 0, 0)
            if b == 3:
                acck[h] = tk
                accv[h] = tv
            else:
                acck[h, 0:n] += tk
                accv[h, 0:n] += tv
            gq = jnp.dot(sg[h], kb[h], preferred_element_type=F32) * SCALE
            res[0, rows, c] = gq.astype(BF16)
            res[3, rows, c] = jnp.dot(pb[h], vb[h], preferred_element_type=F32).astype(BF16)
    for h, c in heads:
        res[1, 0:LC, c] = (acck[h] * SCALE).astype(BF16)
        res[2, 0:LC, c] = accv[h].astype(BF16)
    res[:, LC : LC + 16] = jnp.zeros((4, 16, HW), BF16)
    peer = ctx + 1 - 2 * core
    keep[...] = res[:, pl.ds(pl.multiple_of(ctx * CL, CL), ROWS)]
    send[...] = res[:, pl.ds(pl.multiple_of(peer * CL, CL), ROWS)]


def weights_kernel(res, mine, other, keep, send, nb, gb):
    at = Place()
    core, x, dp = at.core, at.x, at.dp
    for s in range(4):
        for src, c in ((mine, core), (other, 1 - core)):
            for i in range(2):
                row = (lax.rem(x + 4 - s, 4) * 4 + i * 2 + c) * CL
                rows = pl.ds(pl.multiple_of(row, CL), CL)
                nb[rows] = src[s, :, i * 512 : i * 512 + 256]
                gb[rows] = src[s, :, i * 512 + 256 : i * 512 + 512]
    for w in range(4):
        src = gb if w == 3 else nb
        for d, out in ((dp, keep), (1 - dp, send)):
            cols = pl.ds(pl.multiple_of(d * 128, 128), 128)
            out[w] = dg(src[:, cols], res[w, 0:LC], 0, 0).astype(out.dtype)


def sum_kernel(keep, got, r1, r2, r3, own, send):
    core = Place().core
    for w in range(4):
        for c, out in ((core, own), (1 - core, send)):
            rows = pl.ds(pl.multiple_of(c * 64, 64), 64)
            out[w] = (keep[w, rows] + got[w, rows].astype(F32)).astype(out.dtype)


def partial_kernel(
    keep_r, got_r, crow, nxt, after, gain, wq, wk, wv, wo, msg1, msg2, msg3, keep, cz, inv_out, g, c
):
    at = Place()
    z, core = at.z, at.core
    g[:, :, pl.ds(pl.multiple_of(core * HW, HW), HW)] = keep_r[...]
    g[:, :, pl.ds(pl.multiple_of((1 - core) * HW, HW), HW)] = got_r[...]
    c[0:CL] = crow[...]
    c[CL:ROWS] = nxt[...]
    cf = c[...].astype(F32)
    r = lax.rsqrt(jnp.sum(cf * cf, axis=1, keepdims=True) * (1.0 / D) + 1e-6)
    inv_out[...] = jnp.broadcast_to(r, (ROWS, 128))
    lane = lax.broadcasted_iota(jnp.int32, (ROWS, 128), 1)
    dots = jnp.zeros((ROWS, 1), F32)
    for shift, msg in ((1, msg1), (2, msg2), (3, msg3), (0, keep)):
        t = lax.rem(z + shift, 4)
        part = pl.ds(pl.multiple_of(t * WL, WL), WL)
        gn = dg(g[0], wq[part], 1, 1) + dg(g[1], wk[part], 1, 1) + dg(g[2], wv[part], 1, 1)
        cb = c[:, part]
        dots = dots + jnp.sum(gn * gain[0:1, part] * cb.astype(F32), axis=1, keepdims=True)
        msg[0:CL, 0:WL] = dg(g[3, 0:CL], wo[part], 1, 1).astype(msg.dtype)
        msg[CL : CL + ROWS, 0:WL] = gn.astype(msg.dtype)
        msg[0:CL, WL : WL + 128] = jnp.zeros((CL, 128), msg.dtype)
        if shift == 0:
            cz[...] = cb
    keep[CL : CL + ROWS, WL : WL + 128] = jnp.broadcast_to(dots, (ROWS, 128))
    hi = dots.astype(BF16)
    lo = (dots - hi.astype(F32)).astype(BF16)
    lo2 = (dots - hi.astype(F32) - lo.astype(F32)).astype(BF16)
    packed = jnp.where(lane == 0, hi.astype(F32), jnp.where(lane == 1, lo.astype(F32), lo2.astype(F32)))
    packed = jnp.where(lane < 3, packed, 0.0).astype(BF16)
    for msg in (msg1, msg2, msg3):
        msg[CL : CL + ROWS, WL : WL + 128] = packed


def total_kernel(own, other, o0, o1, o2, o3):
    core = Place().core
    for w, o in enumerate((o0, o1, o2, o3)):
        o[:, pl.ds(pl.multiple_of(core * HW, HW), HW)] = own[w]
        o[:, pl.ds(pl.multiple_of((1 - core) * HW, HW), HW)] = other[w].astype(F32)


def after_kernel(
    lens, keep, r1, r2, r3, cz, inv, gain, first, second, up_gain, update, grad, rows
):
    at = Place()
    ctx, doc_len, z = at.ctx, lens[0], at.z
    mask = byte_mask(ctx, doc_len)
    body = slice(0, WL)
    out = keep[0:CL, body]
    gn = keep[CL : CL + ROWS, body]
    dots = keep[CL : CL + ROWS, WL : WL + 1]
    for r in (r1, r2, r3):
        out = out + r[0:CL, body].astype(F32)
        gn = gn + r[CL : CL + ROWS, body].astype(F32)
        dots = dots + jnp.sum(r[CL : CL + ROWS, WL : WL + 128].astype(F32), axis=1, keepdims=True)
    update[...] = ((out[:, None, :] * up_gain[...][None]) * mask).reshape(SEG, WL).astype(BF16)
    i = inv[:, 0:1]
    gained = gn * gain[0:1, pl.ds(pl.multiple_of(z * WL, WL), WL)]
    full = i * gained - cz[...].astype(F32) * (i * i * i) * dots * (1.0 / D)
    exists = lax.broadcasted_iota(jnp.int32, (ROWS, WL), 0) + ctx * CL < LC
    rows[...] = jnp.where(exists, full, 0.0)
    taps = tap_weights(first[...], second[...])
    u = lax.broadcasted_iota(jnp.int32, (CL, 16, WL), 1)
    picked = jnp.where(u == 0, rows[0:CL][:, None, :], rows[1 : CL + 1][:, None, :])
    grad[...] = (picked * taps[None] * mask).reshape(SEG, WL).astype(BF16)


def call(kernel, outs, args, scratch=(), smem=(0,), flops=0, size=0, vmem=8 * 2**20, hbm=(), typed=True):
    def spec(i):
        return pl.BlockSpec(memory_space=SM if i in smem else pltpu.HBM if i in hbm else VM)

    return pl.pallas_call(
        kernel,
        out_shape=[pltpu.VMEM(s, d) if typed else jax.ShapeDtypeStruct(s, d) for s, d in outs],
        in_specs=[spec(i) for i in range(len(args))],
        out_specs=[pl.BlockSpec(memory_space=VM)] * len(outs),
        scratch_shapes=[pltpu.VMEM(*s) if isinstance(s, tuple) else s for s in scratch],
        compiler_params=pltpu.CompilerParams(vmem_limit_bytes=vmem),
        cost_estimate=pl.CostEstimate(flops=flops, bytes_accessed=size, transcendentals=0),
    )(*args)


def shifted(x, axis, steps):
    n = lax.axis_size(axis)
    return lax.ppermute(x, axis, [(i, (i + steps) % n) for i in range(n)])


def local(
    tokens, lengths, conv_first, conv_second, norm_gain, w_query, w_key, w_value, w_out,
    bias_table, buckets, up_gain, grad_out,
):
    weights = (w_query, w_key, w_value, w_out)
    part, last, gco, gain = call(
        before_kernel,
        [((CL, WL), F32), ((8, WL), F32), ((CL, WL), BF16), ((1, D), F32)],
        (lengths, tokens[0], grad_out[0], conv_first, conv_second, up_gain, norm_gain[None]),
        [
            ((SEG, WL), BF16), ((SEG, WL), BF16), ((4, WL), F32), ((4, WL), F32), ((16, WL), F32),
            ((CL + 8, WL), F32), pltpu.SemaphoreType.DMA((6,)),
        ],
        hbm=(1, 2, 3, 4, 5, 6),
        vmem=BIG,
    )
    line = ("x", "y", "core")
    rim = lax.ppermute(last, line, [(i, i + 1) for i in range(15)])
    (piece,) = call(piece_kernel, [((2 * CL, WL), BF16)], (part, gco, rim), smem=())
    across = shifted(piece, "y", 1)
    (piece,) = call(
        pile_kernel,
        [((PIECE, WL), BF16)],
        (piece, across),
        smem=(),
        flops=6 * 10**9,
    )
    n = 640
    near = jnp.concatenate(
        [
            jnp.flip(buckets[:385]),
            jnp.full((n - LC,), bias_table.shape[0], jnp.int32),
            jnp.flip(buckets[385:]),
        ]
    )
    (strip,) = call(
        bias_kernel,
        [((NH, 128, LC), F32)],
        (jnp.broadcast_to(near[None], (8, n)), bias_table),
        smem=(1,),
    )
    pieces = [piece] + [shifted(piece, "tensor", s) for s in (1, 2, 3)]
    keep, send, blocks, crow = call(
        project_kernel,
        [((64, 4 * HW), BF16), ((80, 4 * HW), BF16), ((4, CL, 4 * HW), BF16), ((CL, D), BF16)],
        (*pieces, gain, *weights),
        [((2 * CL, D), BF16), ((2 * CL, D), BF16), ((2 * CL, D), BF16), ((2, 2 * CL, 4 * HW), BF16)],
        smem=(),
        flops=10**9,
    )
    swapped = shifted(send, "core", 1)
    b0, up_far, up_near, down_far, down_near = call(
        pack_kernel,
        [((n, 4 * HW), BF16) for n in (160, 80, 96, 80, 112)],
        (keep, swapped, blocks),
        smem=(),
    )
    low_far, high_far = shifted(up_far, "x", 1), shifted(down_far, "x", -1)
    low_near, high_near = shifted(up_near, "x", 1), shifted(down_near, "x", -1)
    far_low, far_high = shifted(low_far, "x", 1), shifted(high_far, "x", -1)
    mine, nxt = call(
        gather_kernel,
        [((4, CL, 4 * HW), BF16), ((16, D), BF16)],
        (b0, low_near, high_near, far_low, far_high, swapped),
        smem=(),
    )
    other_rows = shifted(mine, "core", 1)
    res, keep_r, send_r = call(
        attend_kernel,
        [((4, LC + 16, HW), BF16), ((4, ROWS, HW), BF16), ((4, ROWS, HW), BF16)],
        (lengths, b0, low_far, low_near, high_far, high_near, far_low, far_high, strip),
        [((LC, HW), BF16)] * 4 + [((NH, LC, HD), F32)] * 2,
        flops=6 * 10**9,
    )
    got_r = shifted(send_r, "core", 1)
    dw_keep, dw_send = call(
        weights_kernel,
        [((4, 128, HW), F32), ((4, 128, HW), BF16)],
        (res, mine, other_rows),
        [((LC, 256), BF16), ((LC, 256), BF16)],
        smem=(),
        flops=10**9,
    )
    dw_got = shifted(dw_send, "dp", 1)
    msg = (CL + ROWS, WL + 128)
    m1, m2, m3, own, cz, inv = call(
        partial_kernel,
        [(msg, BF16), (msg, BF16), (msg, BF16), (msg, F32), ((ROWS, WL), BF16), ((ROWS, 128), F32)],
        (keep_r, got_r, crow, nxt, dw_keep, gain, *weights),
        [((4, ROWS, WL), BF16), ((ROWS, D), BF16)],
        smem=(),
        flops=10**9,
    )
    r1, r2, r3 = shifted(m1, "tensor", 1), shifted(m2, "tensor", 2), shifted(m3, "tensor", 3)
    dw_own, dw_other = call(
        sum_kernel,
        [((4, 64, HW), F32), ((4, 64, HW), BF16)],
        (dw_keep, dw_got, r1, r2, r3),
        smem=(),
    )
    dw_other = shifted(dw_other, "core", 1)
    dw = call(
        total_kernel,
        [((64, WL), F32)] * 4,
        (dw_own, dw_other),
        smem=(),
        flops=6 * 10**9,
        typed=False,
    )
    update, grad_tokens = call(
        after_kernel,
        [((SEG, WL), BF16)] * 2,
        (lengths, own, r1, r2, r3, cz, inv, gain, conv_first, conv_second, up_gain),
        [((ROWS, WL), F32)],
        typed=False,
    )
    return (update[None], grad_tokens[None], *dw)


def solution(mesh):
    ctx = ("x", "y", "core")
    fine = Mesh(
        np.asarray(mesh.devices).reshape(2, 4, 2, 2, 4), ("dp", "x", "y", "core", "tensor")
    )
    tok = P("dp", ctx, "tensor")
    col = P(None, "tensor")
    in_specs = (tok, P("dp"), col, col, P(), col, col, col, col, col, P(), col, tok)
    dw = P(("dp",) + ctx, "tensor")
    return jax.shard_map(
        local, mesh=fine, in_specs=in_specs, out_specs=(tok, tok, dw, dw, dw, dw), check_vma=False
    )
```

```python
import math

import jax
import jax.numpy as jnp
import numpy as np
from jax import lax
from jax.experimental import pallas as pl
from jax.experimental.pallas import tpu as pltpu
from jax.sharding import Mesh, PartitionSpec as P

F32 = jnp.float32
BF16 = jnp.bfloat16
NEG = float("-inf")
D = 2048
WL = 512
LC = 512
CL = 32
SEG = 512
HD = 128
NH = 2
HW = NH * HD
SCALE = 1.0 / math.sqrt(HD)
ROWS = CL + 16
VM = pltpu.VMEM
BIG = 63 * 2**20
SM = pltpu.SMEM
PIECE = 4 * CL


def dg(a, b, ca, cb):
    return lax.dot_general(a, b, (((ca,), (cb,)), ((), ())), preferred_element_type=F32)


class Place:
    def __init__(self):
        self.x, self.y, self.core = (lax.axis_index(a) for a in ("x", "y", "core"))
        self.dp, self.z = lax.axis_index("dp"), lax.axis_index("tensor")
        self.ctx = (self.x * 2 + self.y) * 2 + self.core


def in_three(a):
    hi = a.astype(BF16).astype(F32)
    lo = (a - hi).astype(BF16).astype(F32)
    return hi, lo, (a - hi - lo).astype(BF16).astype(F32)


def tap_weights(first, second):
    taps = jnp.concatenate([second[a : a + 1] * first for a in range(4)], axis=0)
    return jnp.concatenate([taps[15:16], taps[:15]], axis=0)


def byte_mask(ctx, doc_len):
    pos = ctx * SEG + 16 * lax.broadcasted_iota(jnp.int32, (CL, 16, WL), 0)
    pos = pos + lax.broadcasted_iota(jnp.int32, (CL, 16, WL), 1)
    return (pos < doc_len).astype(F32)


def before_kernel(
    lens, tokens_h, grad_h, first_h, second_h, up_h, gain_h, piece, row, last, gain,
    tokens, grad_out, first, second, up_gain, shift, sems,
):
    pairs = ((tokens_h, tokens), (first_h, first), (second_h, second), (grad_h, grad_out), (up_h, up_gain), (gain_h, gain))
    copies = [pltpu.make_async_copy(a, b, sems.at[i]) for i, (a, b) in enumerate(pairs)]
    for c in copies:
        c.start()
    mask = byte_mask(Place().ctx, lens[0])
    u = lax.broadcasted_iota(jnp.int32, (CL, 16, WL), 1)
    for c in copies[:3]:
        c.wait()
    taps = tap_weights(first[...], second[...])
    prod = tokens[...].astype(F32).reshape(CL, 16, WL) * mask * taps[None]
    own = jnp.sum(jnp.where(u == 0, prod, 0.0), axis=1)
    onward = jnp.sum(jnp.where(u == 0, 0.0, prod), axis=1)
    shift[0:8] = jnp.zeros((8, WL), F32)
    shift[8 : 8 + CL] = onward
    part = own + shift[7 : 7 + CL]
    piece[0:CL] = part.astype(BF16)
    row[...] = jnp.broadcast_to(part[0:1], (8, WL))
    piece[64:80] = jnp.concatenate(list(in_three(part[0:1])) + [jnp.zeros((13, WL), F32)], axis=0).astype(BF16)
    last[...] = jnp.broadcast_to(shift[7 + CL : 8 + CL], (8, WL))
    for c in copies[3:]:
        c.wait()
    weighted = grad_out[...].astype(F32).reshape(CL, 16, WL) * mask * up_gain[...][None]
    piece[CL : 2 * CL] = jnp.sum(weighted, axis=1).astype(BF16)


def pile_kernel(piece, row, across, rim, rim_across, out):
    y = Place().y
    first = lax.broadcasted_iota(jnp.int32, (16, WL), 0) == 0
    sent = across[64:80].astype(F32)
    theirs = sent[0:1] + sent[1:2] + sent[2:3] + rim_across[0:1]
    for src, at, top in ((piece, y * 64, row[0:1] + rim[0:1]), (across, 64 - y * 64, theirs)):
        head = jnp.where(first, top, src[0:16].astype(F32))
        out[pl.ds(pl.multiple_of(at, 64), 16)] = head.astype(BF16)
        out[pl.ds(pl.multiple_of(at + 16, 16), 48)] = src[16:64]


def bias_kernel(near, table, strip):
    core = Place().core
    n = near.shape[1]
    which = near[0:1]
    for h in range(NH):
        row = jnp.full((1, n), NEG, F32)
        for b in range(table.shape[0]):
            row = jnp.where(which == b, table[b, core * NH + h], row)
        rolled = pltpu.roll(jnp.broadcast_to(row, (128, n)), 0, 1, stride=1, stride_axis=0)
        strip[h] = rolled[:, :LC]


def project_kernel(
    p0, r1, r2, r3, gain, wq, wk, wv, wo, keep, send, blocks, mine, craw, nrm, gco, both
):
    at = Place()
    z, core, x, y = at.z, at.core, at.x, at.y
    for s, src in enumerate((p0, r1, r2, r3)):
        cols = pl.ds(pl.multiple_of(lax.rem(z + 4 - s, 4) * WL, WL), WL)
        for i in range(2):
            rows = slice(i * CL, i * CL + CL)
            craw[rows, cols] = src[2 * i * CL : 2 * i * CL + CL]
            gco[rows, cols] = src[2 * i * CL + CL : 2 * i * CL + 2 * CL]
    mine[...] = craw[pl.ds(pl.multiple_of(y * CL, CL), CL)]
    c = craw[...].astype(F32)
    r = lax.rsqrt(jnp.sum(c * c, axis=1, keepdims=True) * (1.0 / D) + 1e-6)
    nrm[...] = (c * r * gain[...]).astype(BF16)
    for src, w, slot in ((gco, wo, 3), (nrm, wq, 0), (nrm, wk, 1), (nrm, wv, 2)):
        v = jnp.dot(src[...], w[...], preferred_element_type=F32).astype(BF16)
        for half in range(2):
            both[half, :, slot * HW : slot * HW + HW] = v[:, half * HW : half * HW + HW]
    keep[...] = both[core]
    send[0:64] = both[1 - core]
    tops = [c[i * CL : i * CL + 1, j * 1024 : j * 1024 + 1024] for i in range(2) for j in range(2)]
    send[64:80] = jnp.concatenate(tops + [jnp.zeros((12, 1024), F32)], axis=0).astype(BF16)
    for s in range(4):
        for d in range(2):
            chip = lax.rem(x + s, 4) * 2 + y
            cols = pl.ds(pl.multiple_of((d * 8 + chip) * 128, 128), 128)
            for i in range(2):
                rows = slice(i * CL, i * CL + CL)
                at = i * 512 + d * 128
                blocks[s, :, at : at + 128] = nrm[rows, cols]
                blocks[s, :, at + 256 : at + 384] = gco[rows, cols]


def pack_far_kernel(keep, swapped, blocks, up, down):
    core = Place().core
    for i, out in ((0, up), (1, down)):
        for src, c in ((keep, core), (swapped, 1 - core)):
            out[pl.ds(pl.multiple_of(c * CL, CL), CL)] = src[i * CL : i * CL + CL]
    up[64:80] = blocks[2, 0:16]
    down[64:80] = blocks[2, 16:32]


def pack_near_kernel(keep, swapped, blocks, up, down, b0):
    core = Place().core
    for i, out in ((1, up), (0, down)):
        for src, c in ((keep, core), (swapped, 1 - core)):
            out[pl.ds(pl.multiple_of(32 + c * CL, CL), CL)] = src[i * CL : i * CL + CL]
    for i in range(2):
        for src, c in ((keep, core), (swapped, 1 - core)):
            row = pl.multiple_of(i * 64 + c * CL, CL)
            b0[pl.ds(row, CL)] = src[i * CL : i * CL + CL]
    up[0:32] = blocks[1]
    down[0:32] = blocks[3]
    down[96:112] = swapped[64:80]
    b0[128:160] = blocks[0]


def gather_kernel(b0, low_near, high_near, far_low, far_high, swapped, mine, nxt):
    mine[0] = b0[128:160]
    mine[1] = low_near[0:32]
    mine[2, 0:16] = far_low[64:80]
    mine[2, 16:32] = far_high[64:80]
    mine[3] = high_near[0:32]
    at = Place()
    wraps = jnp.logical_and(at.core == 1, at.y == 1)
    tops = jnp.where(wraps, high_near[96:112].astype(F32), swapped[64:80].astype(F32))
    upper = jnp.where(at.core == 0, at.y, 1 - at.y) == 1
    for j in range(2):
        row = jnp.where(upper, tops[2 + j : 3 + j], tops[j : j + 1])
        nxt[:, j * 1024 : j * 1024 + 1024] = jnp.broadcast_to(row, (16, 1024)).astype(BF16)


def attend_kernel(
    lens, b0, low_far, low_near, high_far, high_near, far_low, far_high, strip,
    res, keep, send, q, k, v, ga, score, dprob, sg, pb,
):
    at = Place()
    ctx, core, x, doc_len = at.ctx, at.core, at.x, lens[0]
    for src, first, n, s, row in (
        (b0, 0, 128, 0, 0),
        (low_far, 0, 64, 1, 0),
        (low_near, 32, 64, 1, 64),
        (far_low, 0, 64, 2, 0),
        (far_high, 0, 64, 2, 64),
        (high_near, 32, 64, 3, 0),
        (high_far, 0, 64, 3, 64),
    ):
        rows = pl.ds(pl.multiple_of(lax.rem(x + 4 - s, 4) * 128 + row, 64), n)
        for i, dst in enumerate((q, k, v, ga)):
            dst[rows] = src[first : first + n, i * HW : i * HW + HW]
    key_pos = lax.broadcasted_iota(jnp.int32, (1, LC), 1)
    key_mask = jnp.where(16 * key_pos < doc_len, 0.0, NEG)
    work = [(b, h, slice(h * HD, h * HD + HD)) for b in (3, 2, 1, 0) for h in range(NH)]
    for b, h, c in work:
        rows, n = slice(b * 128, b * 128 + 128), b * 128 + 128
        score[h, rows, 0:n] = dg(q[rows, c], k[0:n, c], 1, 1)
        dprob[h, rows, 0:n] = dg(ga[rows, c], v[0:n, c], 1, 1)
    for b, h, c in work:
        rows, n = slice(b * 128, b * 128 + 128), b * 128 + 128
        s = score[h, rows, 0:n] * SCALE + strip[h, :, LC - n :] + key_mask[:, :n]
        e = jnp.exp(s - jnp.max(s, axis=1, keepdims=True))
        p = e * (1.0 / jnp.sum(e, axis=1, keepdims=True))
        dp = dprob[h, rows, 0:n]
        dot = jnp.sum(p * dp, axis=1, keepdims=True)
        sg[h, rows, 0:n] = (p * (dp - dot)).astype(BF16)
        pb[h, rows, 0:n] = p.astype(BF16)
    for b, h, c in work:
        rows, n = slice(b * 128, b * 128 + 128), b * 128 + 128
        gq = jnp.dot(sg[h, rows, 0:n], k[0:n, c], preferred_element_type=F32)
        res[0, rows, c] = (gq * SCALE).astype(BF16)
        res[3, rows, c] = jnp.dot(pb[h, rows, 0:n], v[0:n, c], preferred_element_type=F32).astype(BF16)
        tail = slice(b * 128, LC)
        res[1, rows, c] = (dg(sg[h, tail, rows], q[tail, c], 0, 0) * SCALE).astype(BF16)
        res[2, rows, c] = dg(pb[h, tail, rows], ga[tail, c], 0, 0).astype(BF16)
    res[:, LC : LC + 16] = jnp.zeros((4, 16, HW), BF16)
    peer = ctx + 1 - 2 * core
    keep[...] = res[:, pl.ds(pl.multiple_of(ctx * CL, CL), ROWS)]
    send[...] = res[:, pl.ds(pl.multiple_of(peer * CL, CL), ROWS)]


def weights_kernel(res, mine, other, keep, send, nb, gb):
    at = Place()
    core, x, dp = at.core, at.x, at.dp
    for s in range(4):
        for src, c in ((mine, core), (other, 1 - core)):
            for i in range(2):
                row = (lax.rem(x + 4 - s, 4) * 4 + i * 2 + c) * CL
                rows = pl.ds(pl.multiple_of(row, CL), CL)
                nb[rows] = src[s, :, i * 512 : i * 512 + 256]
                gb[rows] = src[s, :, i * 512 + 256 : i * 512 + 512]
    for w in range(4):
        src = gb if w == 3 else nb
        for d, out in ((dp, keep), (1 - dp, send)):
            cols = pl.ds(pl.multiple_of(d * 128, 128), 128)
            out[w] = dg(src[:, cols], res[w, 0:LC], 0, 0).astype(out.dtype)


def sum_kernel(keep, got, r1, own, send):
    core = Place().core
    for w in range(4):
        for c, out in ((core, own), (1 - core, send)):
            rows = pl.ds(pl.multiple_of(c * 64, 64), 64)
            out[w] = (keep[w, rows] + got[w, rows].astype(F32)).astype(out.dtype)


def partial_kernel(
    keep_r, got_r, crow, nxt, after, gain, wq, wk, wv, wo, msg1, msg2, msg3, keep, cz, inv_out, g, c
):
    at = Place()
    z, core = at.z, at.core
    g[:, :, pl.ds(pl.multiple_of(core * HW, HW), HW)] = keep_r[...]
    g[:, :, pl.ds(pl.multiple_of((1 - core) * HW, HW), HW)] = got_r[...]
    c[0:CL] = crow[...]
    c[CL:ROWS] = nxt[...]
    cf = c[...].astype(F32)
    r = lax.rsqrt(jnp.sum(cf * cf, axis=1, keepdims=True) * (1.0 / D) + 1e-6)
    inv_out[...] = jnp.broadcast_to(r, (ROWS, 128))
    lane = lax.broadcasted_iota(jnp.int32, (ROWS, 128), 1)
    dots = jnp.zeros((ROWS, 1), F32)
    for shift, msg in ((1, msg1), (2, msg2), (3, msg3), (0, keep)):
        t = lax.rem(z + shift, 4)
        part = pl.ds(pl.multiple_of(t * WL, WL), WL)
        gn = dg(g[0], wq[part], 1, 1) + dg(g[1], wk[part], 1, 1) + dg(g[2], wv[part], 1, 1)
        cb = c[:, part]
        dots = dots + jnp.sum(gn * gain[0:1, part] * cb.astype(F32), axis=1, keepdims=True)
        msg[0:CL, 0:WL] = dg(g[3, 0:CL], wo[part], 1, 1).astype(msg.dtype)
        msg[CL : CL + ROWS, 0:WL] = gn.astype(msg.dtype)
        msg[0:CL, WL : WL + 128] = jnp.zeros((CL, 128), msg.dtype)
        if shift == 0:
            cz[...] = cb
    keep[CL : CL + ROWS, WL : WL + 128] = jnp.broadcast_to(dots, (ROWS, 128))
    hi = dots.astype(BF16)
    lo = (dots - hi.astype(F32)).astype(BF16)
    lo2 = (dots - hi.astype(F32) - lo.astype(F32)).astype(BF16)
    packed = jnp.where(lane == 0, hi.astype(F32), jnp.where(lane == 1, lo.astype(F32), lo2.astype(F32)))
    packed = jnp.where(lane < 3, packed, 0.0).astype(BF16)
    for msg in (msg1, msg2, msg3):
        msg[CL : CL + ROWS, WL : WL + 128] = packed


def total_kernel(own, other, o0, o1, o2, o3):
    core = Place().core
    for w, o in enumerate((o0, o1, o2, o3)):
        o[:, pl.ds(pl.multiple_of(core * HW, HW), HW)] = own[w]
        o[:, pl.ds(pl.multiple_of((1 - core) * HW, HW), HW)] = other[w].astype(F32)


def after_kernel(
    lens, keep, r1, r2, r3, cz, inv, gain, first, second, up_gain, update, grad, rows
):
    at = Place()
    ctx, doc_len, z = at.ctx, lens[0], at.z
    mask = byte_mask(ctx, doc_len)
    body = slice(0, WL)
    out = keep[0:CL, body]
    gn = keep[CL : CL + ROWS, body]
    dots = keep[CL : CL + ROWS, WL : WL + 1]
    for r in (r1, r2, r3):
        out = out + r[0:CL, body].astype(F32)
        gn = gn + r[CL : CL + ROWS, body].astype(F32)
        dots = dots + jnp.sum(r[CL : CL + ROWS, WL : WL + 128].astype(F32), axis=1, keepdims=True)
    update[...] = ((out[:, None, :] * up_gain[...][None]) * mask).reshape(SEG, WL).astype(BF16)
    i = inv[:, 0:1]
    gained = gn * gain[0:1, pl.ds(pl.multiple_of(z * WL, WL), WL)]
    full = i * gained - cz[...].astype(F32) * (i * i * i) * dots * (1.0 / D)
    exists = lax.broadcasted_iota(jnp.int32, (ROWS, WL), 0) + ctx * CL < LC
    rows[...] = jnp.where(exists, full, 0.0)
    taps = tap_weights(first[...], second[...])
    u = lax.broadcasted_iota(jnp.int32, (CL, 16, WL), 1)
    picked = jnp.where(u == 0, rows[0:CL][:, None, :], rows[1 : CL + 1][:, None, :])
    grad[...] = (picked * taps[None] * mask).reshape(SEG, WL).astype(BF16)


def call(kernel, outs, args, scratch=(), smem=(0,), flops=0, size=0, vmem=8 * 2**20, hbm=(), typed=True):
    def spec(i):
        return pl.BlockSpec(memory_space=SM if i in smem else pltpu.HBM if i in hbm else VM)

    return pl.pallas_call(
        kernel,
        out_shape=[pltpu.VMEM(s, d) if typed else jax.ShapeDtypeStruct(s, d) for s, d in outs],
        in_specs=[spec(i) for i in range(len(args))],
        out_specs=[pl.BlockSpec(memory_space=VM)] * len(outs),
        scratch_shapes=[pltpu.VMEM(*s) if isinstance(s, tuple) else s for s in scratch],
        compiler_params=pltpu.CompilerParams(vmem_limit_bytes=vmem),
        cost_estimate=pl.CostEstimate(flops=flops, bytes_accessed=size, transcendentals=0),
    )(*args)


def shifted(x, axis, steps):
    n = lax.axis_size(axis)
    return lax.ppermute(x, axis, [(i, (i + steps) % n) for i in range(n)])


def local(
    tokens, lengths, conv_first, conv_second, norm_gain, w_query, w_key, w_value, w_out,
    bias_table, buckets, up_gain, grad_out,
):
    weights = (w_query, w_key, w_value, w_out)
    piece, row, last, gain = call(
        before_kernel,
        [((80, WL), BF16), ((8, WL), F32), ((8, WL), F32), ((1, D), F32)],
        (lengths, tokens[0], grad_out[0], conv_first, conv_second, up_gain, norm_gain[None]),
        [
            ((SEG, WL), BF16), ((SEG, WL), BF16), ((4, WL), F32), ((4, WL), F32), ((16, WL), F32),
            ((CL + 8, WL), F32), pltpu.SemaphoreType.DMA((6,)),
        ],
        hbm=(1, 2, 3, 4, 5, 6),
        vmem=BIG,
    )
    line = ("x", "y", "core")
    rim = lax.ppermute(last, line, [(i, i + 1) for i in range(15)])
    over = [(i, ((i + 1) ^ 2)) for i in range(15)]
    across = shifted(piece, "y", 1)
    rim_across = lax.ppermute(last, line, over)
    (piece,) = call(
        pile_kernel,
        [((PIECE, WL), BF16)],
        (piece, row, across, rim, rim_across),
        smem=(),
        flops=6 * 10**9,
    )
    n = 640
    near = jnp.concatenate(
        [
            jnp.flip(buckets[:385]),
            jnp.full((n - LC,), bias_table.shape[0], jnp.int32),
            jnp.flip(buckets[385:]),
        ]
    )
    (strip,) = call(
        bias_kernel,
        [((NH, 128, LC), F32)],
        (jnp.broadcast_to(near[None], (8, n)), bias_table),
        smem=(1,),
    )
    pieces = [piece] + [shifted(piece, "tensor", s) for s in (1, 2, 3)]
    keep, send, blocks, crow = call(
        project_kernel,
        [((64, 4 * HW), BF16), ((80, 4 * HW), BF16), ((4, CL, 4 * HW), BF16), ((CL, D), BF16)],
        (*pieces, gain, *weights),
        [((2 * CL, D), BF16), ((2 * CL, D), BF16), ((2 * CL, D), BF16), ((2, 2 * CL, 4 * HW), BF16)],
        smem=(),
        flops=10**9,
    )
    swapped = shifted(send, "core", 1)
    up_far, down_far = call(
        pack_far_kernel, [((80, 4 * HW), BF16)] * 2, (keep, swapped, blocks), smem=()
    )
    up_near, down_near, b0 = call(
        pack_near_kernel,
        [((n, 4 * HW), BF16) for n in (96, 112, 160)],
        (keep, swapped, blocks),
        smem=(),
    )
    low_far, high_far = shifted(up_far, "x", 1), shifted(down_far, "x", -1)
    low_near, high_near = shifted(up_near, "x", 1), shifted(down_near, "x", -1)
    far_low, far_high = shifted(low_far, "x", 1), shifted(high_far, "x", -1)
    mine, nxt = call(
        gather_kernel,
        [((4, CL, 4 * HW), BF16), ((16, D), BF16)],
        (b0, low_near, high_near, far_low, far_high, swapped),
        smem=(),
    )
    other_rows = shifted(mine, "core", 1)
    res, keep_r, send_r = call(
        attend_kernel,
        [((4, LC + 16, HW), BF16), ((4, ROWS, HW), BF16), ((4, ROWS, HW), BF16)],
        (lengths, b0, low_far, low_near, high_far, high_near, far_low, far_high, strip),
        [((LC, HW), BF16)] * 4 + [((NH, LC, LC), F32)] * 2 + [((NH, LC, LC), BF16)] * 2,
        flops=6 * 10**9,
        vmem=16 * 2**20,
    )
    got_r = shifted(send_r, "core", 1)
    dw_keep, dw_send = call(
        weights_kernel,
        [((4, 128, HW), F32), ((4, 128, HW), BF16)],
        (res, mine, other_rows),
        [((LC, 256), BF16), ((LC, 256), BF16)],
        smem=(),
        flops=10**9,
    )
    dw_got = shifted(dw_send, "dp", 1)
    msg = (CL + ROWS, WL + 128)
    m1, m2, m3, own, cz, inv = call(
        partial_kernel,
        [(msg, BF16), (msg, BF16), (msg, BF16), (msg, F32), ((ROWS, WL), BF16), ((ROWS, 128), F32)],
        (keep_r, got_r, crow, nxt, dw_keep, gain, *weights),
        [((4, ROWS, WL), BF16), ((ROWS, D), BF16)],
        smem=(),
        flops=10**9,
    )
    r1, r2, r3 = shifted(m1, "tensor", 1), shifted(m2, "tensor", 2), shifted(m3, "tensor", 3)
    dw_own, dw_other = call(
        sum_kernel,
        [((4, 64, HW), F32), ((4, 64, HW), BF16)],
        (dw_keep, dw_got, r1),
        smem=(),
    )
    dw_other = shifted(dw_other, "core", 1)
    dw = call(
        total_kernel,
        [((64, WL), F32)] * 4,
        (dw_own, dw_other),
        smem=(),
        flops=6 * 10**9,
        typed=False,
    )
    update, grad_tokens = call(
        after_kernel,
        [((SEG, WL), BF16)] * 2,
        (lengths, own, r1, r2, r3, cz, inv, gain, conv_first, conv_second, up_gain),
        [((ROWS, WL), F32)],
        flops=2 * 10**10,
        typed=False,
    )
    return (update[None], grad_tokens[None], *dw)


def solution(mesh):
    ctx = ("x", "y", "core")
    fine = Mesh(
        np.asarray(mesh.devices).reshape(2, 4, 2, 2, 4), ("dp", "x", "y", "core", "tensor")
    )
    tok = P("dp", ctx, "tensor")
    col = P(None, "tensor")
    in_specs = (tok, P("dp"), col, col, P(), col, col, col, col, col, P(), col, tok)
    dw = P(("dp",) + ctx, "tensor")
    return jax.shard_map(
        local, mesh=fine, in_specs=in_specs, out_specs=(tok, tok, dw, dw, dw, dw), check_vma=False
    )
```

```python
import math

import jax
import jax.numpy as jnp
import numpy as np
from jax import lax
from jax.experimental import pallas as pl
from jax.experimental.pallas import tpu as pltpu
from jax.sharding import Mesh, PartitionSpec as P

F32 = jnp.float32
BF16 = jnp.bfloat16
NEG = float("-inf")
D = 2048
WL = 512
LC = 512
CL = 32
SEG = 512
HD = 128
NH = 2
HW = NH * HD
SCALE = 1.0 / math.sqrt(HD)
ROWS = CL + 16
VM = pltpu.VMEM
BIG = 63 * 2**20
SM = pltpu.SMEM
PIECE = 4 * CL


def dg(a, b, ca, cb):
    return lax.dot_general(a, b, (((ca,), (cb,)), ((), ())), preferred_element_type=F32)


class Place:
    def __init__(self):
        self.x, self.y, self.core = (lax.axis_index(a) for a in ("x", "y", "core"))
        self.dp, self.z = lax.axis_index("dp"), lax.axis_index("tensor")
        self.ctx = (self.x * 2 + self.y) * 2 + self.core


def tap_weights(first, second):
    taps = jnp.concatenate([second[a : a + 1] * first for a in range(4)], axis=0)
    return jnp.concatenate([taps[15:16], taps[:15]], axis=0)


def byte_mask(ctx, doc_len):
    pos = ctx * SEG + 16 * lax.broadcasted_iota(jnp.int32, (CL, 16, WL), 0)
    pos = pos + lax.broadcasted_iota(jnp.int32, (CL, 16, WL), 1)
    return (pos < doc_len).astype(F32)


def before_kernel(
    lens, tokens_h, grad_h, first_h, second_h, up_h, gain_h, part, last, gco, gain,
    tokens, grad_out, first, second, up_gain, shift, sems,
):
    pairs = ((tokens_h, tokens), (first_h, first), (second_h, second), (grad_h, grad_out), (up_h, up_gain), (gain_h, gain))
    copies = [pltpu.make_async_copy(a, b, sems.at[i]) for i, (a, b) in enumerate(pairs)]
    for c in copies:
        c.start()
    mask = byte_mask(Place().ctx, lens[0])
    u = lax.broadcasted_iota(jnp.int32, (CL, 16, WL), 1)
    for c in copies[:3]:
        c.wait()
    taps = tap_weights(first[...], second[...])
    prod = tokens[...].astype(F32).reshape(CL, 16, WL) * mask * taps[None]
    own = jnp.sum(jnp.where(u == 0, prod, 0.0), axis=1)
    onward = jnp.sum(jnp.where(u == 0, 0.0, prod), axis=1)
    shift[0:8] = jnp.zeros((8, WL), F32)
    shift[8 : 8 + CL] = onward
    part[...] = own + shift[7 : 7 + CL]
    last[...] = jnp.broadcast_to(shift[7 + CL : 8 + CL], (8, WL))
    for c in copies[3:]:
        c.wait()
    weighted = grad_out[...].astype(F32).reshape(CL, 16, WL) * mask * up_gain[...][None]
    gco[...] = jnp.sum(weighted, axis=1).astype(BF16)


def piece_kernel(part, gco, rim, piece):
    first = lax.broadcasted_iota(jnp.int32, (CL, WL), 0) == 0
    piece[0:CL] = (part[...] + jnp.where(first, rim[0:1], 0.0)).astype(BF16)
    piece[CL : 2 * CL] = gco[...]


def pile_kernel(piece, across, out):
    y = Place().y
    out[pl.ds(pl.multiple_of(y * 64, 64), 64)] = piece[...]
    out[pl.ds(pl.multiple_of(64 - y * 64, 64), 64)] = across[...]


def bias_kernel(near, table, strip):
    core = Place().core
    n = near.shape[1]
    which = near[0:1]
    for h in range(NH):
        row = jnp.full((1, n), NEG, F32)
        for b in range(table.shape[0]):
            row = jnp.where(which == b, table[b, core * NH + h], row)
        rolled = pltpu.roll(jnp.broadcast_to(row, (128, n)), 0, 1, stride=1, stride_axis=0)
        strip[h] = rolled[:, :LC]


def project_kernel(
    p0, r2, r1, r3, gain, wq, wk, wv, wo, keep, send, blocks, mine, craw, nrm, gco, both
):
    at = Place()
    z, core, x, y = at.z, at.core, at.x, at.y
    for s, src in enumerate((p0, r1, r2, r3)):
        cols = pl.ds(pl.multiple_of(lax.rem(z + 4 - s, 4) * WL, WL), WL)
        for i in range(2):
            rows = slice(i * CL, i * CL + CL)
            craw[rows, cols] = src[2 * i * CL : 2 * i * CL + CL]
            gco[rows, cols] = src[2 * i * CL + CL : 2 * i * CL + 2 * CL]
    mine[...] = craw[pl.ds(pl.multiple_of(y * CL, CL), CL)]
    c = craw[...].astype(F32)
    r = lax.rsqrt(jnp.sum(c * c, axis=1, keepdims=True) * (1.0 / D) + 1e-6)
    nrm[...] = (c * r * gain[...]).astype(BF16)
    for src, w, slot in ((gco, wo, 3), (nrm, wq, 0), (nrm, wk, 1), (nrm, wv, 2)):
        v = jnp.dot(src[...], w[...], preferred_element_type=F32).astype(BF16)
        for half in range(2):
            both[half, :, slot * HW : slot * HW + HW] = v[:, half * HW : half * HW + HW]
    keep[...] = both[core]
    send[0:64] = both[1 - core]
    tops = [c[i * CL : i * CL + 1, j * 1024 : j * 1024 + 1024] for i in range(2) for j in range(2)]
    send[64:80] = jnp.concatenate(tops + [jnp.zeros((12, 1024), F32)], axis=0).astype(BF16)
    for s in range(4):
        for d in range(2):
            chip = lax.rem(x + s, 4) * 2 + y
            cols = pl.ds(pl.multiple_of((d * 8 + chip) * 128, 128), 128)
            for i in range(2):
                rows = slice(i * CL, i * CL + CL)
                at = i * 512 + d * 128
                blocks[s, :, at : at + 128] = nrm[rows, cols]
                blocks[s, :, at + 256 : at + 384] = gco[rows, cols]


def pack_far_kernel(keep, swapped, blocks, up, down):
    core = Place().core
    for i, out in ((0, up), (1, down)):
        for src, c in ((keep, core), (swapped, 1 - core)):
            out[pl.ds(pl.multiple_of(c * CL, CL), CL)] = src[i * CL : i * CL + CL]
    up[64:80] = blocks[2, 0:16]
    down[64:80] = blocks[2, 16:32]


def pack_near_kernel(keep, swapped, blocks, up, down, b0):
    core = Place().core
    for i, out in ((1, up), (0, down)):
        for src, c in ((keep, core), (swapped, 1 - core)):
            out[pl.ds(pl.multiple_of(32 + c * CL, CL), CL)] = src[i * CL : i * CL + CL]
    for i in range(2):
        for src, c in ((keep, core), (swapped, 1 - core)):
            row = pl.multiple_of(i * 64 + c * CL, CL)
            b0[pl.ds(row, CL)] = src[i * CL : i * CL + CL]
    up[0:32] = blocks[1]
    down[0:32] = blocks[3]
    down[96:112] = swapped[64:80]
    b0[128:160] = blocks[0]


def gather_kernel(b0, low_near, high_near, far_low, far_high, swapped, mine, nxt):
    mine[0] = b0[128:160]
    mine[1] = low_near[0:32]
    mine[2, 0:16] = far_low[64:80]
    mine[2, 16:32] = far_high[64:80]
    mine[3] = high_near[0:32]
    at = Place()
    wraps = jnp.logical_and(at.core == 1, at.y == 1)
    tops = jnp.where(wraps, high_near[96:112].astype(F32), swapped[64:80].astype(F32))
    upper = jnp.where(at.core == 0, at.y, 1 - at.y) == 1
    for j in range(2):
        row = jnp.where(upper, tops[2 + j : 3 + j], tops[j : j + 1])
        nxt[:, j * 1024 : j * 1024 + 1024] = jnp.broadcast_to(row, (16, 1024)).astype(BF16)


def attend_kernel(
    lens, b0, low_far, low_near, high_far, high_near, far_low, far_high, strip,
    res, keep, send, q, k, v, ga, score, dprob, sg, pb,
):
    at = Place()
    ctx, core, x, doc_len = at.ctx, at.core, at.x, lens[0]
    for src, first, n, s, row in (
        (b0, 0, 128, 0, 0),
        (low_far, 0, 64, 1, 0),
        (low_near, 32, 64, 1, 64),
        (far_low, 0, 64, 2, 0),
        (far_high, 0, 64, 2, 64),
        (high_near, 32, 64, 3, 0),
        (high_far, 0, 64, 3, 64),
    ):
        rows = pl.ds(pl.multiple_of(lax.rem(x + 4 - s, 4) * 128 + row, 64), n)
        for i, dst in enumerate((q, k, v, ga)):
            dst[rows] = src[first : first + n, i * HW : i * HW + HW]
    key_pos = lax.broadcasted_iota(jnp.int32, (1, LC), 1)
    key_mask = jnp.where(16 * key_pos < doc_len, 0.0, NEG)
    work = [(b, h, slice(h * HD, h * HD + HD)) for b in (3, 2, 1, 0) for h in range(NH)]
    for b, h, c in work:
        rows, n = slice(b * 128, b * 128 + 128), b * 128 + 128
        score[h, rows, 0:n] = dg(q[rows, c], k[0:n, c], 1, 1)
        dprob[h, rows, 0:n] = dg(ga[rows, c], v[0:n, c], 1, 1)
    for b, h, c in work:
        rows, n = slice(b * 128, b * 128 + 128), b * 128 + 128
        s = score[h, rows, 0:n] * SCALE + strip[h, :, LC - n :] + key_mask[:, :n]
        e = jnp.exp(s - jnp.max(s, axis=1, keepdims=True))
        p = e * (1.0 / jnp.sum(e, axis=1, keepdims=True))
        dp = dprob[h, rows, 0:n]
        dot = jnp.sum(p * dp, axis=1, keepdims=True)
        sg[h, rows, 0:n] = (p * (dp - dot)).astype(BF16)
        pb[h, rows, 0:n] = p.astype(BF16)
    for b, h, c in work:
        rows, n = slice(b * 128, b * 128 + 128), b * 128 + 128
        gq = jnp.dot(sg[h, rows, 0:n], k[0:n, c], preferred_element_type=F32)
        res[0, rows, c] = (gq * SCALE).astype(BF16)
        res[3, rows, c] = jnp.dot(pb[h, rows, 0:n], v[0:n, c], preferred_element_type=F32).astype(BF16)
        tail = slice(b * 128, LC)
        res[1, rows, c] = (dg(sg[h, tail, rows], q[tail, c], 0, 0) * SCALE).astype(BF16)
        res[2, rows, c] = dg(pb[h, tail, rows], ga[tail, c], 0, 0).astype(BF16)
    res[:, LC : LC + 16] = jnp.zeros((4, 16, HW), BF16)
    peer = ctx + 1 - 2 * core
    keep[...] = res[:, pl.ds(pl.multiple_of(ctx * CL, CL), ROWS)]
    send[...] = res[:, pl.ds(pl.multiple_of(peer * CL, CL), ROWS)]


def weights_kernel(res, mine, other, keep, send, nb, gb):
    at = Place()
    core, x, dp = at.core, at.x, at.dp
    for s in range(4):
        for src, c in ((mine, core), (other, 1 - core)):
            for i in range(2):
                row = (lax.rem(x + 4 - s, 4) * 4 + i * 2 + c) * CL
                rows = pl.ds(pl.multiple_of(row, CL), CL)
                nb[rows] = src[s, :, i * 512 : i * 512 + 256]
                gb[rows] = src[s, :, i * 512 + 256 : i * 512 + 512]
    for w in range(4):
        src = gb if w == 3 else nb
        for d, out in ((dp, keep), (1 - dp, send)):
            cols = pl.ds(pl.multiple_of(d * 128, 128), 128)
            out[w] = dg(src[:, cols], res[w, 0:LC], 0, 0).astype(out.dtype)


def sum_kernel(keep, got, r2, own, send):
    core = Place().core
    for w in range(4):
        for c, out in ((core, own), (1 - core, send)):
            rows = pl.ds(pl.multiple_of(c * 64, 64), 64)
            out[w] = (keep[w, rows] + got[w, rows].astype(F32)).astype(out.dtype)


def partial_kernel(
    keep_r, got_r, crow, nxt, after, gain, wq, wk, wv, wo, msg1, msg2, msg3, keep, cz, inv_out, g, c
):
    at = Place()
    z, core = at.z, at.core
    g[:, :, pl.ds(pl.multiple_of(core * HW, HW), HW)] = keep_r[...]
    g[:, :, pl.ds(pl.multiple_of((1 - core) * HW, HW), HW)] = got_r[...]
    c[0:CL] = crow[...]
    c[CL:ROWS] = nxt[...]
    cf = c[...].astype(F32)
    r = lax.rsqrt(jnp.sum(cf * cf, axis=1, keepdims=True) * (1.0 / D) + 1e-6)
    inv_out[...] = jnp.broadcast_to(r, (ROWS, 128))
    lane = lax.broadcasted_iota(jnp.int32, (ROWS, 128), 1)
    dots = jnp.zeros((ROWS, 1), F32)
    for shift, msg in ((1, msg1), (2, msg2), (3, msg3), (0, keep)):
        t = lax.rem(z + shift, 4)
        part = pl.ds(pl.multiple_of(t * WL, WL), WL)
        gn = dg(g[0], wq[part], 1, 1) + dg(g[1], wk[part], 1, 1) + dg(g[2], wv[part], 1, 1)
        cb = c[:, part]
        dots = dots + jnp.sum(gn * gain[0:1, part] * cb.astype(F32), axis=1, keepdims=True)
        msg[0:CL, 0:WL] = dg(g[3, 0:CL], wo[part], 1, 1).astype(msg.dtype)
        msg[CL : CL + ROWS, 0:WL] = gn.astype(msg.dtype)
        msg[0:CL, WL : WL + 128] = jnp.zeros((CL, 128), msg.dtype)
        if shift == 0:
            cz[...] = cb
    keep[CL : CL + ROWS, WL : WL + 128] = jnp.broadcast_to(dots, (ROWS, 128))
    hi = dots.astype(BF16)
    lo = (dots - hi.astype(F32)).astype(BF16)
    lo2 = (dots - hi.astype(F32) - lo.astype(F32)).astype(BF16)
    packed = jnp.where(lane == 0, hi.astype(F32), jnp.where(lane == 1, lo.astype(F32), lo2.astype(F32)))
    packed = jnp.where(lane < 3, packed, 0.0).astype(BF16)
    for msg in (msg1, msg2, msg3):
        msg[CL : CL + ROWS, WL : WL + 128] = packed


def total_kernel(own, other, o0, o1, o2, o3):
    core = Place().core
    for w, o in enumerate((o0, o1, o2, o3)):
        o[:, pl.ds(pl.multiple_of(core * HW, HW), HW)] = own[w]
        o[:, pl.ds(pl.multiple_of((1 - core) * HW, HW), HW)] = other[w].astype(F32)


def after_kernel(
    lens, keep, r2, r1, r3, cz, inv, gain, first, second, up_gain, update, grad, rows
):
    at = Place()
    ctx, doc_len, z = at.ctx, lens[0], at.z
    mask = byte_mask(ctx, doc_len)
    body = slice(0, WL)
    out = keep[0:CL, body]
    gn = keep[CL : CL + ROWS, body]
    dots = keep[CL : CL + ROWS, WL : WL + 1]
    for r in (r1, r2, r3):
        out = out + r[0:CL, body].astype(F32)
        gn = gn + r[CL : CL + ROWS, body].astype(F32)
        dots = dots + jnp.sum(r[CL : CL + ROWS, WL : WL + 128].astype(F32), axis=1, keepdims=True)
    update[...] = ((out[:, None, :] * up_gain[...][None]) * mask).reshape(SEG, WL).astype(BF16)
    i = inv[:, 0:1]
    gained = gn * gain[0:1, pl.ds(pl.multiple_of(z * WL, WL), WL)]
    full = i * gained - cz[...].astype(F32) * (i * i * i) * dots * (1.0 / D)
    exists = lax.broadcasted_iota(jnp.int32, (ROWS, WL), 0) + ctx * CL < LC
    rows[...] = jnp.where(exists, full, 0.0)
    taps = tap_weights(first[...], second[...])
    u = lax.broadcasted_iota(jnp.int32, (CL, 16, WL), 1)
    picked = jnp.where(u == 0, rows[0:CL][:, None, :], rows[1 : CL + 1][:, None, :])
    grad[...] = (picked * taps[None] * mask).reshape(SEG, WL).astype(BF16)


def call(kernel, outs, args, scratch=(), smem=(0,), flops=0, size=0, vmem=8 * 2**20, hbm=(), typed=True):
    def spec(i):
        return pl.BlockSpec(memory_space=SM if i in smem else pltpu.HBM if i in hbm else VM)

    return pl.pallas_call(
        kernel,
        out_shape=[pltpu.VMEM(s, d) if typed else jax.ShapeDtypeStruct(s, d) for s, d in outs],
        in_specs=[spec(i) for i in range(len(args))],
        out_specs=[pl.BlockSpec(memory_space=VM)] * len(outs),
        scratch_shapes=[pltpu.VMEM(*s) if isinstance(s, tuple) else s for s in scratch],
        compiler_params=pltpu.CompilerParams(vmem_limit_bytes=vmem),
        cost_estimate=pl.CostEstimate(flops=flops, bytes_accessed=size, transcendentals=0),
    )(*args)


def shifted(x, axis, steps):
    n = lax.axis_size(axis)
    return lax.ppermute(x, axis, [(i, (i + steps) % n) for i in range(n)])


def local(
    tokens, lengths, conv_first, conv_second, norm_gain, w_query, w_key, w_value, w_out,
    bias_table, buckets, up_gain, grad_out,
):
    weights = (w_query, w_key, w_value, w_out)
    part, last, gco, gain = call(
        before_kernel,
        [((CL, WL), F32), ((8, WL), F32), ((CL, WL), BF16), ((1, D), F32)],
        (lengths, tokens[0], grad_out[0], conv_first, conv_second, up_gain, norm_gain[None]),
        [
            ((SEG, WL), BF16), ((SEG, WL), BF16), ((4, WL), F32), ((4, WL), F32), ((16, WL), F32),
            ((CL + 8, WL), F32), pltpu.SemaphoreType.DMA((6,)),
        ],
        hbm=(1, 2, 3, 4, 5, 6),
        vmem=BIG,
    )
    line = ("x", "y", "core")
    rim = lax.ppermute(last, line, [(i, i + 1) for i in range(15)])
    (piece,) = call(piece_kernel, [((2 * CL, WL), BF16)], (part, gco, rim), smem=())
    across = shifted(piece, "y", 1)
    (piece,) = call(
        pile_kernel,
        [((PIECE, WL), BF16)],
        (piece, across),
        smem=(),
        flops=6 * 10**9,
    )
    n = 640
    near = jnp.concatenate(
        [
            jnp.flip(buckets[:385]),
            jnp.full((n - LC,), bias_table.shape[0], jnp.int32),
            jnp.flip(buckets[385:]),
        ]
    )
    (strip,) = call(
        bias_kernel,
        [((NH, 128, LC), F32)],
        (jnp.broadcast_to(near[None], (8, n)), bias_table),
        smem=(1,),
    )
    far = shifted(piece, "tensor", 2)
    pieces = [piece, far, shifted(piece, "tensor", 1), shifted(piece, "tensor", 3)]
    keep, send, blocks, crow = call(
        project_kernel,
        [((64, 4 * HW), BF16), ((80, 4 * HW), BF16), ((4, CL, 4 * HW), BF16), ((CL, D), BF16)],
        (*pieces, gain, *weights),
        [((2 * CL, D), BF16), ((2 * CL, D), BF16), ((2 * CL, D), BF16), ((2, 2 * CL, 4 * HW), BF16)],
        smem=(),
        flops=10**9,
    )
    swapped = shifted(send, "core", 1)
    up_far, down_far = call(
        pack_far_kernel, [((80, 4 * HW), BF16)] * 2, (keep, swapped, blocks), smem=()
    )
    up_near, down_near, b0 = call(
        pack_near_kernel,
        [((n, 4 * HW), BF16) for n in (96, 112, 160)],
        (keep, swapped, blocks),
        smem=(),
    )
    low_far, high_far = shifted(up_far, "x", 1), shifted(down_far, "x", -1)
    low_near, high_near = shifted(up_near, "x", 1), shifted(down_near, "x", -1)
    far_low, far_high = shifted(low_far, "x", 1), shifted(high_far, "x", -1)
    mine, nxt = call(
        gather_kernel,
        [((4, CL, 4 * HW), BF16), ((16, D), BF16)],
        (b0, low_near, high_near, far_low, far_high, swapped),
        smem=(),
    )
    other_rows = shifted(mine, "core", 1)
    res, keep_r, send_r = call(
        attend_kernel,
        [((4, LC + 16, HW), BF16), ((4, ROWS, HW), BF16), ((4, ROWS, HW), BF16)],
        (lengths, b0, low_far, low_near, high_far, high_near, far_low, far_high, strip),
        [((LC, HW), BF16)] * 4 + [((NH, LC, LC), F32)] * 2 + [((NH, LC, LC), BF16)] * 2,
        flops=6 * 10**9,
        vmem=16 * 2**20,
    )
    got_r = shifted(send_r, "core", 1)
    dw_keep, dw_send = call(
        weights_kernel,
        [((4, 128, HW), F32), ((4, 128, HW), BF16)],
        (res, mine, other_rows),
        [((LC, 256), BF16), ((LC, 256), BF16)],
        smem=(),
        flops=10**9,
    )
    dw_got = shifted(dw_send, "dp", 1)
    msg = (CL + ROWS, WL + 128)
    m1, m2, m3, own, cz, inv = call(
        partial_kernel,
        [(msg, BF16), (msg, BF16), (msg, BF16), (msg, F32), ((ROWS, WL), BF16), ((ROWS, 128), F32)],
        (keep_r, got_r, crow, nxt, dw_keep, gain, *weights),
        [((4, ROWS, WL), BF16), ((ROWS, D), BF16)],
        smem=(),
        flops=10**9,
    )
    r2, r1, r3 = shifted(m2, "tensor", 2), shifted(m1, "tensor", 1), shifted(m3, "tensor", 3)
    dw_own, dw_other = call(
        sum_kernel,
        [((4, 64, HW), F32), ((4, 64, HW), BF16)],
        (dw_keep, dw_got, r2),
        smem=(),
    )
    dw_other = shifted(dw_other, "core", 1)
    dw = call(
        total_kernel,
        [((64, WL), F32)] * 4,
        (dw_own, dw_other),
        smem=(),
        flops=6 * 10**9,
        typed=False,
    )
    update, grad_tokens = call(
        after_kernel,
        [((SEG, WL), BF16)] * 2,
        (lengths, own, r2, r1, r3, cz, inv, gain, conv_first, conv_second, up_gain),
        [((ROWS, WL), F32)],
        flops=2 * 10**10,
        typed=False,
    )
    return (update[None], grad_tokens[None], *dw)


def solution(mesh):
    ctx = ("x", "y", "core")
    fine = Mesh(
        np.asarray(mesh.devices).reshape(2, 4, 2, 2, 4), ("dp", "x", "y", "core", "tensor")
    )
    tok = P("dp", ctx, "tensor")
    col = P(None, "tensor")
    in_specs = (tok, P("dp"), col, col, P(), col, col, col, col, col, P(), col, tok)
    dw = P(("dp",) + ctx, "tensor")
    return jax.shard_map(
        local, mesh=fine, in_specs=in_specs, out_specs=(tok, tok, dw, dw, dw, dw), check_vma=False
    )
```

```python
import math

import jax
import jax.numpy as jnp
import numpy as np
from jax import lax
from jax.experimental import pallas as pl
from jax.experimental.pallas import tpu as pltpu
from jax.sharding import Mesh, PartitionSpec as P

F32 = jnp.float32
BF16 = jnp.bfloat16
NEG = float("-inf")
D = 2048
WL = 512
LC = 512
CL = 32
SEG = 512
HD = 128
NH = 2
HW = NH * HD
SCALE = 1.0 / math.sqrt(HD)
ROWS = CL + 16
VM = pltpu.VMEM
BIG = 63 * 2**20
SM = pltpu.SMEM
PIECE = 4 * CL


def dg(a, b, ca, cb):
    return lax.dot_general(a, b, (((ca,), (cb,)), ((), ())), preferred_element_type=F32)


class Place:
    def __init__(self):
        self.x, self.y, self.core = (lax.axis_index(a) for a in ("x", "y", "core"))
        self.dp, self.z = lax.axis_index("dp"), lax.axis_index("tensor")
        self.ctx = (self.x * 2 + self.y) * 2 + self.core


def in_three(a):
    hi = a.astype(BF16).astype(F32)
    lo = (a - hi).astype(BF16).astype(F32)
    return hi, lo, (a - hi - lo).astype(BF16).astype(F32)


def tap_weights(first, second):
    taps = jnp.concatenate([second[a : a + 1] * first for a in range(4)], axis=0)
    return jnp.concatenate([taps[15:16], taps[:15]], axis=0)


def byte_mask(ctx, doc_len):
    pos = ctx * SEG + 16 * lax.broadcasted_iota(jnp.int32, (CL, 16, WL), 0)
    pos = pos + lax.broadcasted_iota(jnp.int32, (CL, 16, WL), 1)
    return (pos < doc_len).astype(F32)


def before_kernel(
    lens, tokens_h, grad_h, first_h, second_h, up_h, gain_h, piece, row, last, gain,
    tokens, grad_out, first, second, up_gain, shift, sems,
):
    pairs = ((tokens_h, tokens), (first_h, first), (second_h, second), (grad_h, grad_out), (up_h, up_gain), (gain_h, gain))
    copies = [pltpu.make_async_copy(a, b, sems.at[i]) for i, (a, b) in enumerate(pairs)]
    for c in copies:
        c.start()
    mask = byte_mask(Place().ctx, lens[0])
    u = lax.broadcasted_iota(jnp.int32, (CL, 16, WL), 1)
    for c in copies[:3]:
        c.wait()
    taps = tap_weights(first[...], second[...])
    prod = tokens[...].astype(F32).reshape(CL, 16, WL) * mask * taps[None]
    own = jnp.sum(jnp.where(u == 0, prod, 0.0), axis=1)
    onward = jnp.sum(jnp.where(u == 0, 0.0, prod), axis=1)
    shift[0:8] = jnp.zeros((8, WL), F32)
    shift[8 : 8 + CL] = onward
    part = own + shift[7 : 7 + CL]
    piece[0:CL] = part.astype(BF16)
    row[...] = jnp.broadcast_to(part[0:1], (8, WL))
    piece[64:80] = jnp.concatenate(list(in_three(part[0:1])) + [jnp.zeros((13, WL), F32)], axis=0).astype(BF16)
    last[...] = jnp.broadcast_to(shift[7 + CL : 8 + CL], (8, WL))
    for c in copies[3:]:
        c.wait()
    weighted = grad_out[...].astype(F32).reshape(CL, 16, WL) * mask * up_gain[...][None]
    piece[CL : 2 * CL] = jnp.sum(weighted, axis=1).astype(BF16)


def pile_kernel(piece, row, across, rim, rim_across, out):
    y = Place().y
    first = lax.broadcasted_iota(jnp.int32, (16, WL), 0) == 0
    sent = across[64:80].astype(F32)
    theirs = sent[0:1] + sent[1:2] + sent[2:3] + rim_across[0:1]
    for src, at, top in ((piece, y * 64, row[0:1] + rim[0:1]), (across, 64 - y * 64, theirs)):
        head = jnp.where(first, top, src[0:16].astype(F32))
        out[pl.ds(pl.multiple_of(at, 64), 16)] = head.astype(BF16)
        out[pl.ds(pl.multiple_of(at + 16, 16), 48)] = src[16:64]


def bias_kernel(near, table, strip):
    core = Place().core
    n = near.shape[1]
    which = near[0:1]
    for h in range(NH):
        row = jnp.full((1, n), NEG, F32)
        for b in range(table.shape[0]):
            row = jnp.where(which == b, table[b, core * NH + h], row)
        rolled = pltpu.roll(jnp.broadcast_to(row, (128, n)), 0, 1, stride=1, stride_axis=0)
        strip[h] = rolled[:, :LC]


def project_kernel(
    p0, r2, r1, r3, gain, wq, wk, wv, wo, keep, send, blocks, mine, craw, nrm, gco, both
):
    at = Place()
    z, core, x, y = at.z, at.core, at.x, at.y
    for s, src in enumerate((p0, r1, r2, r3)):
        cols = pl.ds(pl.multiple_of(lax.rem(z + 4 - s, 4) * WL, WL), WL)
        for i in range(2):
            rows = slice(i * CL, i * CL + CL)
            craw[rows, cols] = src[2 * i * CL : 2 * i * CL + CL]
            gco[rows, cols] = src[2 * i * CL + CL : 2 * i * CL + 2 * CL]
    mine[...] = craw[pl.ds(pl.multiple_of(y * CL, CL), CL)]
    c = craw[...].astype(F32)
    r = lax.rsqrt(jnp.sum(c * c, axis=1, keepdims=True) * (1.0 / D) + 1e-6)
    nrm[...] = (c * r * gain[...]).astype(BF16)
    for src, w, slot in ((gco, wo, 3), (nrm, wq, 0), (nrm, wk, 1), (nrm, wv, 2)):
        v = jnp.dot(src[...], w[...], preferred_element_type=F32).astype(BF16)
        for half in range(2):
            both[half, :, slot * HW : slot * HW + HW] = v[:, half * HW : half * HW + HW]
    keep[...] = both[core]
    send[0:64] = both[1 - core]
    tops = [c[i * CL : i * CL + 1, j * 1024 : j * 1024 + 1024] for i in range(2) for j in range(2)]
    send[64:80] = jnp.concatenate(tops + [jnp.zeros((12, 1024), F32)], axis=0).astype(BF16)
    for s in range(4):
        for d in range(2):
            chip = lax.rem(x + s, 4) * 2 + y
            cols = pl.ds(pl.multiple_of((d * 8 + chip) * 128, 128), 128)
            for i in range(2):
                rows = slice(i * CL, i * CL + CL)
                at = i * 512 + d * 128
                blocks[s, :, at : at + 128] = nrm[rows, cols]
                blocks[s, :, at + 256 : at + 384] = gco[rows, cols]


def pack_far_kernel(keep, swapped, blocks, up, down):
    core = Place().core
    for i, out in ((0, up), (1, down)):
        for src, c in ((keep, core), (swapped, 1 - core)):
            out[pl.ds(pl.multiple_of(c * CL, CL), CL)] = src[i * CL : i * CL + CL]
    up[64:80] = blocks[2, 0:16]
    down[64:80] = blocks[2, 16:32]


def pack_near_kernel(keep, swapped, blocks, up, down, b0):
    core = Place().core
    for i, out in ((1, up), (0, down)):
        for src, c in ((keep, core), (swapped, 1 - core)):
            out[pl.ds(pl.multiple_of(32 + c * CL, CL), CL)] = src[i * CL : i * CL + CL]
    for i in range(2):
        for src, c in ((keep, core), (swapped, 1 - core)):
            row = pl.multiple_of(i * 64 + c * CL, CL)
            b0[pl.ds(row, CL)] = src[i * CL : i * CL + CL]
    up[0:32] = blocks[1]
    down[0:32] = blocks[3]
    down[96:112] = swapped[64:80]
    b0[128:160] = blocks[0]


def gather_kernel(b0, low_near, high_near, far_low, far_high, swapped, mine, nxt):
    mine[0] = b0[128:160]
    mine[1] = low_near[0:32]
    mine[2, 0:16] = far_low[64:80]
    mine[2, 16:32] = far_high[64:80]
    mine[3] = high_near[0:32]
    at = Place()
    wraps = jnp.logical_and(at.core == 1, at.y == 1)
    tops = jnp.where(wraps, high_near[96:112].astype(F32), swapped[64:80].astype(F32))
    upper = jnp.where(at.core == 0, at.y, 1 - at.y) == 1
    for j in range(2):
        row = jnp.where(upper, tops[2 + j : 3 + j], tops[j : j + 1])
        nxt[:, j * 1024 : j * 1024 + 1024] = jnp.broadcast_to(row, (16, 1024)).astype(BF16)


def attend_kernel(
    lens, b0, low_far, low_near, high_far, high_near, far_low, far_high, strip,
    res, keep, send, q, k, v, ga, score, dprob, sg, pb,
):
    at = Place()
    ctx, core, x, doc_len = at.ctx, at.core, at.x, lens[0]
    for src, first, n, s, row in (
        (b0, 0, 128, 0, 0),
        (low_far, 0, 64, 1, 0),
        (low_near, 32, 64, 1, 64),
        (far_low, 0, 64, 2, 0),
        (far_high, 0, 64, 2, 64),
        (high_near, 32, 64, 3, 0),
        (high_far, 0, 64, 3, 64),
    ):
        rows = pl.ds(pl.multiple_of(lax.rem(x + 4 - s, 4) * 128 + row, 64), n)
        for i, dst in enumerate((q, k, v, ga)):
            dst[rows] = src[first : first + n, i * HW : i * HW + HW]
    key_pos = lax.broadcasted_iota(jnp.int32, (1, LC), 1)
    key_mask = jnp.where(16 * key_pos < doc_len, 0.0, NEG)
    work = [(b, h, slice(h * HD, h * HD + HD)) for b in (3, 2, 1, 0) for h in range(NH)]
    for b, h, c in work:
        rows, n = slice(b * 128, b * 128 + 128), b * 128 + 128
        score[h, rows, 0:n] = dg(q[rows, c], k[0:n, c], 1, 1)
        dprob[h, rows, 0:n] = dg(ga[rows, c], v[0:n, c], 1, 1)
    for b, h, c in work:
        rows, n = slice(b * 128, b * 128 + 128), b * 128 + 128
        s = score[h, rows, 0:n] * SCALE + strip[h, :, LC - n :] + key_mask[:, :n]
        e = jnp.exp(s - jnp.max(s, axis=1, keepdims=True))
        p = e * (1.0 / jnp.sum(e, axis=1, keepdims=True))
        dp = dprob[h, rows, 0:n]
        dot = jnp.sum(p * dp, axis=1, keepdims=True)
        sg[h, rows, 0:n] = (p * (dp - dot)).astype(BF16)
        pb[h, rows, 0:n] = p.astype(BF16)
    for b, h, c in work:
        rows, n = slice(b * 128, b * 128 + 128), b * 128 + 128
        gq = jnp.dot(sg[h, rows, 0:n], k[0:n, c], preferred_element_type=F32)
        res[0, rows, c] = (gq * SCALE).astype(BF16)
        res[3, rows, c] = jnp.dot(pb[h, rows, 0:n], v[0:n, c], preferred_element_type=F32).astype(BF16)
        tail = slice(b * 128, LC)
        res[1, rows, c] = (dg(sg[h, tail, rows], q[tail, c], 0, 0) * SCALE).astype(BF16)
        res[2, rows, c] = dg(pb[h, tail, rows], ga[tail, c], 0, 0).astype(BF16)
    res[:, LC : LC + 16] = jnp.zeros((4, 16, HW), BF16)
    peer = ctx + 1 - 2 * core
    keep[...] = res[:, pl.ds(pl.multiple_of(ctx * CL, CL), ROWS)]
    send[...] = res[:, pl.ds(pl.multiple_of(peer * CL, CL), ROWS)]


def weights_kernel(res, mine, other, send_r, keep, to_core, to_dp, to_both, nb, gb, tile):
    at = Place()
    core, x, dp = at.core, at.x, at.dp
    for s in range(4):
        for src, c in ((mine, core), (other, 1 - core)):
            for i in range(2):
                row = (lax.rem(x + 4 - s, 4) * 4 + i * 2 + c) * CL
                rows = pl.ds(pl.multiple_of(row, CL), CL)
                nb[rows] = src[s, :, i * 512 : i * 512 + 256]
                gb[rows] = src[s, :, i * 512 + 256 : i * 512 + 512]
    for w in range(4):
        src = gb if w == 3 else nb
        for d, a, b in ((dp, keep.at[w], to_core.at[w, ROWS:]), (1 - dp, to_dp.at[w], to_both.at[w])):
            cols = pl.ds(pl.multiple_of(d * 128, 128), 128)
            tile[...] = dg(src[:, cols], res[w, 0:LC], 0, 0)
            a[...] = tile[pl.ds(pl.multiple_of(core * 64, 64), 64)].astype(a.dtype)
            b[...] = tile[pl.ds(pl.multiple_of(64 - core * 64, 64), 64)].astype(BF16)
    to_core[:, 0:ROWS] = send_r[...]


def partial_kernel(
    keep_r, got_r, crow, nxt, after, gain, wq, wk, wv, wo, msg1, msg2, msg3, keep, cz, inv_out, g, c
):
    at = Place()
    z, core = at.z, at.core
    g[:, :, pl.ds(pl.multiple_of(core * HW, HW), HW)] = keep_r[...]
    g[:, :, pl.ds(pl.multiple_of((1 - core) * HW, HW), HW)] = got_r[:, 0:ROWS]
    c[0:CL] = crow[...]
    c[CL:ROWS] = nxt[...]
    cf = c[...].astype(F32)
    r = lax.rsqrt(jnp.sum(cf * cf, axis=1, keepdims=True) * (1.0 / D) + 1e-6)
    inv_out[...] = jnp.broadcast_to(r, (ROWS, 128))
    lane = lax.broadcasted_iota(jnp.int32, (ROWS, 128), 1)
    dots = jnp.zeros((ROWS, 1), F32)
    for shift, msg in ((1, msg1), (2, msg2), (3, msg3), (0, keep)):
        t = lax.rem(z + shift, 4)
        part = pl.ds(pl.multiple_of(t * WL, WL), WL)
        gn = dg(g[0], wq[part], 1, 1) + dg(g[1], wk[part], 1, 1) + dg(g[2], wv[part], 1, 1)
        cb = c[:, part]
        dots = dots + jnp.sum(gn * gain[0:1, part] * cb.astype(F32), axis=1, keepdims=True)
        msg[0:CL, 0:WL] = dg(g[3, 0:CL], wo[part], 1, 1).astype(msg.dtype)
        msg[CL : CL + ROWS, 0:WL] = gn.astype(msg.dtype)
        msg[0:CL, WL : WL + 128] = jnp.zeros((CL, 128), msg.dtype)
        if shift == 0:
            cz[...] = cb
    keep[CL : CL + ROWS, WL : WL + 128] = jnp.broadcast_to(dots, (ROWS, 128))
    hi = dots.astype(BF16)
    lo = (dots - hi.astype(F32)).astype(BF16)
    lo2 = (dots - hi.astype(F32) - lo.astype(F32)).astype(BF16)
    packed = jnp.where(lane == 0, hi.astype(F32), jnp.where(lane == 1, lo.astype(F32), lo2.astype(F32)))
    packed = jnp.where(lane < 3, packed, 0.0).astype(BF16)
    for msg in (msg1, msg2, msg3):
        msg[CL : CL + ROWS, WL : WL + 128] = packed


def total_kernel(keep, got, from_dp, from_both, after, o0, o1, o2, o3):
    core = Place().core
    for w, o in enumerate((o0, o1, o2, o3)):
        o[:, pl.ds(pl.multiple_of(core * HW, HW), HW)] = keep[w] + from_dp[w].astype(F32)
        there = got[w, ROWS:].astype(F32) + from_both[w].astype(F32)
        o[:, pl.ds(pl.multiple_of((1 - core) * HW, HW), HW)] = there


def after_kernel(
    lens, keep, r1, r2, r3, cz, inv, gain, first, second, up_gain, update, grad, rows
):
    at = Place()
    ctx, doc_len, z = at.ctx, lens[0], at.z
    mask = byte_mask(ctx, doc_len)
    body = slice(0, WL)
    out = keep[0:CL, body]
    gn = keep[CL : CL + ROWS, body]
    dots = keep[CL : CL + ROWS, WL : WL + 1]
    for r in (r1, r2, r3):
        out = out + r[0:CL, body].astype(F32)
        gn = gn + r[CL : CL + ROWS, body].astype(F32)
        dots = dots + jnp.sum(r[CL : CL + ROWS, WL : WL + 128].astype(F32), axis=1, keepdims=True)
    update[...] = ((out[:, None, :] * up_gain[...][None]) * mask).reshape(SEG, WL).astype(BF16)
    i = inv[:, 0:1]
    gained = gn * gain[0:1, pl.ds(pl.multiple_of(z * WL, WL), WL)]
    full = i * gained - cz[...].astype(F32) * (i * i * i) * dots * (1.0 / D)
    exists = lax.broadcasted_iota(jnp.int32, (ROWS, WL), 0) + ctx * CL < LC
    rows[...] = jnp.where(exists, full, 0.0)
    taps = tap_weights(first[...], second[...])
    u = lax.broadcasted_iota(jnp.int32, (CL, 16, WL), 1)
    picked = jnp.where(u == 0, rows[0:CL][:, None, :], rows[1 : CL + 1][:, None, :])
    grad[...] = (picked * taps[None] * mask).reshape(SEG, WL).astype(BF16)


def call(kernel, outs, args, scratch=(), smem=(0,), flops=0, size=0, vmem=8 * 2**20, hbm=(), typed=True):
    def spec(i):
        return pl.BlockSpec(memory_space=SM if i in smem else pltpu.HBM if i in hbm else VM)

    return pl.pallas_call(
        kernel,
        out_shape=[pltpu.VMEM(s, d) if typed else jax.ShapeDtypeStruct(s, d) for s, d in outs],
        in_specs=[spec(i) for i in range(len(args))],
        out_specs=[pl.BlockSpec(memory_space=VM)] * len(outs),
        scratch_shapes=[pltpu.VMEM(*s) if isinstance(s, tuple) else s for s in scratch],
        compiler_params=pltpu.CompilerParams(vmem_limit_bytes=vmem),
        cost_estimate=pl.CostEstimate(flops=flops, bytes_accessed=size, transcendentals=0),
    )(*args)


def shifted(x, axis, steps):
    n = lax.axis_size(axis)
    return lax.ppermute(x, axis, [(i, (i + steps) % n) for i in range(n)])


def local(
    tokens, lengths, conv_first, conv_second, norm_gain, w_query, w_key, w_value, w_out,
    bias_table, buckets, up_gain, grad_out,
):
    weights = (w_query, w_key, w_value, w_out)
    piece, row, last, gain = call(
        before_kernel,
        [((80, WL), BF16), ((8, WL), F32), ((8, WL), F32), ((1, D), F32)],
        (lengths, tokens[0], grad_out[0], conv_first, conv_second, up_gain, norm_gain[None]),
        [
            ((SEG, WL), BF16), ((SEG, WL), BF16), ((4, WL), F32), ((4, WL), F32), ((16, WL), F32),
            ((CL + 8, WL), F32), pltpu.SemaphoreType.DMA((6,)),
        ],
        hbm=(1, 2, 3, 4, 5, 6),
        vmem=BIG,
    )
    line = ("x", "y", "core")
    rim = lax.ppermute(last, line, [(i, i + 1) for i in range(15)])
    over = [(i, ((i + 1) ^ 2)) for i in range(15)]
    across = shifted(piece, "y", 1)
    rim_across = lax.ppermute(last, line, over)
    (piece,) = call(
        pile_kernel,
        [((PIECE, WL), BF16)],
        (piece, row, across, rim, rim_across),
        smem=(),
        flops=6 * 10**9,
    )
    n = 640
    near = jnp.concatenate(
        [
            jnp.flip(buckets[:385]),
            jnp.full((n - LC,), bias_table.shape[0], jnp.int32),
            jnp.flip(buckets[385:]),
        ]
    )
    (strip,) = call(
        bias_kernel,
        [((NH, 128, LC), F32)],
        (jnp.broadcast_to(near[None], (8, n)), bias_table),
        smem=(1,),
    )
    pieces = [piece] + [shifted(piece, "tensor", s) for s in (2, 1, 3)]
    keep, send, blocks, crow = call(
        project_kernel,
        [((64, 4 * HW), BF16), ((80, 4 * HW), BF16), ((4, CL, 4 * HW), BF16), ((CL, D), BF16)],
        (*pieces, gain, *weights),
        [((2 * CL, D), BF16), ((2 * CL, D), BF16), ((2 * CL, D), BF16), ((2, 2 * CL, 4 * HW), BF16)],
        smem=(),
        flops=10**9,
    )
    swapped = shifted(send, "core", 1)
    up_far, down_far = call(
        pack_far_kernel, [((80, 4 * HW), BF16)] * 2, (keep, swapped, blocks), smem=()
    )
    up_near, down_near, b0 = call(
        pack_near_kernel,
        [((n, 4 * HW), BF16) for n in (96, 112, 160)],
        (keep, swapped, blocks),
        smem=(),
    )
    low_far, high_far = shifted(up_far, "x", 1), shifted(down_far, "x", -1)
    low_near, high_near = shifted(up_near, "x", 1), shifted(down_near, "x", -1)
    far_low, far_high = shifted(low_far, "x", 1), shifted(high_far, "x", -1)
    mine, nxt = call(
        gather_kernel,
        [((4, CL, 4 * HW), BF16), ((16, D), BF16)],
        (b0, low_near, high_near, far_low, far_high, swapped),
        smem=(),
    )
    other_rows = shifted(mine, "core", 1)
    res, keep_r, send_r = call(
        attend_kernel,
        [((4, LC + 16, HW), BF16), ((4, ROWS, HW), BF16), ((4, ROWS, HW), BF16)],
        (lengths, b0, low_far, low_near, high_far, high_near, far_low, far_high, strip),
        [((LC, HW), BF16)] * 4 + [((NH, LC, LC), F32)] * 2 + [((NH, LC, LC), BF16)] * 2,
        flops=6 * 10**9,
        vmem=16 * 2**20,
    )
    dw_keep, to_core, to_dp, to_both = call(
        weights_kernel,
        [((4, 64, HW), F32), ((4, ROWS + 64, HW), BF16), ((4, 64, HW), BF16), ((4, 64, HW), BF16)],
        (res, mine, other_rows, send_r),
        [((LC, 256), BF16), ((LC, 256), BF16), ((128, HW), F32)],
        smem=(),
        flops=10**9,
    )
    got_r = shifted(to_core, "core", 1)
    from_dp = shifted(to_dp, "dp", 1)
    from_both = lax.ppermute(to_both, ("dp", "core"), [(i, 3 - i) for i in range(4)])
    msg = (CL + ROWS, WL + 128)
    m1, m2, m3, own, cz, inv = call(
        partial_kernel,
        [(msg, BF16), (msg, BF16), (msg, BF16), (msg, F32), ((ROWS, WL), BF16), ((ROWS, 128), F32)],
        (keep_r, got_r, crow, nxt, dw_keep, gain, *weights),
        [((4, ROWS, WL), BF16), ((ROWS, D), BF16)],
        smem=(),
        flops=10**9,
    )
    r1, r2, r3 = shifted(m1, "tensor", 1), shifted(m2, "tensor", 2), shifted(m3, "tensor", 3)
    dw = call(
        total_kernel,
        [((64, WL), F32)] * 4,
        (dw_keep, got_r, from_dp, from_both, r1),
        smem=(),
        flops=6 * 10**9,
        typed=False,
    )
    update, grad_tokens = call(
        after_kernel,
        [((SEG, WL), BF16)] * 2,
        (lengths, own, r1, r2, r3, cz, inv, gain, conv_first, conv_second, up_gain),
        [((ROWS, WL), F32)],
        flops=2 * 10**10,
        typed=False,
    )
    return (update[None], grad_tokens[None], *dw)


def solution(mesh):
    ctx = ("x", "y", "core")
    fine = Mesh(
        np.asarray(mesh.devices).reshape(2, 4, 2, 2, 4), ("dp", "x", "y", "core", "tensor")
    )
    tok = P("dp", ctx, "tensor")
    col = P(None, "tensor")
    in_specs = (tok, P("dp"), col, col, P(), col, col, col, col, col, P(), col, tok)
    dw = P(("dp",) + ctx, "tensor")
    return jax.shard_map(
        local, mesh=fine, in_specs=in_specs, out_specs=(tok, tok, dw, dw, dw, dw), check_vma=False
    )
```

```python
import math

import jax
import jax.numpy as jnp
import numpy as np
from jax import lax
from jax.experimental import pallas as pl
from jax.experimental.pallas import tpu as pltpu
from jax.sharding import Mesh, PartitionSpec as P

F32 = jnp.float32
BF16 = jnp.bfloat16
NEG = float("-inf")
D = 2048
WL = 512
LC = 512
CL = 32
SEG = 512
HD = 128
NH = 2
HW = NH * HD
SCALE = 1.0 / math.sqrt(HD)
ROWS = CL + 16
VM = pltpu.VMEM
BIG = 63 * 2**20
SM = pltpu.SMEM
PIECE = 4 * CL


def dg(a, b, ca, cb):
    return lax.dot_general(a, b, (((ca,), (cb,)), ((), ())), preferred_element_type=F32)


class Place:
    def __init__(self):
        self.x, self.y, self.core = (lax.axis_index(a) for a in ("x", "y", "core"))
        self.dp, self.z = lax.axis_index("dp"), lax.axis_index("tensor")
        self.ctx = (self.x * 2 + self.y) * 2 + self.core


def in_three(a):
    hi = a.astype(BF16).astype(F32)
    lo = (a - hi).astype(BF16).astype(F32)
    return hi, lo, (a - hi - lo).astype(BF16).astype(F32)


def tap_weights(first, second):
    taps = jnp.concatenate([second[a : a + 1] * first for a in range(4)], axis=0)
    return jnp.concatenate([taps[15:16], taps[:15]], axis=0)


def byte_mask(ctx, doc_len):
    pos = ctx * SEG + 16 * lax.broadcasted_iota(jnp.int32, (CL, 16, WL), 0)
    pos = pos + lax.broadcasted_iota(jnp.int32, (CL, 16, WL), 1)
    return (pos < doc_len[None]).astype(F32)


def before_kernel(
    lens_h, tokens_h, grad_h, first_h, second_h, up_h, gain_h, piece, row, last, gain, lens_out,
    tokens, grad_out, first, second, up_gain, lens, shift, sems,
):
    pairs = (
        (lens_h, lens), (tokens_h, tokens), (first_h, first), (second_h, second),
        (grad_h, grad_out), (up_h, up_gain), (gain_h, gain),
    )
    copies = [pltpu.make_async_copy(a, b, sems.at[i]) for i, (a, b) in enumerate(pairs)]
    for c in copies:
        c.start()
    u = lax.broadcasted_iota(jnp.int32, (CL, 16, WL), 1)
    for c in copies[:4]:
        c.wait()
    lens_out[...] = jnp.broadcast_to(lens[...], (8, 128))
    mask = byte_mask(Place().ctx, lens[...])
    taps = tap_weights(first[...], second[...])
    prod = tokens[...].astype(F32).reshape(CL, 16, WL) * mask * taps[None]
    own = jnp.sum(jnp.where(u == 0, prod, 0.0), axis=1)
    onward = jnp.sum(jnp.where(u == 0, 0.0, prod), axis=1)
    shift[0:8] = jnp.zeros((8, WL), F32)
    shift[8 : 8 + CL] = onward
    part = own + shift[7 : 7 + CL]
    piece[0:CL] = part.astype(BF16)
    row[...] = jnp.broadcast_to(part[0:1], (8, WL))
    piece[64:80] = jnp.concatenate(list(in_three(part[0:1])) + [jnp.zeros((13, WL), F32)], axis=0).astype(BF16)
    last[...] = jnp.broadcast_to(shift[7 + CL : 8 + CL], (8, WL))
    for c in copies[4:]:
        c.wait()
    weighted = grad_out[...].astype(F32).reshape(CL, 16, WL) * mask * up_gain[...][None]
    piece[CL : 2 * CL] = jnp.sum(weighted, axis=1).astype(BF16)


def pile_kernel(piece, row, across, rim, rim_across, out):
    y = Place().y
    first = lax.broadcasted_iota(jnp.int32, (16, WL), 0) == 0
    sent = across[64:80].astype(F32)
    theirs = sent[0:1] + sent[1:2] + sent[2:3] + rim_across[0:1]
    for src, at, top in ((piece, y * 64, row[0:1] + rim[0:1]), (across, 64 - y * 64, theirs)):
        head = jnp.where(first, top, src[0:16].astype(F32))
        out[pl.ds(pl.multiple_of(at, 64), 16)] = head.astype(BF16)
        out[pl.ds(pl.multiple_of(at + 16, 16), 48)] = src[16:64]


def bias_kernel(near, table, strip):
    core = Place().core
    n = near.shape[1]
    which = near[0:1]
    for h in range(NH):
        row = jnp.full((1, n), NEG, F32)
        for b in range(table.shape[0]):
            row = jnp.where(which == b, table[b, core * NH + h], row)
        rolled = pltpu.roll(jnp.broadcast_to(row, (128, n)), 0, 1, stride=1, stride_axis=0)
        strip[h] = rolled[:, :LC]


def project_kernel(
    p0, r2, r1, r3, gain, wq, wk, wv, wo, keep, send, blocks, mine, craw, nrm, gco, both
):
    at = Place()
    z, core, x, y = at.z, at.core, at.x, at.y
    for s, src in enumerate((p0, r1, r2, r3)):
        cols = pl.ds(pl.multiple_of(lax.rem(z + 4 - s, 4) * WL, WL), WL)
        for i in range(2):
            rows = slice(i * CL, i * CL + CL)
            craw[rows, cols] = src[2 * i * CL : 2 * i * CL + CL]
            gco[rows, cols] = src[2 * i * CL + CL : 2 * i * CL + 2 * CL]
    mine[...] = craw[pl.ds(pl.multiple_of(y * CL, CL), CL)]
    c = craw[...].astype(F32)
    r = lax.rsqrt(jnp.sum(c * c, axis=1, keepdims=True) * (1.0 / D) + 1e-6)
    nrm[...] = (c * r * gain[...]).astype(BF16)
    for src, w, slot in ((gco, wo, 3), (nrm, wq, 0), (nrm, wk, 1), (nrm, wv, 2)):
        v = jnp.dot(src[...], w[...], preferred_element_type=F32).astype(BF16)
        for half in range(2):
            both[half, :, slot * HW : slot * HW + HW] = v[:, half * HW : half * HW + HW]
    keep[...] = both[core]
    send[0:64] = both[1 - core]
    tops = [c[i * CL : i * CL + 1, j * 1024 : j * 1024 + 1024] for i in range(2) for j in range(2)]
    send[64:80] = jnp.concatenate(tops + [jnp.zeros((12, 1024), F32)], axis=0).astype(BF16)
    for s in range(4):
        for d in range(2):
            chip = lax.rem(x + s, 4) * 2 + y
            cols = pl.ds(pl.multiple_of((d * 8 + chip) * 128, 128), 128)
            for i in range(2):
                rows = slice(i * CL, i * CL + CL)
                at = i * 512 + d * 128
                blocks[s, :, at : at + 128] = nrm[rows, cols]
                blocks[s, :, at + 256 : at + 384] = gco[rows, cols]


def pack_far_kernel(keep, swapped, blocks, up, down):
    core = Place().core
    for i, out in ((0, up), (1, down)):
        for src, c in ((keep, core), (swapped, 1 - core)):
            out[pl.ds(pl.multiple_of(c * CL, CL), CL)] = src[i * CL : i * CL + CL]
    up[64:80] = blocks[2, 0:16]
    down[64:80] = blocks[2, 16:32]


def pack_near_kernel(keep, swapped, blocks, up, down, b0):
    core = Place().core
    for i, out in ((1, up), (0, down)):
        for src, c in ((keep, core), (swapped, 1 - core)):
            out[pl.ds(pl.multiple_of(32 + c * CL, CL), CL)] = src[i * CL : i * CL + CL]
    for i in range(2):
        for src, c in ((keep, core), (swapped, 1 - core)):
            row = pl.multiple_of(i * 64 + c * CL, CL)
            b0[pl.ds(row, CL)] = src[i * CL : i * CL + CL]
    up[0:32] = blocks[1]
    down[0:32] = blocks[3]
    down[96:112] = swapped[64:80]
    b0[128:160] = blocks[0]


def gather_kernel(b0, low_near, high_near, far_low, far_high, swapped, mine, nxt):
    mine[0] = b0[128:160]
    mine[1] = low_near[0:32]
    mine[2, 0:16] = far_low[64:80]
    mine[2, 16:32] = far_high[64:80]
    mine[3] = high_near[0:32]
    at = Place()
    wraps = jnp.logical_and(at.core == 1, at.y == 1)
    tops = jnp.where(wraps, high_near[96:112].astype(F32), swapped[64:80].astype(F32))
    upper = jnp.where(at.core == 0, at.y, 1 - at.y) == 1
    for j in range(2):
        row = jnp.where(upper, tops[2 + j : 3 + j], tops[j : j + 1])
        nxt[:, j * 1024 : j * 1024 + 1024] = jnp.broadcast_to(row, (16, 1024)).astype(BF16)


def attend_kernel(
    lens, b0, low_far, low_near, high_far, high_near, far_low, far_high, strip,
    res, keep, send, q, k, v, ga, score, dprob, sg, pb,
):
    at = Place()
    ctx, core, x, doc_len = at.ctx, at.core, at.x, lens[0:1, 0:1]
    for src, first, n, s, row in (
        (b0, 0, 128, 0, 0),
        (low_far, 0, 64, 1, 0),
        (low_near, 32, 64, 1, 64),
        (far_low, 0, 64, 2, 0),
        (far_high, 0, 64, 2, 64),
        (high_near, 32, 64, 3, 0),
        (high_far, 0, 64, 3, 64),
    ):
        rows = pl.ds(pl.multiple_of(lax.rem(x + 4 - s, 4) * 128 + row, 64), n)
        for i, dst in enumerate((q, k, v, ga)):
            dst[rows] = src[first : first + n, i * HW : i * HW + HW]
    key_pos = lax.broadcasted_iota(jnp.int32, (1, LC), 1)
    key_mask = jnp.where(16 * key_pos < doc_len, 0.0, NEG)
    work = [(b, h, slice(h * HD, h * HD + HD)) for b in (3, 2, 1, 0) for h in range(NH)]
    for b, h, c in work:
        rows, n = slice(b * 128, b * 128 + 128), b * 128 + 128
        score[h, rows, 0:n] = dg(q[rows, c], k[0:n, c], 1, 1)
        dprob[h, rows, 0:n] = dg(ga[rows, c], v[0:n, c], 1, 1)
    for b, h, c in work:
        rows, n = slice(b * 128, b * 128 + 128), b * 128 + 128
        s = score[h, rows, 0:n] * SCALE + strip[h, :, LC - n :] + key_mask[:, :n]
        e = jnp.exp(s - jnp.max(s, axis=1, keepdims=True))
        p = e * (1.0 / jnp.sum(e, axis=1, keepdims=True))
        dp = dprob[h, rows, 0:n]
        dot = jnp.sum(p * dp, axis=1, keepdims=True)
        sg[h, rows, 0:n] = (p * (dp - dot)).astype(BF16)
        pb[h, rows, 0:n] = p.astype(BF16)
    for b, h, c in work:
        rows, n = slice(b * 128, b * 128 + 128), b * 128 + 128
        gq = jnp.dot(sg[h, rows, 0:n], k[0:n, c], preferred_element_type=F32)
        res[0, rows, c] = (gq * SCALE).astype(BF16)
        res[3, rows, c] = jnp.dot(pb[h, rows, 0:n], v[0:n, c], preferred_element_type=F32).astype(BF16)
        tail = slice(b * 128, LC)
        res[1, rows, c] = (dg(sg[h, tail, rows], q[tail, c], 0, 0) * SCALE).astype(BF16)
        res[2, rows, c] = dg(pb[h, tail, rows], ga[tail, c], 0, 0).astype(BF16)
    res[:, LC : LC + 16] = jnp.zeros((4, 16, HW), BF16)
    peer = ctx + 1 - 2 * core
    keep[...] = res[:, pl.ds(pl.multiple_of(ctx * CL, CL), ROWS)]
    send[...] = res[:, pl.ds(pl.multiple_of(peer * CL, CL), ROWS)]


def weights_kernel(res, mine, other, keep, send, nb, gb):
    at = Place()
    core, x, dp = at.core, at.x, at.dp
    for s in range(4):
        for src, c in ((mine, core), (other, 1 - core)):
            for i in range(2):
                row = (lax.rem(x + 4 - s, 4) * 4 + i * 2 + c) * CL
                rows = pl.ds(pl.multiple_of(row, CL), CL)
                nb[rows] = src[s, :, i * 512 : i * 512 + 256]
                gb[rows] = src[s, :, i * 512 + 256 : i * 512 + 512]
    for w in range(4):
        src = gb if w == 3 else nb
        for d, out in ((dp, keep), (1 - dp, send)):
            cols = pl.ds(pl.multiple_of(d * 128, 128), 128)
            out[w] = dg(src[:, cols], res[w, 0:LC], 0, 0).astype(out.dtype)


def sum_kernel(keep, got, r1, own, send):
    core = Place().core
    for w in range(4):
        for c, out in ((core, own), (1 - core, send)):
            rows = pl.ds(pl.multiple_of(c * 64, 64), 64)
            out[w] = (keep[w, rows] + got[w, rows].astype(F32)).astype(out.dtype)


def partial_kernel(
    keep_r, got_r, crow, nxt, after, gain, wq, wk, wv, wo, msg1, msg2, msg3, keep, cz, inv_out, g, c
):
    at = Place()
    z, core = at.z, at.core
    g[:, :, pl.ds(pl.multiple_of(core * HW, HW), HW)] = keep_r[...]
    g[:, :, pl.ds(pl.multiple_of((1 - core) * HW, HW), HW)] = got_r[...]
    c[0:CL] = crow[...]
    c[CL:ROWS] = nxt[...]
    cf = c[...].astype(F32)
    r = lax.rsqrt(jnp.sum(cf * cf, axis=1, keepdims=True) * (1.0 / D) + 1e-6)
    inv_out[...] = jnp.broadcast_to(r, (ROWS, 128))
    lane = lax.broadcasted_iota(jnp.int32, (ROWS, 128), 1)
    dots = jnp.zeros((ROWS, 1), F32)
    for shift, msg in ((1, msg1), (2, msg2), (3, msg3), (0, keep)):
        t = lax.rem(z + shift, 4)
        part = pl.ds(pl.multiple_of(t * WL, WL), WL)
        gn = dg(g[0], wq[part], 1, 1) + dg(g[1], wk[part], 1, 1) + dg(g[2], wv[part], 1, 1)
        cb = c[:, part]
        dots = dots + jnp.sum(gn * gain[0:1, part] * cb.astype(F32), axis=1, keepdims=True)
        msg[0:CL, 0:WL] = dg(g[3, 0:CL], wo[part], 1, 1).astype(msg.dtype)
        msg[CL : CL + ROWS, 0:WL] = gn.astype(msg.dtype)
        msg[0:CL, WL : WL + 128] = jnp.zeros((CL, 128), msg.dtype)
        if shift == 0:
            cz[...] = cb
    keep[CL : CL + ROWS, WL : WL + 128] = jnp.broadcast_to(dots, (ROWS, 128))
    hi = dots.astype(BF16)
    lo = (dots - hi.astype(F32)).astype(BF16)
    lo2 = (dots - hi.astype(F32) - lo.astype(F32)).astype(BF16)
    packed = jnp.where(lane == 0, hi.astype(F32), jnp.where(lane == 1, lo.astype(F32), lo2.astype(F32)))
    packed = jnp.where(lane < 3, packed, 0.0).astype(BF16)
    for msg in (msg1, msg2, msg3):
        msg[CL : CL + ROWS, WL : WL + 128] = packed


def total_kernel(own, other, o0, o1, o2, o3):
    core = Place().core
    for w, o in enumerate((o0, o1, o2, o3)):
        o[:, pl.ds(pl.multiple_of(core * HW, HW), HW)] = own[w]
        o[:, pl.ds(pl.multiple_of((1 - core) * HW, HW), HW)] = other[w].astype(F32)


def after_kernel(
    lens, keep, r1, r2, r3, cz, inv, gain, first, second, up_gain, update, grad, rows
):
    at = Place()
    ctx, doc_len, z = at.ctx, lens[0:1, 0:1], at.z
    mask = byte_mask(ctx, doc_len)
    body = slice(0, WL)
    out = keep[0:CL, body]
    gn = keep[CL : CL + ROWS, body]
    dots = keep[CL : CL + ROWS, WL : WL + 1]
    for r in (r1, r2, r3):
        out = out + r[0:CL, body].astype(F32)
        gn = gn + r[CL : CL + ROWS, body].astype(F32)
        dots = dots + jnp.sum(r[CL : CL + ROWS, WL : WL + 128].astype(F32), axis=1, keepdims=True)
    update[...] = ((out[:, None, :] * up_gain[...][None]) * mask).reshape(SEG, WL).astype(BF16)
    i = inv[:, 0:1]
    gained = gn * gain[0:1, pl.ds(pl.multiple_of(z * WL, WL), WL)]
    full = i * gained - cz[...].astype(F32) * (i * i * i) * dots * (1.0 / D)
    exists = lax.broadcasted_iota(jnp.int32, (ROWS, WL), 0) + ctx * CL < LC
    rows[...] = jnp.where(exists, full, 0.0)
    taps = tap_weights(first[...], second[...])
    u = lax.broadcasted_iota(jnp.int32, (CL, 16, WL), 1)
    picked = jnp.where(u == 0, rows[0:CL][:, None, :], rows[1 : CL + 1][:, None, :])
    grad[...] = (picked * taps[None] * mask).reshape(SEG, WL).astype(BF16)


def call(kernel, outs, args, scratch=(), smem=(0,), flops=0, size=0, vmem=8 * 2**20, hbm=(), typed=True):
    def spec(i):
        return pl.BlockSpec(memory_space=SM if i in smem else pltpu.HBM if i in hbm else VM)

    return pl.pallas_call(
        kernel,
        out_shape=[pltpu.VMEM(s, d) if typed else jax.ShapeDtypeStruct(s, d) for s, d in outs],
        in_specs=[spec(i) for i in range(len(args))],
        out_specs=[pl.BlockSpec(memory_space=VM)] * len(outs),
        scratch_shapes=[pltpu.VMEM(*s) if isinstance(s, tuple) else s for s in scratch],
        compiler_params=pltpu.CompilerParams(vmem_limit_bytes=vmem),
        cost_estimate=pl.CostEstimate(flops=flops, bytes_accessed=size, transcendentals=0),
    )(*args)


def shifted(x, axis, steps):
    n = lax.axis_size(axis)
    return lax.ppermute(x, axis, [(i, (i + steps) % n) for i in range(n)])


def local(
    tokens, lengths, conv_first, conv_second, norm_gain, w_query, w_key, w_value, w_out,
    bias_table, buckets, up_gain, grad_out,
):
    weights = (w_query, w_key, w_value, w_out)
    piece, row, last, gain, lens = call(
        before_kernel,
        [((80, WL), BF16), ((8, WL), F32), ((8, WL), F32), ((1, D), F32), ((8, 128), jnp.int32)],
        (lengths.reshape(1, 1), tokens[0], grad_out[0], conv_first, conv_second, up_gain, norm_gain[None]),
        [
            ((SEG, WL), BF16), ((SEG, WL), BF16), ((4, WL), F32), ((4, WL), F32), ((16, WL), F32),
            ((1, 1), jnp.int32), ((CL + 8, WL), F32), pltpu.SemaphoreType.DMA((7,)),
        ],
        smem=(),
        hbm=range(7),
        vmem=BIG,
    )
    line = ("x", "y", "core")
    rim = lax.ppermute(last, line, [(i, i + 1) for i in range(15)])
    over = [(i, ((i + 1) ^ 2)) for i in range(15)]
    across = shifted(piece, "y", 1)
    rim_across = lax.ppermute(last, line, over)
    (piece,) = call(
        pile_kernel,
        [((PIECE, WL), BF16)],
        (piece, row, across, rim, rim_across),
        smem=(),
        flops=6 * 10**9,
    )
    n = 640
    near = jnp.concatenate(
        [
            jnp.flip(buckets[:385]),
            jnp.full((n - LC,), bias_table.shape[0], jnp.int32),
            jnp.flip(buckets[385:]),
        ]
    )
    (strip,) = call(
        bias_kernel,
        [((NH, 128, LC), F32)],
        (jnp.broadcast_to(near[None], (8, n)), bias_table),
        smem=(1,),
    )
    pieces = [piece] + [shifted(piece, "tensor", s) for s in (2, 1, 3)]
    keep, send, blocks, crow = call(
        project_kernel,
        [((64, 4 * HW), BF16), ((80, 4 * HW), BF16), ((4, CL, 4 * HW), BF16), ((CL, D), BF16)],
        (*pieces, gain, *weights),
        [((2 * CL, D), BF16), ((2 * CL, D), BF16), ((2 * CL, D), BF16), ((2, 2 * CL, 4 * HW), BF16)],
        smem=(),
        flops=10**9,
    )
    swapped = shifted(send, "core", 1)
    up_far, down_far = call(
        pack_far_kernel, [((80, 4 * HW), BF16)] * 2, (keep, swapped, blocks), smem=()
    )
    up_near, down_near, b0 = call(
        pack_near_kernel,
        [((n, 4 * HW), BF16) for n in (96, 112, 160)],
        (keep, swapped, blocks),
        smem=(),
    )
    low_far, high_far = shifted(up_far, "x", 1), shifted(down_far, "x", -1)
    low_near, high_near = shifted(up_near, "x", 1), shifted(down_near, "x", -1)
    far_low, far_high = shifted(low_far, "x", 1), shifted(high_far, "x", -1)
    mine, nxt = call(
        gather_kernel,
        [((4, CL, 4 * HW), BF16), ((16, D), BF16)],
        (b0, low_near, high_near, far_low, far_high, swapped),
        smem=(),
    )
    other_rows = shifted(mine, "core", 1)
    res, keep_r, send_r = call(
        attend_kernel,
        [((4, LC + 16, HW), BF16), ((4, ROWS, HW), BF16), ((4, ROWS, HW), BF16)],
        (lens, b0, low_far, low_near, high_far, high_near, far_low, far_high, strip),
        [((LC, HW), BF16)] * 4 + [((NH, LC, LC), F32)] * 2 + [((NH, LC, LC), BF16)] * 2,
        smem=(),
        flops=6 * 10**9,
        vmem=16 * 2**20,
    )
    got_r = shifted(send_r, "core", 1)
    dw_keep, dw_send = call(
        weights_kernel,
        [((4, 128, HW), F32), ((4, 128, HW), BF16)],
        (res, mine, other_rows),
        [((LC, 256), BF16), ((LC, 256), BF16)],
        smem=(),
        flops=10**9,
    )
    dw_got = shifted(dw_send, "dp", 1)
    msg = (CL + ROWS, WL + 128)
    m1, m2, m3, own, cz, inv = call(
        partial_kernel,
        [(msg, BF16), (msg, BF16), (msg, BF16), (msg, F32), ((ROWS, WL), BF16), ((ROWS, 128), F32)],
        (keep_r, got_r, crow, nxt, dw_keep, gain, *weights),
        [((4, ROWS, WL), BF16), ((ROWS, D), BF16)],
        smem=(),
        flops=10**9,
    )
    r1, r2, r3 = shifted(m1, "tensor", 1), shifted(m2, "tensor", 2), shifted(m3, "tensor", 3)
    dw_own, dw_other = call(
        sum_kernel,
        [((4, 64, HW), F32), ((4, 64, HW), BF16)],
        (dw_keep, dw_got, r1),
        smem=(),
    )
    dw_other = shifted(dw_other, "core", 1)
    dw = call(
        total_kernel,
        [((64, WL), F32)] * 4,
        (dw_own, dw_other),
        smem=(),
        flops=6 * 10**9,
        typed=False,
    )
    update, grad_tokens = call(
        after_kernel,
        [((SEG, WL), BF16)] * 2,
        (lens, own, r1, r2, r3, cz, inv, gain, conv_first, conv_second, up_gain),
        [((ROWS, WL), F32)],
        flops=2 * 10**10,
        smem=(),
        typed=False,
    )
    return (update[None], grad_tokens[None], *dw)


def solution(mesh):
    ctx = ("x", "y", "core")
    fine = Mesh(
        np.asarray(mesh.devices).reshape(2, 4, 2, 2, 4), ("dp", "x", "y", "core", "tensor")
    )
    tok = P("dp", ctx, "tensor")
    col = P(None, "tensor")
    in_specs = (tok, P("dp"), col, col, P(), col, col, col, col, col, P(), col, tok)
    dw = P(("dp",) + ctx, "tensor")
    return jax.shard_map(
        local, mesh=fine, in_specs=in_specs, out_specs=(tok, tok, dw, dw, dw, dw), check_vma=False
    )
```

```python
import math

import jax
import jax.numpy as jnp
import numpy as np
from jax import lax
from jax.experimental import pallas as pl
from jax.experimental.pallas import tpu as pltpu
from jax.sharding import Mesh, PartitionSpec as P

F32 = jnp.float32
BF16 = jnp.bfloat16
NEG = float("-inf")
D = 2048
WL = 512
LC = 512
CL = 32
SEG = 512
HD = 128
NH = 2
HW = NH * HD
SCALE = 1.0 / math.sqrt(HD)
ROWS = CL + 16
VM = pltpu.VMEM
BIG = 63 * 2**20
SM = pltpu.SMEM
PIECE = 4 * CL


def dg(a, b, ca, cb):
    return lax.dot_general(a, b, (((ca,), (cb,)), ((), ())), preferred_element_type=F32)


class Place:
    def __init__(self):
        self.x, self.y, self.core = (lax.axis_index(a) for a in ("x", "y", "core"))
        self.dp, self.z = lax.axis_index("dp"), lax.axis_index("tensor")
        self.ctx = (self.x * 2 + self.y) * 2 + self.core


def in_three(a):
    hi = a.astype(BF16).astype(F32)
    lo = (a - hi).astype(BF16).astype(F32)
    return hi, lo, (a - hi - lo).astype(BF16).astype(F32)


def tap_weights(first, second):
    taps = jnp.concatenate([second[a : a + 1] * first for a in range(4)], axis=0)
    return jnp.concatenate([taps[15:16], taps[:15]], axis=0)


def byte_mask(ctx, doc_len):
    pos = ctx * SEG + 16 * lax.broadcasted_iota(jnp.int32, (CL, 16, WL), 0)
    pos = pos + lax.broadcasted_iota(jnp.int32, (CL, 16, WL), 1)
    return (pos < doc_len).astype(F32)


def before_kernel(
    lens, tokens_h, grad_h, first_h, second_h, up_h, gain_h, piece, row, last, gain,
    tokens, grad_out, first, second, up_gain, shift, sems,
):
    pairs = ((tokens_h, tokens), (first_h, first), (second_h, second), (grad_h, grad_out), (up_h, up_gain), (gain_h, gain))
    copies = [pltpu.make_async_copy(a, b, sems.at[i]) for i, (a, b) in enumerate(pairs)]
    for c in copies:
        c.start()
    mask = byte_mask(Place().ctx, lens[0])
    u = lax.broadcasted_iota(jnp.int32, (CL, 16, WL), 1)
    for c in copies[:3]:
        c.wait()
    taps = tap_weights(first[...], second[...])
    prod = tokens[...].astype(F32).reshape(CL, 16, WL) * mask * taps[None]
    own = jnp.sum(jnp.where(u == 0, prod, 0.0), axis=1)
    onward = jnp.sum(jnp.where(u == 0, 0.0, prod), axis=1)
    shift[0:8] = jnp.zeros((8, WL), F32)
    shift[8 : 8 + CL] = onward
    part = own + shift[7 : 7 + CL]
    piece[0:CL] = part.astype(BF16)
    row[...] = jnp.broadcast_to(part[0:1], (8, WL))
    piece[64:80] = jnp.concatenate(list(in_three(part[0:1])) + [jnp.zeros((13, WL), F32)], axis=0).astype(BF16)
    last[...] = jnp.broadcast_to(shift[7 + CL : 8 + CL], (8, WL))
    for c in copies[3:]:
        c.wait()
    weighted = grad_out[...].astype(F32).reshape(CL, 16, WL) * mask * up_gain[...][None]
    piece[CL : 2 * CL] = jnp.sum(weighted, axis=1).astype(BF16)


def pile_kernel(piece, row, across, rim, rim_across, out):
    y = Place().y
    first = lax.broadcasted_iota(jnp.int32, (16, WL), 0) == 0
    sent = across[64:80].astype(F32)
    theirs = sent[0:1] + sent[1:2] + sent[2:3] + rim_across[0:1]
    for src, at, top in ((piece, y * 64, row[0:1] + rim[0:1]), (across, 64 - y * 64, theirs)):
        head = jnp.where(first, top, src[0:16].astype(F32))
        out[pl.ds(pl.multiple_of(at, 64), 16)] = head.astype(BF16)
        out[pl.ds(pl.multiple_of(at + 16, 16), 48)] = src[16:64]


def bias_kernel(near, table, strip):
    core = Place().core
    n = near.shape[1]
    which = near[0:1]
    for h in range(NH):
        row = jnp.full((1, n), NEG, F32)
        for b in range(table.shape[0]):
            row = jnp.where(which == b, table[b, core * NH + h], row)
        rolled = pltpu.roll(jnp.broadcast_to(row, (128, n)), 0, 1, stride=1, stride_axis=0)
        strip[h] = rolled[:, :LC]


def project_kernel(
    p0, r1, r2, r3, gain, wq, wk, wv, wo, keep, send, blocks, mine, hown, craw, nrm, gco, both, hs
):
    at = Place()
    z, core, x, y = at.z, at.core, at.x, at.y
    for s, src in enumerate((p0, r1, r2, r3)):
        cols = pl.ds(pl.multiple_of(lax.rem(z + 4 - s, 4) * WL, WL), WL)
        for i in range(2):
            rows = slice(i * CL, i * CL + CL)
            craw[rows, cols] = src[2 * i * CL : 2 * i * CL + CL]
            gco[rows, cols] = src[2 * i * CL + CL : 2 * i * CL + 2 * CL]
    mine[...] = craw[pl.ds(pl.multiple_of(y * CL, CL), CL)]
    c = craw[...].astype(F32)
    square = jnp.sum(c * c, axis=1, keepdims=True) * (1.0 / D) + 1e-6
    r = lax.rsqrt(square)
    rms = jnp.sqrt(square)
    nrm[...] = (c * r * gain[...]).astype(BF16)
    for src, w, slot in ((gco, wo, 3), (nrm, wq, 0), (nrm, wk, 1), (nrm, wv, 2)):
        full = jnp.dot(src[...], w[...], preferred_element_type=F32)
        v = full.astype(BF16)
        if slot < 3:
            hs[...] = full * rms
            hown[slot] = hs[pl.ds(pl.multiple_of(y * CL, CL), CL)]
        for half in range(2):
            both[half, :, slot * HW : slot * HW + HW] = v[:, half * HW : half * HW + HW]
    keep[...] = both[core]
    send[0:64] = both[1 - core]
    tops = [c[i * CL : i * CL + 1, j * 1024 : j * 1024 + 1024] for i in range(2) for j in range(2)]
    send[64:80] = jnp.concatenate(tops + [jnp.zeros((12, 1024), F32)], axis=0).astype(BF16)
    for s in range(4):
        for d in range(2):
            chip = lax.rem(x + s, 4) * 2 + y
            cols = pl.ds(pl.multiple_of((d * 8 + chip) * 128, 128), 128)
            for i in range(2):
                rows = slice(i * CL, i * CL + CL)
                at = i * 512 + d * 128
                blocks[s, :, at : at + 128] = nrm[rows, cols]
                blocks[s, :, at + 256 : at + 384] = gco[rows, cols]


def pack_far_kernel(keep, swapped, blocks, up, down):
    core = Place().core
    for i, out in ((0, up), (1, down)):
        for src, c in ((keep, core), (swapped, 1 - core)):
            out[pl.ds(pl.multiple_of(c * CL, CL), CL)] = src[i * CL : i * CL + CL]
    up[64:80] = blocks[2, 0:16]
    down[64:80] = blocks[2, 16:32]


def pack_near_kernel(keep, swapped, blocks, up, down, b0):
    core = Place().core
    for i, out in ((1, up), (0, down)):
        for src, c in ((keep, core), (swapped, 1 - core)):
            out[pl.ds(pl.multiple_of(32 + c * CL, CL), CL)] = src[i * CL : i * CL + CL]
    for i in range(2):
        for src, c in ((keep, core), (swapped, 1 - core)):
            row = pl.multiple_of(i * 64 + c * CL, CL)
            b0[pl.ds(row, CL)] = src[i * CL : i * CL + CL]
    up[0:32] = blocks[1]
    down[0:32] = blocks[3]
    down[96:112] = swapped[64:80]
    b0[128:160] = blocks[0]


def gather_kernel(b0, low_near, high_near, far_low, far_high, after, mine):
    mine[0] = b0[128:160]
    mine[1] = low_near[0:32]
    mine[2, 0:16] = far_low[64:80]
    mine[2, 16:32] = far_high[64:80]
    mine[3] = high_near[0:32]


def next_kernel(high_near, swapped, gain, wq, wk, wv, nxt, hnext):
    at = Place()
    wraps = jnp.logical_and(at.core == 1, at.y == 1)
    tops = jnp.where(wraps, high_near[96:112].astype(F32), swapped[64:80].astype(F32))
    upper = jnp.where(at.core == 0, at.y, 1 - at.y) == 1
    for j in range(2):
        row = jnp.where(upper, tops[2 + j : 3 + j], tops[j : j + 1])
        nxt[:, j * 1024 : j * 1024 + 1024] = jnp.broadcast_to(row, (16, 1024)).astype(BF16)
    gained = (nxt[...].astype(F32) * gain[...]).astype(BF16)
    for i, w in enumerate((wq, wk, wv)):
        hnext[i] = jnp.dot(gained, w[...], preferred_element_type=F32)


def attend_kernel(
    lens, b0, low_far, low_near, high_far, high_near, far_low, far_high, strip,
    res, keep, send, q, k, v, ga, score, dprob, sg, pb,
):
    at = Place()
    ctx, core, x, doc_len = at.ctx, at.core, at.x, lens[0]
    for src, first, n, s, row in (
        (b0, 0, 128, 0, 0),
        (low_far, 0, 64, 1, 0),
        (low_near, 32, 64, 1, 64),
        (far_low, 0, 64, 2, 0),
        (far_high, 0, 64, 2, 64),
        (high_near, 32, 64, 3, 0),
        (high_far, 0, 64, 3, 64),
    ):
        rows = pl.ds(pl.multiple_of(lax.rem(x + 4 - s, 4) * 128 + row, 64), n)
        for i, dst in enumerate((q, k, v, ga)):
            dst[rows] = src[first : first + n, i * HW : i * HW + HW]
    key_pos = lax.broadcasted_iota(jnp.int32, (1, LC), 1)
    key_mask = jnp.where(16 * key_pos < doc_len, 0.0, NEG)
    work = [(b, h, slice(h * HD, h * HD + HD)) for b in (3, 2, 1, 0) for h in range(NH)]
    for b, h, c in work:
        rows, n = slice(b * 128, b * 128 + 128), b * 128 + 128
        score[h, rows, 0:n] = dg(q[rows, c], k[0:n, c], 1, 1)
        dprob[h, rows, 0:n] = dg(ga[rows, c], v[0:n, c], 1, 1)
    for b, h, c in work:
        rows, n = slice(b * 128, b * 128 + 128), b * 128 + 128
        s = score[h, rows, 0:n] * SCALE + strip[h, :, LC - n :] + key_mask[:, :n]
        e = jnp.exp(s - jnp.max(s, axis=1, keepdims=True))
        p = e * (1.0 / jnp.sum(e, axis=1, keepdims=True))
        dp = dprob[h, rows, 0:n]
        dot = jnp.sum(p * dp, axis=1, keepdims=True)
        sg[h, rows, 0:n] = (p * (dp - dot)).astype(BF16)
        pb[h, rows, 0:n] = p.astype(BF16)
    for b, h, c in work:
        rows, n = slice(b * 128, b * 128 + 128), b * 128 + 128
        gq = jnp.dot(sg[h, rows, 0:n], k[0:n, c], preferred_element_type=F32)
        res[0, rows, c] = (gq * SCALE).astype(BF16)
        res[3, rows, c] = jnp.dot(pb[h, rows, 0:n], v[0:n, c], preferred_element_type=F32).astype(BF16)
        tail = slice(b * 128, LC)
        res[1, rows, c] = (dg(sg[h, tail, rows], q[tail, c], 0, 0) * SCALE).astype(BF16)
        res[2, rows, c] = dg(pb[h, tail, rows], ga[tail, c], 0, 0).astype(BF16)
    res[:, LC : LC + 16] = jnp.zeros((4, 16, HW), BF16)
    peer = ctx + 1 - 2 * core
    keep[...] = res[:, pl.ds(pl.multiple_of(ctx * CL, CL), ROWS)]
    send[...] = res[:, pl.ds(pl.multiple_of(peer * CL, CL), ROWS)]


def weights_kernel(res, mine, other, keep, send, nb, gb):
    at = Place()
    core, x, dp = at.core, at.x, at.dp
    for s in range(4):
        for src, c in ((mine, core), (other, 1 - core)):
            for i in range(2):
                row = (lax.rem(x + 4 - s, 4) * 4 + i * 2 + c) * CL
                rows = pl.ds(pl.multiple_of(row, CL), CL)
                nb[rows] = src[s, :, i * 512 : i * 512 + 256]
                gb[rows] = src[s, :, i * 512 + 256 : i * 512 + 512]
    for w in range(4):
        src = gb if w == 3 else nb
        for d, out in ((dp, keep), (1 - dp, send)):
            cols = pl.ds(pl.multiple_of(d * 128, 128), 128)
            out[w] = dg(src[:, cols], res[w, 0:LC], 0, 0).astype(out.dtype)


def sum_kernel(keep, got, r2, own, send):
    core = Place().core
    for w in range(4):
        for c, out in ((core, own), (1 - core, send)):
            rows = pl.ds(pl.multiple_of(c * 64, 64), 64)
            out[w] = (keep[w, rows] + got[w, rows].astype(F32)).astype(out.dtype)


def message(g, weights, t, msg):
    part = pl.ds(pl.multiple_of(t * WL, WL), WL)
    wq, wk, wv, wo = weights
    gn = dg(g[0], wq[part], 1, 1) + dg(g[1], wk[part], 1, 1) + dg(g[2], wv[part], 1, 1)
    msg[0:CL, 0:WL] = dg(g[3, 0:CL], wo[part], 1, 1).astype(msg.dtype)
    msg[CL : CL + ROWS, 0:WL] = gn.astype(msg.dtype)
    msg[0:CL, WL : WL + 128] = jnp.zeros((CL, 128), msg.dtype)


def partial_far_kernel(keep_r, got_r, hown, hnext, after, wq, wk, wv, wo, msg2, g, sums):
    at = Place()
    z, core = at.z, at.core
    g[:, :, pl.ds(pl.multiple_of(core * HW, HW), HW)] = keep_r[...]
    g[:, :, pl.ds(pl.multiple_of((1 - core) * HW, HW), HW)] = got_r[...]
    both = []
    for rows, h in ((slice(0, CL), hown), (slice(CL, ROWS), hnext)):
        total = sum(g[i, rows].astype(F32) * h[i] for i in range(3))
        both.append(jnp.sum(total, axis=1, keepdims=True))
    dots = jnp.concatenate(both, axis=0)
    sums[...] = jnp.broadcast_to(dots, (ROWS, 128))
    lane = lax.broadcasted_iota(jnp.int32, (ROWS, 128), 1)
    hi = dots.astype(BF16).astype(F32)
    lo = (dots - hi).astype(BF16).astype(F32)
    lo2 = dots - hi - lo
    packed = jnp.where(lane == 0, hi, jnp.where(lane == 1, lo, lo2))
    message(g, (wq, wk, wv, wo), lax.rem(z + 2, 4), msg2)
    msg2[CL : CL + ROWS, WL : WL + 128] = jnp.where(lane < 3, packed, 0.0).astype(BF16)


def partial_near_kernel(g, sums, msg2, crow, nxt, wq, wk, wv, wo, msg1, msg3, keep, cz, inv_out, c):
    z = Place().z
    weights = (wq, wk, wv, wo)
    for shift, msg in ((1, msg1), (3, msg3)):
        message(g, weights, lax.rem(z + shift, 4), msg)
        msg[CL : CL + ROWS, WL : WL + 128] = msg2[CL : CL + ROWS, WL : WL + 128]
    message(g, weights, z, keep)
    keep[CL : CL + ROWS, WL : WL + 128] = sums[...]
    c[0:CL] = crow[...]
    c[CL:ROWS] = nxt[...]
    cf = c[...].astype(F32)
    r = lax.rsqrt(jnp.sum(cf * cf, axis=1, keepdims=True) * (1.0 / D) + 1e-6)
    inv_out[...] = jnp.broadcast_to(r, (ROWS, 128))
    cz[...] = c[:, pl.ds(pl.multiple_of(z * WL, WL), WL)]


def total_kernel(own, other, o0, o1, o2, o3):
    core = Place().core
    for w, o in enumerate((o0, o1, o2, o3)):
        o[:, pl.ds(pl.multiple_of(core * HW, HW), HW)] = own[w]
        o[:, pl.ds(pl.multiple_of((1 - core) * HW, HW), HW)] = other[w].astype(F32)


def after_kernel(
    lens, keep, r1, r2, r3, cz, inv, gain, first, second, up_gain, update, grad, rows
):
    at = Place()
    ctx, doc_len, z = at.ctx, lens[0], at.z
    mask = byte_mask(ctx, doc_len)
    body = slice(0, WL)
    out = keep[0:CL, body]
    gn = keep[CL : CL + ROWS, body]
    dots = keep[CL : CL + ROWS, WL : WL + 1]
    for r in (r1, r2, r3):
        out = out + r[0:CL, body].astype(F32)
        gn = gn + r[CL : CL + ROWS, body].astype(F32)
        dots = dots + jnp.sum(r[CL : CL + ROWS, WL : WL + 128].astype(F32), axis=1, keepdims=True)
    update[...] = ((out[:, None, :] * up_gain[...][None]) * mask).reshape(SEG, WL).astype(BF16)
    i = inv[:, 0:1]
    gained = gn * gain[0:1, pl.ds(pl.multiple_of(z * WL, WL), WL)]
    full = i * gained - cz[...].astype(F32) * (i * i * i) * dots * (1.0 / D)
    exists = lax.broadcasted_iota(jnp.int32, (ROWS, WL), 0) + ctx * CL < LC
    rows[...] = jnp.where(exists, full, 0.0)
    taps = tap_weights(first[...], second[...])
    u = lax.broadcasted_iota(jnp.int32, (CL, 16, WL), 1)
    picked = jnp.where(u == 0, rows[0:CL][:, None, :], rows[1 : CL + 1][:, None, :])
    grad[...] = (picked * taps[None] * mask).reshape(SEG, WL).astype(BF16)


def call(kernel, outs, args, scratch=(), smem=(0,), flops=0, size=0, vmem=8 * 2**20, hbm=(), typed=True):
    def spec(i):
        return pl.BlockSpec(memory_space=SM if i in smem else pltpu.HBM if i in hbm else VM)

    return pl.pallas_call(
        kernel,
        out_shape=[pltpu.VMEM(s, d) if typed else jax.ShapeDtypeStruct(s, d) for s, d in outs],
        in_specs=[spec(i) for i in range(len(args))],
        out_specs=[pl.BlockSpec(memory_space=VM)] * len(outs),
        scratch_shapes=[pltpu.VMEM(*s) if isinstance(s, tuple) else s for s in scratch],
        compiler_params=pltpu.CompilerParams(vmem_limit_bytes=vmem),
        cost_estimate=pl.CostEstimate(flops=flops, bytes_accessed=size, transcendentals=0),
    )(*args)


def shifted(x, axis, steps):
    n = lax.axis_size(axis)
    return lax.ppermute(x, axis, [(i, (i + steps) % n) for i in range(n)])


def local(
    tokens, lengths, conv_first, conv_second, norm_gain, w_query, w_key, w_value, w_out,
    bias_table, buckets, up_gain, grad_out,
):
    weights = (w_query, w_key, w_value, w_out)
    piece, row, last, gain = call(
        before_kernel,
        [((80, WL), BF16), ((8, WL), F32), ((8, WL), F32), ((1, D), F32)],
        (lengths, tokens[0], grad_out[0], conv_first, conv_second, up_gain, norm_gain[None]),
        [
            ((SEG, WL), BF16), ((SEG, WL), BF16), ((4, WL), F32), ((4, WL), F32), ((16, WL), F32),
            ((CL + 8, WL), F32), pltpu.SemaphoreType.DMA((6,)),
        ],
        hbm=(1, 2, 3, 4, 5, 6),
        vmem=BIG,
    )
    line = ("x", "y", "core")
    rim = lax.ppermute(last, line, [(i, i + 1) for i in range(15)])
    over = [(i, ((i + 1) ^ 2)) for i in range(15)]
    across = shifted(piece, "y", 1)
    rim_across = lax.ppermute(last, line, over)
    (piece,) = call(
        pile_kernel,
        [((PIECE, WL), BF16)],
        (piece, row, across, rim, rim_across),
        smem=(),
        flops=6 * 10**9,
    )
    n = 640
    near = jnp.concatenate(
        [
            jnp.flip(buckets[:385]),
            jnp.full((n - LC,), bias_table.shape[0], jnp.int32),
            jnp.flip(buckets[385:]),
        ]
    )
    (strip,) = call(
        bias_kernel,
        [((NH, 128, LC), F32)],
        (jnp.broadcast_to(near[None], (8, n)), bias_table),
        smem=(1,),
    )
    pieces = [piece] + [shifted(piece, "tensor", s) for s in (1, 2, 3)]
    keep, send, blocks, crow, hown = call(
        project_kernel,
        [((64, 4 * HW), BF16), ((80, 4 * HW), BF16), ((4, CL, 4 * HW), BF16), ((CL, D), BF16), ((3, CL, WL), F32)],
        (*pieces, gain, *weights),
        [((2 * CL, D), BF16), ((2 * CL, D), BF16), ((2 * CL, D), BF16), ((2, 2 * CL, 4 * HW), BF16), ((2 * CL, WL), F32)],
        smem=(),
        flops=10**9,
    )
    swapped = shifted(send, "core", 1)
    up_far, down_far = call(
        pack_far_kernel, [((80, 4 * HW), BF16)] * 2, (keep, swapped, blocks), smem=()
    )
    up_near, down_near, b0 = call(
        pack_near_kernel,
        [((n, 4 * HW), BF16) for n in (96, 112, 160)],
        (keep, swapped, blocks),
        smem=(),
    )
    low_far, high_far = shifted(up_far, "x", 1), shifted(down_far, "x", -1)
    low_near, high_near = shifted(up_near, "x", 1), shifted(down_near, "x", -1)
    far_low, far_high = shifted(low_far, "x", 1), shifted(high_far, "x", -1)
    nxt, hnext = call(
        next_kernel,
        [((16, D), BF16), ((3, 16, WL), F32)],
        (high_near, swapped, gain, *weights[:3]),
        smem=(),
        flops=10**9,
    )
    (mine,) = call(
        gather_kernel,
        [((4, CL, 4 * HW), BF16)],
        (b0, low_near, high_near, far_low, far_high, nxt),
        smem=(),
    )
    other_rows = shifted(mine, "core", 1)
    res, keep_r, send_r = call(
        attend_kernel,
        [((4, LC + 16, HW), BF16), ((4, ROWS, HW), BF16), ((4, ROWS, HW), BF16)],
        (lengths, b0, low_far, low_near, high_far, high_near, far_low, far_high, strip),
        [((LC, HW), BF16)] * 4 + [((NH, LC, LC), F32)] * 2 + [((NH, LC, LC), BF16)] * 2,
        flops=6 * 10**9,
        vmem=16 * 2**20,
    )
    got_r = shifted(send_r, "core", 1)
    dw_keep, dw_send = call(
        weights_kernel,
        [((4, 128, HW), F32), ((4, 128, HW), BF16)],
        (res, mine, other_rows),
        [((LC, 256), BF16), ((LC, 256), BF16)],
        smem=(),
        flops=10**9,
    )
    dw_got = shifted(dw_send, "dp", 1)
    msg = (CL + ROWS, WL + 128)
    m2, g, sums = call(
        partial_far_kernel,
        [(msg, BF16), ((4, ROWS, WL), BF16), ((ROWS, 128), F32)],
        (keep_r, got_r, hown, hnext, dw_keep, *weights),
        smem=(),
        flops=3 * 10**8,
    )
    m1, m3, own, cz, inv = call(
        partial_near_kernel,
        [(msg, BF16), (msg, BF16), (msg, F32), ((ROWS, WL), BF16), ((ROWS, 128), F32)],
        (g, sums, m2, crow, nxt, *weights),
        [((ROWS, D), BF16)],
        smem=(),
        flops=10**9,
    )
    r1, r2, r3 = shifted(m1, "tensor", 1), shifted(m2, "tensor", 2), shifted(m3, "tensor", 3)
    dw_own, dw_other = call(
        sum_kernel,
        [((4, 64, HW), F32), ((4, 64, HW), BF16)],
        (dw_keep, dw_got, r2),
        smem=(),
    )
    dw_other = shifted(dw_other, "core", 1)
    dw = call(
        total_kernel,
        [((64, WL), F32)] * 4,
        (dw_own, dw_other),
        smem=(),
        flops=6 * 10**9,
        typed=False,
    )
    update, grad_tokens = call(
        after_kernel,
        [((SEG, WL), BF16)] * 2,
        (lengths, own, r1, r2, r3, cz, inv, gain, conv_first, conv_second, up_gain),
        [((ROWS, WL), F32)],
        flops=2 * 10**10,
        typed=False,
    )
    return (update[None], grad_tokens[None], *dw)


def solution(mesh):
    ctx = ("x", "y", "core")
    fine = Mesh(
        np.asarray(mesh.devices).reshape(2, 4, 2, 2, 4), ("dp", "x", "y", "core", "tensor")
    )
    tok = P("dp", ctx, "tensor")
    col = P(None, "tensor")
    in_specs = (tok, P("dp"), col, col, P(), col, col, col, col, col, P(), col, tok)
    dw = P(("dp",) + ctx, "tensor")
    return jax.shard_map(
        local, mesh=fine, in_specs=in_specs, out_specs=(tok, tok, dw, dw, dw, dw), check_vma=False
    )
```

```python
import math

import jax
import jax.numpy as jnp
import numpy as np
from jax import lax
from jax.experimental import pallas as pl
from jax.experimental.pallas import tpu as pltpu
from jax.sharding import Mesh, PartitionSpec as P

F32 = jnp.float32
BF16 = jnp.bfloat16
NEG = float("-inf")
D = 2048
WL = 512
LC = 512
CL = 32
SEG = 512
HD = 128
NH = 2
HW = NH * HD
SCALE = 1.0 / math.sqrt(HD)
ROWS = CL + 16
VM = pltpu.VMEM
BIG = 63 * 2**20
SM = pltpu.SMEM
PIECE = 4 * CL


def dg(a, b, ca, cb):
    return lax.dot_general(a, b, (((ca,), (cb,)), ((), ())), preferred_element_type=F32)


class Place:
    def __init__(self):
        self.x, self.y, self.core = (lax.axis_index(a) for a in ("x", "y", "core"))
        self.dp, self.z = lax.axis_index("dp"), lax.axis_index("tensor")
        self.ctx = (self.x * 2 + self.y) * 2 + self.core


def in_three(a):
    hi = a.astype(BF16).astype(F32)
    lo = (a - hi).astype(BF16).astype(F32)
    return hi, lo, (a - hi - lo).astype(BF16).astype(F32)


def tap_weights(first, second):
    taps = jnp.concatenate([second[a : a + 1] * first for a in range(4)], axis=0)
    return jnp.concatenate([taps[15:16], taps[:15]], axis=0)


def byte_mask(ctx, doc_len):
    pos = ctx * SEG + 16 * lax.broadcasted_iota(jnp.int32, (CL, 16, WL), 0)
    pos = pos + lax.broadcasted_iota(jnp.int32, (CL, 16, WL), 1)
    return (pos < doc_len).astype(F32)


def before_kernel(
    lens, tokens_h, grad_h, first_h, second_h, up_h, gain_h, piece, row, last, gain,
    tokens, grad_out, first, second, up_gain, shift, sems,
):
    pairs = ((tokens_h, tokens), (first_h, first), (second_h, second), (grad_h, grad_out), (up_h, up_gain), (gain_h, gain))
    copies = [pltpu.make_async_copy(a, b, sems.at[i]) for i, (a, b) in enumerate(pairs)]
    for c in copies:
        c.start()
    mask = byte_mask(Place().ctx, lens[0])
    u = lax.broadcasted_iota(jnp.int32, (CL, 16, WL), 1)
    for c in copies[:3]:
        c.wait()
    taps = tap_weights(first[...], second[...])
    prod = tokens[...].astype(F32).reshape(CL, 16, WL) * mask * taps[None]
    own = jnp.sum(jnp.where(u == 0, prod, 0.0), axis=1)
    onward = jnp.sum(jnp.where(u == 0, 0.0, prod), axis=1)
    shift[0:8] = jnp.zeros((8, WL), F32)
    shift[8 : 8 + CL] = onward
    part = own + shift[7 : 7 + CL]
    piece[0:CL] = part.astype(BF16)
    row[...] = jnp.broadcast_to(part[0:1], (8, WL))
    piece[64:80] = jnp.concatenate(list(in_three(part[0:1])) + [jnp.zeros((13, WL), F32)], axis=0).astype(BF16)
    last[...] = jnp.broadcast_to(shift[7 + CL : 8 + CL], (8, WL))
    for c in copies[3:]:
        c.wait()
    weighted = grad_out[...].astype(F32).reshape(CL, 16, WL) * mask * up_gain[...][None]
    piece[CL : 2 * CL] = jnp.sum(weighted, axis=1).astype(BF16)


def pile_kernel(piece, row, across, rim, rim_across, out):
    y = Place().y
    first = lax.broadcasted_iota(jnp.int32, (16, WL), 0) == 0
    sent = across[64:80].astype(F32)
    theirs = sent[0:1] + sent[1:2] + sent[2:3] + rim_across[0:1]
    for src, at, top in ((piece, y * 64, row[0:1] + rim[0:1]), (across, 64 - y * 64, theirs)):
        head = jnp.where(first, top, src[0:16].astype(F32))
        out[pl.ds(pl.multiple_of(at, 64), 16)] = head.astype(BF16)
        out[pl.ds(pl.multiple_of(at + 16, 16), 48)] = src[16:64]


def bias_kernel(near, table, strip):
    core = Place().core
    n = near.shape[1]
    which = near[0:1]
    for h in range(NH):
        row = jnp.full((1, n), NEG, F32)
        for b in range(table.shape[0]):
            row = jnp.where(which == b, table[b, core * NH + h], row)
        rolled = pltpu.roll(jnp.broadcast_to(row, (128, n)), 0, 1, stride=1, stride_axis=0)
        strip[h] = rolled[:, :LC]


def project_kernel(
    p0, r1, r2, r3, gain, wq, wk, wv, wo, keep, send, blocks, mine, hown, craw, nrm, gco, both, hs
):
    at = Place()
    z, core, x, y = at.z, at.core, at.x, at.y
    for s, src in enumerate((p0, r1, r2, r3)):
        cols = pl.ds(pl.multiple_of(lax.rem(z + 4 - s, 4) * WL, WL), WL)
        for i in range(2):
            rows = slice(i * CL, i * CL + CL)
            craw[rows, cols] = src[2 * i * CL : 2 * i * CL + CL]
            gco[rows, cols] = src[2 * i * CL + CL : 2 * i * CL + 2 * CL]
    mine[...] = craw[pl.ds(pl.multiple_of(y * CL, CL), CL)]
    c = craw[...].astype(F32)
    square = jnp.sum(c * c, axis=1, keepdims=True) * (1.0 / D) + 1e-6
    r = lax.rsqrt(square)
    rms = jnp.sqrt(square)
    nrm[...] = (c * r * gain[...]).astype(BF16)
    heads_of = [[], []]
    for src, w, slot in ((gco, wo, 3), (nrm, wq, 0), (nrm, wk, 1), (nrm, wv, 2)):
        full = jnp.dot(src[...], w[...], preferred_element_type=F32)
        v = full.astype(BF16)
        if slot < 3:
            h = full * rms
            hs[...] = h
            for i in range(2):
                heads_of[i].append(in_three(h[i * CL : i * CL + 1])[:2])
            hown[slot] = hs[pl.ds(pl.multiple_of(y * CL, CL), CL)]
        for half in range(2):
            both[half, :, slot * HW : slot * HW + HW] = v[:, half * HW : half * HW + HW]
    keep[...] = both[core]
    send[0:64] = both[1 - core]
    tops = [c[i * CL : i * CL + 1, j * 1024 : j * 1024 + 1024] for i in range(2) for j in range(2)]
    for (q_hi, q_lo), (k_hi, k_lo), (v_hi, v_lo) in heads_of:
        tops += [jnp.concatenate(p, axis=1) for p in ((q_hi, k_hi), (v_hi, q_lo), (k_lo, v_lo))]
    send[64:80] = jnp.concatenate(tops + [jnp.zeros((6, 1024), F32)], axis=0).astype(BF16)
    for s in range(4):
        for d in range(2):
            chip = lax.rem(x + s, 4) * 2 + y
            cols = pl.ds(pl.multiple_of((d * 8 + chip) * 128, 128), 128)
            for i in range(2):
                rows = slice(i * CL, i * CL + CL)
                at = i * 512 + d * 128
                blocks[s, :, at : at + 128] = nrm[rows, cols]
                blocks[s, :, at + 256 : at + 384] = gco[rows, cols]


def pack_far_kernel(keep, swapped, blocks, up, down):
    core = Place().core
    for i, out in ((0, up), (1, down)):
        for src, c in ((keep, core), (swapped, 1 - core)):
            out[pl.ds(pl.multiple_of(c * CL, CL), CL)] = src[i * CL : i * CL + CL]
    up[64:80] = blocks[2, 0:16]
    down[64:80] = blocks[2, 16:32]


def pack_near_kernel(keep, swapped, blocks, up, down, b0):
    core = Place().core
    for i, out in ((1, up), (0, down)):
        for src, c in ((keep, core), (swapped, 1 - core)):
            out[pl.ds(pl.multiple_of(32 + c * CL, CL), CL)] = src[i * CL : i * CL + CL]
    for i in range(2):
        for src, c in ((keep, core), (swapped, 1 - core)):
            row = pl.multiple_of(i * 64 + c * CL, CL)
            b0[pl.ds(row, CL)] = src[i * CL : i * CL + CL]
    up[0:32] = blocks[1]
    down[0:32] = blocks[3]
    down[96:112] = swapped[64:80]
    b0[128:160] = blocks[0]


def gather_kernel(b0, low_near, high_near, far_low, far_high, swapped, mine, nxt, hnext):
    mine[0] = b0[128:160]
    mine[1] = low_near[0:32]
    mine[2, 0:16] = far_low[64:80]
    mine[2, 16:32] = far_high[64:80]
    mine[3] = high_near[0:32]
    at = Place()
    wraps = jnp.logical_and(at.core == 1, at.y == 1)
    tops = jnp.where(wraps, high_near[96:112].astype(F32), swapped[64:80].astype(F32))
    upper = jnp.where(at.core == 0, at.y, 1 - at.y) == 1
    for j in range(2):
        row = jnp.where(upper, tops[2 + j : 3 + j], tops[j : j + 1])
        nxt[:, j * 1024 : j * 1024 + 1024] = jnp.broadcast_to(row, (16, 1024)).astype(BF16)
    a, b, c = [jnp.where(upper, tops[7 + j : 8 + j], tops[4 + j : 5 + j]) for j in range(3)]
    left, right = slice(0, WL), slice(WL, 2 * WL)
    products = (a[:, left] + b[:, right], a[:, right] + c[:, left], b[:, left] + c[:, right])
    for i, h in enumerate(products):
        hnext[i] = jnp.broadcast_to(h, (16, WL))


def attend_kernel(
    lens, b0, low_far, low_near, high_far, high_near, far_low, far_high, strip,
    res, keep, send, q, k, v, ga, score, dprob, sg, pb,
):
    at = Place()
    ctx, core, x, doc_len = at.ctx, at.core, at.x, lens[0]
    for src, first, n, s, row in (
        (b0, 0, 128, 0, 0),
        (low_far, 0, 64, 1, 0),
        (low_near, 32, 64, 1, 64),
        (far_low, 0, 64, 2, 0),
        (far_high, 0, 64, 2, 64),
        (high_near, 32, 64, 3, 0),
        (high_far, 0, 64, 3, 64),
    ):
        rows = pl.ds(pl.multiple_of(lax.rem(x + 4 - s, 4) * 128 + row, 64), n)
        for i, dst in enumerate((q, k, v, ga)):
            dst[rows] = src[first : first + n, i * HW : i * HW + HW]
    key_pos = lax.broadcasted_iota(jnp.int32, (1, LC), 1)
    key_mask = jnp.where(16 * key_pos < doc_len, 0.0, NEG)
    work = [(b, h, slice(h * HD, h * HD + HD)) for b in (3, 2, 1, 0) for h in range(NH)]
    for b, h, c in work:
        rows, n = slice(b * 128, b * 128 + 128), b * 128 + 128
        score[h, rows, 0:n] = dg(q[rows, c], k[0:n, c], 1, 1)
        dprob[h, rows, 0:n] = dg(ga[rows, c], v[0:n, c], 1, 1)
    for b, h, c in work:
        rows, n = slice(b * 128, b * 128 + 128), b * 128 + 128
        s = score[h, rows, 0:n] * SCALE + strip[h, :, LC - n :] + key_mask[:, :n]
        e = jnp.exp(s - jnp.max(s, axis=1, keepdims=True))
        p = e * (1.0 / jnp.sum(e, axis=1, keepdims=True))
        dp = dprob[h, rows, 0:n]
        dot = jnp.sum(p * dp, axis=1, keepdims=True)
        sg[h, rows, 0:n] = (p * (dp - dot)).astype(BF16)
        pb[h, rows, 0:n] = p.astype(BF16)
    for b, h, c in work:
        rows, n = slice(b * 128, b * 128 + 128), b * 128 + 128
        gq = jnp.dot(sg[h, rows, 0:n], k[0:n, c], preferred_element_type=F32)
        res[0, rows, c] = (gq * SCALE).astype(BF16)
        res[3, rows, c] = jnp.dot(pb[h, rows, 0:n], v[0:n, c], preferred_element_type=F32).astype(BF16)
        tail = slice(b * 128, LC)
        res[1, rows, c] = (dg(sg[h, tail, rows], q[tail, c], 0, 0) * SCALE).astype(BF16)
        res[2, rows, c] = dg(pb[h, tail, rows], ga[tail, c], 0, 0).astype(BF16)
    res[:, LC : LC + 16] = jnp.zeros((4, 16, HW), BF16)
    peer = ctx + 1 - 2 * core
    keep[...] = res[:, pl.ds(pl.multiple_of(ctx * CL, CL), ROWS)]
    send[...] = res[:, pl.ds(pl.multiple_of(peer * CL, CL), ROWS)]


def weights_kernel(res, mine, other, keep, send, nb, gb):
    at = Place()
    core, x, dp = at.core, at.x, at.dp
    for s in range(4):
        for src, c in ((mine, core), (other, 1 - core)):
            for i in range(2):
                row = (lax.rem(x + 4 - s, 4) * 4 + i * 2 + c) * CL
                rows = pl.ds(pl.multiple_of(row, CL), CL)
                nb[rows] = src[s, :, i * 512 : i * 512 + 256]
                gb[rows] = src[s, :, i * 512 + 256 : i * 512 + 512]
    for w in range(4):
        src = gb if w == 3 else nb
        for d, out in ((dp, keep), (1 - dp, send)):
            cols = pl.ds(pl.multiple_of(d * 128, 128), 128)
            out[w] = dg(src[:, cols], res[w, 0:LC], 0, 0).astype(out.dtype)


def sum_kernel(keep, got, r2, own, send):
    core = Place().core
    for w in range(4):
        for c, out in ((core, own), (1 - core, send)):
            rows = pl.ds(pl.multiple_of(c * 64, 64), 64)
            out[w] = (keep[w, rows] + got[w, rows].astype(F32)).astype(out.dtype)


def message(g, weights, t, msg):
    part = pl.ds(pl.multiple_of(t * WL, WL), WL)
    wq, wk, wv, wo = weights
    gn = dg(g[0], wq[part], 1, 1) + dg(g[1], wk[part], 1, 1) + dg(g[2], wv[part], 1, 1)
    msg[0:CL, 0:WL] = dg(g[3, 0:CL], wo[part], 1, 1).astype(msg.dtype)
    msg[CL : CL + ROWS, 0:WL] = gn.astype(msg.dtype)
    msg[0:CL, WL : WL + 128] = jnp.zeros((CL, 128), msg.dtype)


def partial_far_kernel(keep_r, got_r, hown, hnext, after, wq, wk, wv, wo, msg2, g, sums):
    at = Place()
    z, core = at.z, at.core
    g[:, :, pl.ds(pl.multiple_of(core * HW, HW), HW)] = keep_r[...]
    g[:, :, pl.ds(pl.multiple_of((1 - core) * HW, HW), HW)] = got_r[...]
    both = []
    for rows, h in ((slice(0, CL), hown), (slice(CL, ROWS), hnext)):
        total = sum(g[i, rows].astype(F32) * h[i] for i in range(3))
        both.append(jnp.sum(total, axis=1, keepdims=True))
    dots = jnp.concatenate(both, axis=0)
    sums[...] = jnp.broadcast_to(dots, (ROWS, 128))
    lane = lax.broadcasted_iota(jnp.int32, (ROWS, 128), 1)
    hi = dots.astype(BF16).astype(F32)
    lo = (dots - hi).astype(BF16).astype(F32)
    lo2 = dots - hi - lo
    packed = jnp.where(lane == 0, hi, jnp.where(lane == 1, lo, lo2))
    message(g, (wq, wk, wv, wo), lax.rem(z + 2, 4), msg2)
    msg2[CL : CL + ROWS, WL : WL + 128] = jnp.where(lane < 3, packed, 0.0).astype(BF16)


def partial_near_kernel(g, sums, msg2, crow, nxt, wq, wk, wv, wo, msg1, msg3, keep, cz, inv_out, c):
    z = Place().z
    weights = (wq, wk, wv, wo)
    for shift, msg in ((1, msg1), (3, msg3)):
        message(g, weights, lax.rem(z + shift, 4), msg)
        msg[CL : CL + ROWS, WL : WL + 128] = msg2[CL : CL + ROWS, WL : WL + 128]
    message(g, weights, z, keep)
    keep[CL : CL + ROWS, WL : WL + 128] = sums[...]
    c[0:CL] = crow[...]
    c[CL:ROWS] = nxt[...]
    cf = c[...].astype(F32)
    r = lax.rsqrt(jnp.sum(cf * cf, axis=1, keepdims=True) * (1.0 / D) + 1e-6)
    inv_out[...] = jnp.broadcast_to(r, (ROWS, 128))
    cz[...] = c[:, pl.ds(pl.multiple_of(z * WL, WL), WL)]


def total_kernel(own, other, o0, o1, o2, o3):
    core = Place().core
    for w, o in enumerate((o0, o1, o2, o3)):
        o[:, pl.ds(pl.multiple_of(core * HW, HW), HW)] = own[w]
        o[:, pl.ds(pl.multiple_of((1 - core) * HW, HW), HW)] = other[w].astype(F32)


def after_kernel(
    lens, keep, r1, r2, r3, cz, inv, gain, first, second, up_gain, update, grad, rows
):
    at = Place()
    ctx, doc_len, z = at.ctx, lens[0], at.z
    mask = byte_mask(ctx, doc_len)
    body = slice(0, WL)
    out = keep[0:CL, body]
    gn = keep[CL : CL + ROWS, body]
    dots = keep[CL : CL + ROWS, WL : WL + 1]
    for r in (r1, r2, r3):
        out = out + r[0:CL, body].astype(F32)
        gn = gn + r[CL : CL + ROWS, body].astype(F32)
        dots = dots + jnp.sum(r[CL : CL + ROWS, WL : WL + 128].astype(F32), axis=1, keepdims=True)
    update[...] = ((out[:, None, :] * up_gain[...][None]) * mask).reshape(SEG, WL).astype(BF16)
    i = inv[:, 0:1]
    gained = gn * gain[0:1, pl.ds(pl.multiple_of(z * WL, WL), WL)]
    full = i * gained - cz[...].astype(F32) * (i * i * i) * dots * (1.0 / D)
    exists = lax.broadcasted_iota(jnp.int32, (ROWS, WL), 0) + ctx * CL < LC
    rows[...] = jnp.where(exists, full, 0.0)
    taps = tap_weights(first[...], second[...])
    u = lax.broadcasted_iota(jnp.int32, (CL, 16, WL), 1)
    picked = jnp.where(u == 0, rows[0:CL][:, None, :], rows[1 : CL + 1][:, None, :])
    grad[...] = (picked * taps[None] * mask).reshape(SEG, WL).astype(BF16)


def call(kernel, outs, args, scratch=(), smem=(0,), flops=0, size=0, vmem=8 * 2**20, hbm=(), typed=True):
    def spec(i):
        return pl.BlockSpec(memory_space=SM if i in smem else pltpu.HBM if i in hbm else VM)

    return pl.pallas_call(
        kernel,
        out_shape=[pltpu.VMEM(s, d) if typed else jax.ShapeDtypeStruct(s, d) for s, d in outs],
        in_specs=[spec(i) for i in range(len(args))],
        out_specs=[pl.BlockSpec(memory_space=VM)] * len(outs),
        scratch_shapes=[pltpu.VMEM(*s) if isinstance(s, tuple) else s for s in scratch],
        compiler_params=pltpu.CompilerParams(vmem_limit_bytes=vmem),
        cost_estimate=pl.CostEstimate(flops=flops, bytes_accessed=size, transcendentals=0),
    )(*args)


def shifted(x, axis, steps):
    n = lax.axis_size(axis)
    return lax.ppermute(x, axis, [(i, (i + steps) % n) for i in range(n)])


def local(
    tokens, lengths, conv_first, conv_second, norm_gain, w_query, w_key, w_value, w_out,
    bias_table, buckets, up_gain, grad_out,
):
    weights = (w_query, w_key, w_value, w_out)
    piece, row, last, gain = call(
        before_kernel,
        [((80, WL), BF16), ((8, WL), F32), ((8, WL), F32), ((1, D), F32)],
        (lengths, tokens[0], grad_out[0], conv_first, conv_second, up_gain, norm_gain[None]),
        [
            ((SEG, WL), BF16), ((SEG, WL), BF16), ((4, WL), F32), ((4, WL), F32), ((16, WL), F32),
            ((CL + 8, WL), F32), pltpu.SemaphoreType.DMA((6,)),
        ],
        hbm=(1, 2, 3, 4, 5, 6),
        vmem=BIG,
    )
    line = ("x", "y", "core")
    rim = lax.ppermute(last, line, [(i, i + 1) for i in range(15)])
    over = [(i, ((i + 1) ^ 2)) for i in range(15)]
    across = shifted(piece, "y", 1)
    rim_across = lax.ppermute(last, line, over)
    (piece,) = call(
        pile_kernel,
        [((PIECE, WL), BF16)],
        (piece, row, across, rim, rim_across),
        smem=(),
        flops=6 * 10**9,
    )
    n = 640
    near = jnp.concatenate(
        [
            jnp.flip(buckets[:385]),
            jnp.full((n - LC,), bias_table.shape[0], jnp.int32),
            jnp.flip(buckets[385:]),
        ]
    )
    (strip,) = call(
        bias_kernel,
        [((NH, 128, LC), F32)],
        (jnp.broadcast_to(near[None], (8, n)), bias_table),
        smem=(1,),
    )
    pieces = [piece] + [shifted(piece, "tensor", s) for s in (1, 2, 3)]
    keep, send, blocks, crow, hown = call(
        project_kernel,
        [((64, 4 * HW), BF16), ((80, 4 * HW), BF16), ((4, CL, 4 * HW), BF16), ((CL, D), BF16), ((3, CL, WL), F32)],
        (*pieces, gain, *weights),
        [((2 * CL, D), BF16), ((2 * CL, D), BF16), ((2 * CL, D), BF16), ((2, 2 * CL, 4 * HW), BF16), ((2 * CL, WL), F32)],
        smem=(),
        flops=10**9,
    )
    swapped = shifted(send, "core", 1)
    up_far, down_far = call(
        pack_far_kernel, [((80, 4 * HW), BF16)] * 2, (keep, swapped, blocks), smem=()
    )
    up_near, down_near, b0 = call(
        pack_near_kernel,
        [((n, 4 * HW), BF16) for n in (96, 112, 160)],
        (keep, swapped, blocks),
        smem=(),
    )
    low_far, high_far = shifted(up_far, "x", 1), shifted(down_far, "x", -1)
    low_near, high_near = shifted(up_near, "x", 1), shifted(down_near, "x", -1)
    far_low, far_high = shifted(low_far, "x", 1), shifted(high_far, "x", -1)
    mine, nxt, hnext = call(
        gather_kernel,
        [((4, CL, 4 * HW), BF16), ((16, D), BF16), ((3, 16, WL), F32)],
        (b0, low_near, high_near, far_low, far_high, swapped),
        smem=(),
    )
    other_rows = shifted(mine, "core", 1)
    res, keep_r, send_r = call(
        attend_kernel,
        [((4, LC + 16, HW), BF16), ((4, ROWS, HW), BF16), ((4, ROWS, HW), BF16)],
        (lengths, b0, low_far, low_near, high_far, high_near, far_low, far_high, strip),
        [((LC, HW), BF16)] * 4 + [((NH, LC, LC), F32)] * 2 + [((NH, LC, LC), BF16)] * 2,
        flops=6 * 10**9,
        vmem=16 * 2**20,
    )
    got_r = shifted(send_r, "core", 1)
    dw_keep, dw_send = call(
        weights_kernel,
        [((4, 128, HW), F32), ((4, 128, HW), BF16)],
        (res, mine, other_rows),
        [((LC, 256), BF16), ((LC, 256), BF16)],
        smem=(),
        flops=10**9,
    )
    dw_got = shifted(dw_send, "dp", 1)
    msg = (CL + ROWS, WL + 128)
    m2, g, sums = call(
        partial_far_kernel,
        [(msg, BF16), ((4, ROWS, WL), BF16), ((ROWS, 128), F32)],
        (keep_r, got_r, hown, hnext, dw_keep, *weights),
        smem=(),
        flops=3 * 10**8,
    )
    m1, m3, own, cz, inv = call(
        partial_near_kernel,
        [(msg, BF16), (msg, BF16), (msg, F32), ((ROWS, WL), BF16), ((ROWS, 128), F32)],
        (g, sums, m2, crow, nxt, *weights),
        [((ROWS, D), BF16)],
        smem=(),
        flops=10**9,
    )
    r1, r2, r3 = shifted(m1, "tensor", 1), shifted(m2, "tensor", 2), shifted(m3, "tensor", 3)
    dw_own, dw_other = call(
        sum_kernel,
        [((4, 64, HW), F32), ((4, 64, HW), BF16)],
        (dw_keep, dw_got, r2),
        smem=(),
    )
    dw_other = shifted(dw_other, "core", 1)
    dw = call(
        total_kernel,
        [((64, WL), F32)] * 4,
        (dw_own, dw_other),
        smem=(),
        flops=6 * 10**9,
        typed=False,
    )
    update, grad_tokens = call(
        after_kernel,
        [((SEG, WL), BF16)] * 2,
        (lengths, own, r1, r2, r3, cz, inv, gain, conv_first, conv_second, up_gain),
        [((ROWS, WL), F32)],
        flops=2 * 10**10,
        typed=False,
    )
    return (update[None], grad_tokens[None], *dw)


def solution(mesh):
    ctx = ("x", "y", "core")
    fine = Mesh(
        np.asarray(mesh.devices).reshape(2, 4, 2, 2, 4), ("dp", "x", "y", "core", "tensor")
    )
    tok = P("dp", ctx, "tensor")
    col = P(None, "tensor")
    in_specs = (tok, P("dp"), col, col, P(), col, col, col, col, col, P(), col, tok)
    dw = P(("dp",) + ctx, "tensor")
    return jax.shard_map(
        local, mesh=fine, in_specs=in_specs, out_specs=(tok, tok, dw, dw, dw, dw), check_vma=False
    )
```

```python
import math

import jax
import jax.numpy as jnp
import numpy as np
from jax import lax
from jax.experimental import pallas as pl
from jax.experimental.pallas import tpu as pltpu
from jax.sharding import Mesh, PartitionSpec as P

F32 = jnp.float32
BF16 = jnp.bfloat16
NEG = float("-inf")
D = 2048
WL = 512
LC = 512
CL = 32
SEG = 512
HD = 128
NH = 2
HW = NH * HD
SCALE = 1.0 / math.sqrt(HD)
ROWS = CL + 16
VM = pltpu.VMEM
BIG = 63 * 2**20
SM = pltpu.SMEM
PIECE = 4 * CL


def dg(a, b, ca, cb):
    return lax.dot_general(a, b, (((ca,), (cb,)), ((), ())), preferred_element_type=F32)


class Place:
    def __init__(self):
        self.x, self.y, self.core = (lax.axis_index(a) for a in ("x", "y", "core"))
        self.dp, self.z = lax.axis_index("dp"), lax.axis_index("tensor")
        self.ctx = (self.x * 2 + self.y) * 2 + self.core


def in_three(a):
    hi = a.astype(BF16).astype(F32)
    lo = (a - hi).astype(BF16).astype(F32)
    return hi, lo, (a - hi - lo).astype(BF16).astype(F32)


def tap_weights(first, second):
    taps = jnp.concatenate([second[a : a + 1] * first for a in range(4)], axis=0)
    return jnp.concatenate([taps[15:16], taps[:15]], axis=0)


def byte_mask(ctx, doc_len):
    pos = ctx * SEG + 16 * lax.broadcasted_iota(jnp.int32, (CL, 16, WL), 0)
    pos = pos + lax.broadcasted_iota(jnp.int32, (CL, 16, WL), 1)
    return (pos < doc_len).astype(F32)


def before_kernel(
    lens, tokens_h, grad_h, first_h, second_h, up_h, gain_h, piece, row, last, gain,
    tokens, grad_out, first, second, up_gain, shift, sems,
):
    pairs = ((tokens_h, tokens), (first_h, first), (second_h, second), (grad_h, grad_out), (up_h, up_gain), (gain_h, gain))
    copies = [pltpu.make_async_copy(a, b, sems.at[i]) for i, (a, b) in enumerate(pairs)]
    for c in copies:
        c.start()
    mask = byte_mask(Place().ctx, lens[0])
    u = lax.broadcasted_iota(jnp.int32, (CL, 16, WL), 1)
    for c in copies[:3]:
        c.wait()
    taps = tap_weights(first[...], second[...])
    prod = tokens[...].astype(F32).reshape(CL, 16, WL) * mask * taps[None]
    own = jnp.sum(jnp.where(u == 0, prod, 0.0), axis=1)
    onward = jnp.sum(jnp.where(u == 0, 0.0, prod), axis=1)
    shift[0:8] = jnp.zeros((8, WL), F32)
    shift[8 : 8 + CL] = onward
    part = own + shift[7 : 7 + CL]
    piece[0:CL] = part.astype(BF16)
    row[...] = jnp.broadcast_to(part[0:1], (8, WL))
    piece[64:80] = jnp.concatenate(list(in_three(part[0:1])) + [jnp.zeros((13, WL), F32)], axis=0).astype(BF16)
    last[...] = jnp.broadcast_to(shift[7 + CL : 8 + CL], (8, WL))
    for c in copies[3:]:
        c.wait()
    weighted = grad_out[...].astype(F32).reshape(CL, 16, WL) * mask * up_gain[...][None]
    piece[CL : 2 * CL] = jnp.sum(weighted, axis=1).astype(BF16)


def pile_kernel(piece, row, across, rim, rim_across, out):
    y = Place().y
    first = lax.broadcasted_iota(jnp.int32, (16, WL), 0) == 0
    sent = across[64:80].astype(F32)
    theirs = sent[0:1] + sent[1:2] + sent[2:3] + rim_across[0:1]
    for src, at, top in ((piece, y * 64, row[0:1] + rim[0:1]), (across, 64 - y * 64, theirs)):
        head = jnp.where(first, top, src[0:16].astype(F32))
        out[pl.ds(pl.multiple_of(at, 64), 16)] = head.astype(BF16)
        out[pl.ds(pl.multiple_of(at + 16, 16), 48)] = src[16:64]


def bias_kernel(near, table, strip):
    core = Place().core
    n = near.shape[1]
    which = near[0:1]
    for h in range(NH):
        row = jnp.full((1, n), NEG, F32)
        for b in range(table.shape[0]):
            row = jnp.where(which == b, table[b, core * NH + h], row)
        rolled = pltpu.roll(jnp.broadcast_to(row, (128, n)), 0, 1, stride=1, stride_axis=0)
        strip[h] = rolled[:, :LC]


def project_kernel(
    p0, r1, r2, r3, gain, wq, wk, wv, wo, keep, send, blocks, cown, iown, hown, craw, nrm, gco, both, hs
):
    at = Place()
    z, core, x, y = at.z, at.core, at.x, at.y
    for s, src in enumerate((p0, r1, r2, r3)):
        cols = pl.ds(pl.multiple_of(lax.rem(z + 4 - s, 4) * WL, WL), WL)
        for i in range(2):
            rows = slice(i * CL, i * CL + CL)
            craw[rows, cols] = src[2 * i * CL : 2 * i * CL + CL]
            gco[rows, cols] = src[2 * i * CL + CL : 2 * i * CL + 2 * CL]
    own_rows = pl.ds(pl.multiple_of(y * CL, CL), CL)
    cown[...] = craw[own_rows, pl.ds(pl.multiple_of(z * WL, WL), WL)]
    c = craw[...].astype(F32)
    square = jnp.sum(c * c, axis=1, keepdims=True) * (1.0 / D) + 1e-6
    r = lax.rsqrt(square)
    rms = jnp.sqrt(square)
    hs[:, 0:128] = jnp.broadcast_to(r, (2 * CL, 128))
    iown[...] = hs[own_rows, 0:128]
    nrm[...] = (c * r * gain[...]).astype(BF16)
    heads_of = [[], []]
    for src, w, slot in ((gco, wo, 3), (nrm, wq, 0), (nrm, wk, 1), (nrm, wv, 2)):
        full = jnp.dot(src[...], w[...], preferred_element_type=F32)
        v = full.astype(BF16)
        if slot < 3:
            h = full * rms
            hs[...] = h
            for i in range(2):
                heads_of[i].append(in_three(h[i * CL : i * CL + 1])[:2])
            hown[slot] = hs[pl.ds(pl.multiple_of(y * CL, CL), CL)]
        for half in range(2):
            both[half, :, slot * HW : slot * HW + HW] = v[:, half * HW : half * HW + HW]
    keep[...] = both[core]
    send[0:64] = both[1 - core]
    tops = [c[i * CL : i * CL + 1, j * 1024 : j * 1024 + 1024] for i in range(2) for j in range(2)]
    for (q_hi, q_lo), (k_hi, k_lo), (v_hi, v_lo) in heads_of:
        tops += [jnp.concatenate(p, axis=1) for p in ((q_hi, k_hi), (v_hi, q_lo), (k_lo, v_lo))]
    send[64:80] = jnp.concatenate(tops + [jnp.zeros((6, 1024), F32)], axis=0).astype(BF16)
    for s in range(4):
        for d in range(2):
            chip = lax.rem(x + s, 4) * 2 + y
            cols = pl.ds(pl.multiple_of((d * 8 + chip) * 128, 128), 128)
            for i in range(2):
                rows = slice(i * CL, i * CL + CL)
                at = i * 512 + d * 128
                blocks[s, :, at : at + 128] = nrm[rows, cols]
                blocks[s, :, at + 256 : at + 384] = gco[rows, cols]


def pack_far_kernel(keep, swapped, blocks, up, down):
    core = Place().core
    for i, out in ((0, up), (1, down)):
        for src, c in ((keep, core), (swapped, 1 - core)):
            out[pl.ds(pl.multiple_of(c * CL, CL), CL)] = src[i * CL : i * CL + CL]
    up[64:80] = blocks[2, 0:16]
    down[64:80] = blocks[2, 16:32]


def pack_near_kernel(keep, swapped, blocks, up, down, b0):
    core = Place().core
    for i, out in ((1, up), (0, down)):
        for src, c in ((keep, core), (swapped, 1 - core)):
            out[pl.ds(pl.multiple_of(32 + c * CL, CL), CL)] = src[i * CL : i * CL + CL]
    for i in range(2):
        for src, c in ((keep, core), (swapped, 1 - core)):
            row = pl.multiple_of(i * 64 + c * CL, CL)
            b0[pl.ds(row, CL)] = src[i * CL : i * CL + CL]
    up[0:32] = blocks[1]
    down[0:32] = blocks[3]
    down[96:112] = swapped[64:80]
    b0[128:160] = blocks[0]


def gather_kernel(b0, low_near, high_near, far_low, far_high, swapped, mine, cnext, inext, hnext, row):
    mine[0] = b0[128:160]
    mine[1] = low_near[0:32]
    mine[2, 0:16] = far_low[64:80]
    mine[2, 16:32] = far_high[64:80]
    mine[3] = high_near[0:32]
    at = Place()
    wraps = jnp.logical_and(at.core == 1, at.y == 1)
    tops = jnp.where(wraps, high_near[96:112].astype(F32), swapped[64:80].astype(F32))
    upper = jnp.where(at.core == 0, at.y, 1 - at.y) == 1
    square = jnp.zeros((1, 1), F32)
    for j in range(2):
        half = jnp.where(upper, tops[2 + j : 3 + j], tops[j : j + 1])
        square = square + jnp.sum(half * half, axis=1, keepdims=True)
        row[:, j * 1024 : j * 1024 + 1024] = jnp.broadcast_to(half, (16, 1024)).astype(BF16)
    inext[...] = jnp.broadcast_to(lax.rsqrt(square * (1.0 / D) + 1e-6), (16, 128))
    cnext[...] = row[:, pl.ds(pl.multiple_of(at.z * WL, WL), WL)]
    a, b, c = [jnp.where(upper, tops[7 + j : 8 + j], tops[4 + j : 5 + j]) for j in range(3)]
    left, right = slice(0, WL), slice(WL, 2 * WL)
    products = (a[:, left] + b[:, right], a[:, right] + c[:, left], b[:, left] + c[:, right])
    for i, h in enumerate(products):
        hnext[i] = jnp.broadcast_to(h, (16, WL))


def attend_kernel(
    lens, b0, low_far, low_near, high_far, high_near, far_low, far_high, strip,
    res, keep, send, q, k, v, ga, score, dprob, sg, pb,
):
    at = Place()
    ctx, core, x, doc_len = at.ctx, at.core, at.x, lens[0]
    for src, first, n, s, row in (
        (b0, 0, 128, 0, 0),
        (low_far, 0, 64, 1, 0),
        (low_near, 32, 64, 1, 64),
        (far_low, 0, 64, 2, 0),
        (far_high, 0, 64, 2, 64),
        (high_near, 32, 64, 3, 0),
        (high_far, 0, 64, 3, 64),
    ):
        rows = pl.ds(pl.multiple_of(lax.rem(x + 4 - s, 4) * 128 + row, 64), n)
        for i, dst in enumerate((q, k, v, ga)):
            dst[rows] = src[first : first + n, i * HW : i * HW + HW]
    key_pos = lax.broadcasted_iota(jnp.int32, (1, LC), 1)
    key_mask = jnp.where(16 * key_pos < doc_len, 0.0, NEG)
    work = [(b, h, slice(h * HD, h * HD + HD)) for b in (3, 2, 1, 0) for h in range(NH)]
    for b, h, c in work:
        rows, n = slice(b * 128, b * 128 + 128), b * 128 + 128
        score[h, rows, 0:n] = dg(q[rows, c], k[0:n, c], 1, 1)
        dprob[h, rows, 0:n] = dg(ga[rows, c], v[0:n, c], 1, 1)
    for b, h, c in work:
        rows, n = slice(b * 128, b * 128 + 128), b * 128 + 128
        s = score[h, rows, 0:n] * SCALE + strip[h, :, LC - n :] + key_mask[:, :n]
        e = jnp.exp(s - jnp.max(s, axis=1, keepdims=True))
        p = e * (1.0 / jnp.sum(e, axis=1, keepdims=True))
        dp = dprob[h, rows, 0:n]
        dot = jnp.sum(p * dp, axis=1, keepdims=True)
        sg[h, rows, 0:n] = (p * (dp - dot)).astype(BF16)
        pb[h, rows, 0:n] = p.astype(BF16)
    for b, h, c in work:
        rows, n = slice(b * 128, b * 128 + 128), b * 128 + 128
        gq = jnp.dot(sg[h, rows, 0:n], k[0:n, c], preferred_element_type=F32)
        res[0, rows, c] = (gq * SCALE).astype(BF16)
        res[3, rows, c] = jnp.dot(pb[h, rows, 0:n], v[0:n, c], preferred_element_type=F32).astype(BF16)
        tail = slice(b * 128, LC)
        res[1, rows, c] = (dg(sg[h, tail, rows], q[tail, c], 0, 0) * SCALE).astype(BF16)
        res[2, rows, c] = dg(pb[h, tail, rows], ga[tail, c], 0, 0).astype(BF16)
    res[:, LC : LC + 16] = jnp.zeros((4, 16, HW), BF16)
    peer = ctx + 1 - 2 * core
    keep[...] = res[:, pl.ds(pl.multiple_of(ctx * CL, CL), ROWS)]
    send[...] = res[:, pl.ds(pl.multiple_of(peer * CL, CL), ROWS)]


def weights_kernel(res, mine, other, keep, send, nb, gb):
    at = Place()
    core, x, dp = at.core, at.x, at.dp
    for s in range(4):
        for src, c in ((mine, core), (other, 1 - core)):
            for i in range(2):
                row = (lax.rem(x + 4 - s, 4) * 4 + i * 2 + c) * CL
                rows = pl.ds(pl.multiple_of(row, CL), CL)
                nb[rows] = src[s, :, i * 512 : i * 512 + 256]
                gb[rows] = src[s, :, i * 512 + 256 : i * 512 + 512]
    for w in range(4):
        src = gb if w == 3 else nb
        for d, out in ((dp, keep), (1 - dp, send)):
            cols = pl.ds(pl.multiple_of(d * 128, 128), 128)
            out[w] = dg(src[:, cols], res[w, 0:LC], 0, 0).astype(out.dtype)


def sum_kernel(keep, got, r2, own, send):
    core = Place().core
    for w in range(4):
        for c, out in ((core, own), (1 - core, send)):
            rows = pl.ds(pl.multiple_of(c * 64, 64), 64)
            out[w] = (keep[w, rows] + got[w, rows].astype(F32)).astype(out.dtype)


def message(g, weights, t, msg):
    part = pl.ds(pl.multiple_of(t * WL, WL), WL)
    wq, wk, wv, wo = weights
    gn = dg(g[0], wq[part], 1, 1) + dg(g[1], wk[part], 1, 1) + dg(g[2], wv[part], 1, 1)
    msg[0:CL, 0:WL] = dg(g[3, 0:CL], wo[part], 1, 1).astype(msg.dtype)
    msg[CL : CL + ROWS, 0:WL] = gn.astype(msg.dtype)
    msg[0:CL, WL : WL + 128] = jnp.zeros((CL, 128), msg.dtype)


def partial_far_kernel(
    keep_r, got_r, hown, hnext, cown, cnext, iown, inext, after, wq, wk, wv, wo, msg2, g, sums, cz, inv_out
):
    at = Place()
    z, core = at.z, at.core
    g[:, :, pl.ds(pl.multiple_of(core * HW, HW), HW)] = keep_r[...]
    g[:, :, pl.ds(pl.multiple_of((1 - core) * HW, HW), HW)] = got_r[...]
    cz[0:CL] = cown[...]
    cz[CL:ROWS] = cnext[...]
    inv_out[0:CL] = iown[...]
    inv_out[CL:ROWS] = inext[...]
    both = []
    for rows, h in ((slice(0, CL), hown), (slice(CL, ROWS), hnext)):
        total = sum(g[i, rows].astype(F32) * h[i] for i in range(3))
        both.append(jnp.sum(total, axis=1, keepdims=True))
    dots = jnp.concatenate(both, axis=0)
    sums[...] = jnp.broadcast_to(dots, (ROWS, 128))
    lane = lax.broadcasted_iota(jnp.int32, (ROWS, 128), 1)
    hi = dots.astype(BF16).astype(F32)
    lo = (dots - hi).astype(BF16).astype(F32)
    lo2 = dots - hi - lo
    packed = jnp.where(lane == 0, hi, jnp.where(lane == 1, lo, lo2))
    message(g, (wq, wk, wv, wo), lax.rem(z + 2, 4), msg2)
    msg2[CL : CL + ROWS, WL : WL + 128] = jnp.where(lane < 3, packed, 0.0).astype(BF16)


def partial_near_kernel(
    g, sums, msg2, wq, wk, wv, wo, msg1, msg3, keep
):
    z = Place().z
    weights = (wq, wk, wv, wo)
    for shift, msg in ((1, msg1), (3, msg3)):
        message(g, weights, lax.rem(z + shift, 4), msg)
        msg[CL : CL + ROWS, WL : WL + 128] = msg2[CL : CL + ROWS, WL : WL + 128]
    message(g, weights, z, keep)
    keep[CL : CL + ROWS, WL : WL + 128] = sums[...]


def total_kernel(own, other, o0, o1, o2, o3):
    core = Place().core
    for w, o in enumerate((o0, o1, o2, o3)):
        o[:, pl.ds(pl.multiple_of(core * HW, HW), HW)] = own[w]
        o[:, pl.ds(pl.multiple_of((1 - core) * HW, HW), HW)] = other[w].astype(F32)


def after_kernel(
    lens, keep, r1, r2, r3, cz, inv, gain, first, second, up_gain, update, grad, rows
):
    at = Place()
    ctx, doc_len, z = at.ctx, lens[0], at.z
    mask = byte_mask(ctx, doc_len)
    body = slice(0, WL)
    out = keep[0:CL, body]
    gn = keep[CL : CL + ROWS, body]
    dots = keep[CL : CL + ROWS, WL : WL + 1]
    for r in (r1, r2, r3):
        out = out + r[0:CL, body].astype(F32)
        gn = gn + r[CL : CL + ROWS, body].astype(F32)
        dots = dots + jnp.sum(r[CL : CL + ROWS, WL : WL + 128].astype(F32), axis=1, keepdims=True)
    update[...] = ((out[:, None, :] * up_gain[...][None]) * mask).reshape(SEG, WL).astype(BF16)
    i = inv[:, 0:1]
    gained = gn * gain[0:1, pl.ds(pl.multiple_of(z * WL, WL), WL)]
    full = i * gained - cz[...].astype(F32) * (i * i * i) * dots * (1.0 / D)
    exists = lax.broadcasted_iota(jnp.int32, (ROWS, WL), 0) + ctx * CL < LC
    rows[...] = jnp.where(exists, full, 0.0)
    taps = tap_weights(first[...], second[...])
    u = lax.broadcasted_iota(jnp.int32, (CL, 16, WL), 1)
    picked = jnp.where(u == 0, rows[0:CL][:, None, :], rows[1 : CL + 1][:, None, :])
    grad[...] = (picked * taps[None] * mask).reshape(SEG, WL).astype(BF16)


def call(kernel, outs, args, scratch=(), smem=(0,), flops=0, size=0, vmem=8 * 2**20, hbm=(), typed=True):
    def spec(i):
        return pl.BlockSpec(memory_space=SM if i in smem else pltpu.HBM if i in hbm else VM)

    return pl.pallas_call(
        kernel,
        out_shape=[pltpu.VMEM(s, d) if typed else jax.ShapeDtypeStruct(s, d) for s, d in outs],
        in_specs=[spec(i) for i in range(len(args))],
        out_specs=[pl.BlockSpec(memory_space=VM)] * len(outs),
        scratch_shapes=[pltpu.VMEM(*s) if isinstance(s, tuple) else s for s in scratch],
        compiler_params=pltpu.CompilerParams(vmem_limit_bytes=vmem),
        cost_estimate=pl.CostEstimate(flops=flops, bytes_accessed=size, transcendentals=0),
    )(*args)


def shifted(x, axis, steps):
    n = lax.axis_size(axis)
    return lax.ppermute(x, axis, [(i, (i + steps) % n) for i in range(n)])


def local(
    tokens, lengths, conv_first, conv_second, norm_gain, w_query, w_key, w_value, w_out,
    bias_table, buckets, up_gain, grad_out,
):
    weights = (w_query, w_key, w_value, w_out)
    piece, row, last, gain = call(
        before_kernel,
        [((80, WL), BF16), ((8, WL), F32), ((8, WL), F32), ((1, D), F32)],
        (lengths, tokens[0], grad_out[0], conv_first, conv_second, up_gain, norm_gain[None]),
        [
            ((SEG, WL), BF16), ((SEG, WL), BF16), ((4, WL), F32), ((4, WL), F32), ((16, WL), F32),
            ((CL + 8, WL), F32), pltpu.SemaphoreType.DMA((6,)),
        ],
        hbm=(1, 2, 3, 4, 5, 6),
        vmem=BIG,
    )
    line = ("x", "y", "core")
    rim = lax.ppermute(last, line, [(i, i + 1) for i in range(15)])
    over = [(i, ((i + 1) ^ 2)) for i in range(15)]
    across = shifted(piece, "y", 1)
    rim_across = lax.ppermute(last, line, over)
    (piece,) = call(
        pile_kernel,
        [((PIECE, WL), BF16)],
        (piece, row, across, rim, rim_across),
        smem=(),
        flops=6 * 10**9,
    )
    n = 640
    near = jnp.concatenate(
        [
            jnp.flip(buckets[:385]),
            jnp.full((n - LC,), bias_table.shape[0], jnp.int32),
            jnp.flip(buckets[385:]),
        ]
    )
    (strip,) = call(
        bias_kernel,
        [((NH, 128, LC), F32)],
        (jnp.broadcast_to(near[None], (8, n)), bias_table),
        smem=(1,),
    )
    pieces = [piece] + [shifted(piece, "tensor", s) for s in (1, 2, 3)]
    keep, send, blocks, cown, iown, hown = call(
        project_kernel,
        [((64, 4 * HW), BF16), ((80, 4 * HW), BF16), ((4, CL, 4 * HW), BF16), ((CL, WL), BF16), ((CL, 128), F32), ((3, CL, WL), F32)],
        (*pieces, gain, *weights),
        [((2 * CL, D), BF16), ((2 * CL, D), BF16), ((2 * CL, D), BF16), ((2, 2 * CL, 4 * HW), BF16), ((2 * CL, WL), F32)],
        smem=(),
        flops=10**9,
    )
    swapped = shifted(send, "core", 1)
    up_far, down_far = call(
        pack_far_kernel, [((80, 4 * HW), BF16)] * 2, (keep, swapped, blocks), smem=()
    )
    up_near, down_near, b0 = call(
        pack_near_kernel,
        [((n, 4 * HW), BF16) for n in (96, 112, 160)],
        (keep, swapped, blocks),
        smem=(),
    )
    low_far, high_far = shifted(up_far, "x", 1), shifted(down_far, "x", -1)
    low_near, high_near = shifted(up_near, "x", 1), shifted(down_near, "x", -1)
    far_low, far_high = shifted(low_far, "x", 1), shifted(high_far, "x", -1)
    mine, cnext, inext, hnext = call(
        gather_kernel,
        [((4, CL, 4 * HW), BF16), ((16, WL), BF16), ((16, 128), F32), ((3, 16, WL), F32)],
        (b0, low_near, high_near, far_low, far_high, swapped),
        [((16, D), BF16)],
        smem=(),
    )
    other_rows = shifted(mine, "core", 1)
    res, keep_r, send_r = call(
        attend_kernel,
        [((4, LC + 16, HW), BF16), ((4, ROWS, HW), BF16), ((4, ROWS, HW), BF16)],
        (lengths, b0, low_far, low_near, high_far, high_near, far_low, far_high, strip),
        [((LC, HW), BF16)] * 4 + [((NH, LC, LC), F32)] * 2 + [((NH, LC, LC), BF16)] * 2,
        flops=6 * 10**9,
        vmem=10 * 2**20,
    )
    got_r = shifted(send_r, "core", 1)
    dw_keep, dw_send = call(
        weights_kernel,
        [((4, 128, HW), F32), ((4, 128, HW), BF16)],
        (res, mine, other_rows),
        [((LC, 256), BF16), ((LC, 256), BF16)],
        smem=(),
        flops=10**9,
    )
    dw_got = shifted(dw_send, "dp", 1)
    msg = (CL + ROWS, WL + 128)
    m2, g, sums, cz, inv = call(
        partial_far_kernel,
        [(msg, BF16), ((4, ROWS, WL), BF16), ((ROWS, 128), F32), ((ROWS, WL), BF16), ((ROWS, 128), F32)],
        (keep_r, got_r, hown, hnext, cown, cnext, iown, inext, dw_keep, *weights),
        smem=(),
        flops=3 * 10**8,
    )
    m1, m3, own = call(
        partial_near_kernel,
        [(msg, BF16), (msg, BF16), (msg, F32)],
        (g, sums, m2, *weights),
        smem=(),
        flops=10**9,
    )
    r1, r2, r3 = shifted(m1, "tensor", 1), shifted(m2, "tensor", 2), shifted(m3, "tensor", 3)
    dw_own, dw_other = call(
        sum_kernel,
        [((4, 64, HW), F32), ((4, 64, HW), BF16)],
        (dw_keep, dw_got, r2),
        smem=(),
    )
    dw_other = shifted(dw_other, "core", 1)
    dw = call(
        total_kernel,
        [((64, WL), F32)] * 4,
        (dw_own, dw_other),
        smem=(),
        flops=6 * 10**9,
        typed=False,
    )
    update, grad_tokens = call(
        after_kernel,
        [((SEG, WL), BF16)] * 2,
        (lengths, own, r1, r2, r3, cz, inv, gain, conv_first, conv_second, up_gain),
        [((ROWS, WL), F32)],
        flops=2 * 10**10,
        typed=False,
    )
    return (update[None], grad_tokens[None], *dw)


def solution(mesh):
    ctx = ("x", "y", "core")
    fine = Mesh(
        np.asarray(mesh.devices).reshape(2, 4, 2, 2, 4), ("dp", "x", "y", "core", "tensor")
    )
    tok = P("dp", ctx, "tensor")
    col = P(None, "tensor")
    in_specs = (tok, P("dp"), col, col, P(), col, col, col, col, col, P(), col, tok)
    dw = P(("dp",) + ctx, "tensor")
    return jax.shard_map(
        local, mesh=fine, in_specs=in_specs, out_specs=(tok, tok, dw, dw, dw, dw), check_vma=False
    )
```
